512 devices in a mesh: gx: 16 (over x_hi, y), gy: 4 (over x_lo, core), gz: 8 (over z).
Axes of the slice: x: 4 (x_hi: 2, x_lo: 2; x = x_hi * 2 + x_lo), y: 8, z: 8, core: 2. Of those that a mesh axis runs over, the one named last changes fastest.
Arguments:
- efield: float32 [3, 32, 2048, 512], P(None, 'gz', 'gx', 'gy'), may hold values from -6 to 6
- density: float32 [32, 2048, 512], P('gz', 'gx', 'gy'), may hold values from 0.5 to 2
- mobility_prev: float32 [32, 2048, 512], P('gz', 'gx', 'gy'), may hold values from 0.5 to 2
- thermal_prev: float32 [32, 2048, 512], P('gz', 'gx', 'gy'), may hold values from 0 to 2
- owner: int32 [8, 16, 4, 512, 1], P('gz', 'gx', 'gy'), may hold values from 0 to 63; in each aligned block of 512 rows (0 to 511, 512 to 1023, ..., all dimensions but the last counted through in order) at most 16 rows name the same one
- block: int32 [8, 16, 4, 512], P('gz', 'gx', 'gy'), may hold values from 0 to 511
- live: int32 [8, 16, 4, 512], P('gz', 'gx', 'gy'), may hold values from 1 to 128
- material: int32 [8, 16, 4, 512], P('gz', 'gx', 'gy'), may hold values from 0 to 7
- mat_conductivity: float32 [8], replicated, may hold values from 0.5 to 5
- mat_softening: float32 [8], replicated, may hold values from 0.1 to 0.8
- mat_capacity: float32 [8], replicated, may hold values from 0.01 to 0.1
Outputs:
- thermal: float32 [32, 2048, 512], P('gz', 'gx', 'gy')
- mobility: float32 [32, 2048, 512], P('gz', 'gx', 'gy')
- ionization: float32 [32, 2048, 512], P('gz', 'gx', 'gy')
The draws below stay inside these ranges and needn't reach their ends.
Inputs may be any that keep to these rules, and one draw needn't show every extreme that they name: Among the rows of one device, at most 16 name the same owner; some device reaches 16.
All inputs are finite; a program needn't handle non-finite values.
Results may differ from the reference program's by a relative error of at most 0.0001.
Values sent between devices are 32-bit elements; how exact they have to be, the bound alone decides.
No kernel may reach another device: no remote copies, remote signals or barrier semaphores. Data moves between devices by JAX's collectives and lax.ppermute only.
A program may use at most 64 MiB of HBM per device.

```python
import math
import jax
import jax.numpy as jnp
import numpy as np
from jax import lax

DL = 4
DXD = 128
ROW = 128
TZD = 4
TXD = 128
NMAT = 8
SWEEPS = 6
ROWS = 512
BPD = 512
PEERS = 64
CAP = 16
DZ = 32
DX = 2048
DY = 512
TZ = 32
TX = 2048
TY = 512
N_GX = 16
N_GY = 4
N_GZ = 8


def set_ends(array, rng, smallest, high):
    longest = array.shape.index(max(array.shape))
    spots = []
    for shift in (0, 1):
        where = [jax.random.randint(jax.random.fold_in(rng, axis), (), 0, length) for axis, length in enumerate(array.shape)]
        where[longest] = (where[longest] + shift) % array.shape[longest]
        spots.append(tuple(where))
    return array.at[spots[0]].set(smallest).at[spots[1]].set(high)


def block_levels(stream_key, shape, split, low, high):
    def one(axis_at, parts):
        draws = jax.random.uniform(jax.random.fold_in(jax.random.fold_in(stream_key, 6), axis_at), (parts,), jnp.float32, low / len(split), high / len(split))
        return jnp.repeat(jnp.exp(draws), shape[axis_at] // parts).reshape((-1,) + (1,) * (len(shape) - axis_at - 1))

    factor_of = one(*split[0])
    for cut in split[1:]:
        factor_of = factor_of * one(*cut)
    return factor_of


def shared_out(own_key, own, number, rows, number_of, top, reach, lean):
    sequence = jax.random.permutation(own_key, number_of)
    heavy_load, ordinary = portions_of(number_of, rows * top, reach, lean, True), portions_of(number_of, rows * top, reach, lean, False)
    places = jnp.arange(number_of)

    def named(tallies, rotation):
        used = int((tallies > 0).sum())
        fixed = max(1, used // 4)
        moved = fixed + (places - fixed + rotation * (used - fixed)) % max(1, number_of - fixed)
        return jnp.zeros((number_of,), jnp.int32).at[sequence[jnp.where(places < fixed, places, moved)]].set(jnp.asarray(tallies, jnp.int32))

    tallies = jnp.where(number % 4 == 0, named(heavy_load, number // 4), named(ordinary, number - number // 4 - 1))
    mixed = jax.random.permutation(jax.random.fold_in(own, 3), number_of)
    donor, taker = mixed[0:number_of // 2 * 2:2], mixed[1:number_of // 2 * 2:2]
    room = jnp.minimum(tallies[donor] - 1, reach - tallies[taker]) // 2
    room = jnp.where((donor == sequence[0]) | (taker == sequence[0]) | (tallies[taker] == 0), 0, jnp.maximum(room, 0))
    moved = jax.random.randint(jax.random.fold_in(own, 4), (number_of // 2,), 0, 1 << 20) % (room + 1)
    tallies = tallies.at[donor].add(-moved).at[taker].add(moved)
    members = jnp.searchsorted(jnp.cumsum(tallies), jnp.arange(rows * top), side="right").astype(jnp.int32)
    listing = members.reshape(top, rows).T
    listing = listing[jax.random.permutation(jax.random.fold_in(own, 1), rows)]
    rotation = jax.random.randint(jax.random.fold_in(own, 2), (rows, 1), 0, top)
    return jnp.take_along_axis(listing, (jnp.arange(top)[None, :] + rotation) % top, axis=1)


def portions_of(number_of, total, bound, lean, full):
    portions = [(1 << 20) // math.isqrt(standing ** lean) + 1 for standing in range(1, number_of + 1)]
    largest = bound if full else min(bound, max(-(-total // number_of), total * portions[0] // sum(portions)))
    least = 1 if total - largest >= number_of - 1 else 0
    holding, rest = [largest] + [least] * (number_of - 1), total - largest - least * (number_of - 1)
    while rest > 0:
        free = [i for i in range(1, number_of) if holding[i] < largest] or [i for i in range(1, number_of) if holding[i] < bound]
        whole, left = sum([portions[i] for i in free]), rest
        for i in free:
            extra = min(bound - holding[i], max(1, left * portions[i] // whole), rest)
            holding[i] = holding[i] + extra
            rest = rest - extra
    return np.array(holding)


def centred(own_key, dims, spread, reach, pieces=(), kind=jnp.bfloat16):
    gain = block_levels(own_key, dims, pieces, -0.22, 0.18) if pieces else 1.0
    entries = jax.random.normal(own_key, dims, jnp.float32) * spread * gain
    return jnp.minimum(jnp.maximum(entries, -reach), reach).astype(kind)


def setup_inputs(seed: int = 0) -> dict:
    key_list = jax.random.split(jax.random.key(seed), 12)
    efield = centred(key_list[0], (3, DZ, DX, DY), 1.0, 6.0, ((1, 8), (2, 16), (3, 4)), jnp.float32)
    density = jnp.clip(0.5 + 1.5 * jax.random.uniform(key_list[1], (DZ, DX, DY), jnp.float32) ** block_levels(key_list[1], (DZ, DX, DY), ((0, 8), (1, 16), (2, 4)), -0.2, 0.2), 0.5, 2.0)
    mobility_prev = jnp.clip(jnp.exp(math.log(2.0) - 1.3862944 * jax.random.uniform(key_list[2], (DZ, DX, DY), jnp.float32) ** block_levels(key_list[2], (DZ, DX, DY), ((0, 8), (1, 16), (2, 4)), -0.2, 0.2)), 0.5, 2.0)
    thermal_prev = jnp.clip(2.0 * jax.random.uniform(key_list[3], (TZ, TX, TY), jnp.float32) ** block_levels(key_list[3], (TZ, TX, TY), ((0, 8), (1, 16), (2, 4)), -0.2, 0.2), 0.0, 2.0)
    owner_keys = jax.random.split(jax.random.fold_in(key_list[4], 1), N_GZ * N_GX * N_GY * ROWS // ROWS)
    owner_turns = jax.random.permutation(jax.random.fold_in(key_list[4], 3), N_GZ * N_GX * N_GY * ROWS // ROWS)
    owner = jax.vmap(lambda own, number: shared_out(jax.random.fold_in(key_list[4], 2), own, number, ROWS, PEERS, 1, CAP, 2))(owner_keys, owner_turns).reshape((N_GZ, N_GX, N_GY, ROWS, 1))
    block = set_ends(jax.random.randint(key_list[5], (N_GZ, N_GX, N_GY, ROWS), 0, BPD), jax.random.fold_in(key_list[5], 1), 0, BPD - 1).astype(jnp.int32)
    live = set_ends(jax.random.randint(key_list[6], (N_GZ, N_GX, N_GY, ROWS), 1, ROW + 1), jax.random.fold_in(key_list[6], 1), 1, ROW).astype(jnp.int32)
    material = set_ends(jax.random.randint(key_list[7], (N_GZ, N_GX, N_GY, BPD), 0, NMAT), jax.random.fold_in(key_list[7], 1), 0, NMAT - 1).astype(jnp.int32)
    mat_conductivity = jnp.clip(jnp.exp(jax.random.uniform(key_list[8], (NMAT,), jnp.float32, math.log(0.5), math.log(5.0))), 0.5, 5.0)
    mat_softening = jnp.clip(jax.random.uniform(key_list[9], (NMAT,), jnp.float32, 0.1, 0.8), 0.1, 0.8)
    mat_capacity = jnp.clip(jnp.exp(jax.random.uniform(key_list[10], (NMAT,), jnp.float32, math.log(0.01), math.log(0.1))), 0.01, 0.1)
    return {"efield": efield, "density": density, "mobility_prev": mobility_prev, "thermal_prev": thermal_prev, "owner": owner, "block": block, "live": live, "material": material, "mat_conductivity": mat_conductivity, "mat_softening": mat_softening, "mat_capacity": mat_capacity}


def to_rows(field, nz, nx, ny):
    a = field.shape[0] // nz
    b = field.shape[1] // nx
    c = field.shape[2] // ny
    f = field.reshape(nz, a, nx, b, ny, c).transpose(0, 2, 4, 1, 3, 5)
    return f.reshape(nz, nx, ny, a * b, c)

def from_rows(rows, a, b):
    nz, nx, ny, _, c = rows.shape
    f = rows.reshape(nz, nx, ny, a, b, c).transpose(0, 3, 1, 4, 2, 5)
    return f.reshape(nz * a, nx * b, ny * c)

def neighbours(padded):
    return [padded[2:, 1:-1, 1:-1], padded[:-2, 1:-1, 1:-1], padded[1:-1, 2:, 1:-1], padded[1:-1, :-2, 1:-1], padded[1:-1, 1:-1, 2:], padded[1:-1, 1:-1, :-2]]

def reference(efield, density, mobility_prev, thermal_prev, owner, block, live, material, mat_conductivity, mat_softening, mat_capacity):
    esq = efield[0] * efield[0] + efield[1] * efield[1] + efield[2] * efield[2]
    heat = 0.2 * density * mobility_prev * esq
    heat_rows = to_rows(heat, N_GZ, N_GX, N_GY)
    cells = jnp.arange(ROW, dtype=jnp.int32)
    heat_rows = jnp.where(cells < live[..., None], heat_rows, jnp.float32(0.0))
    owners = owner[..., 0]
    slab = jnp.broadcast_to(jnp.arange(N_GZ, dtype=jnp.int32)[:, None, None, None], owners.shape)
    tile_x = owners // N_GY
    tile_y = owners % N_GY
    source_rows = jnp.zeros((N_GZ, N_GX, N_GY, BPD, ROW), jnp.float32).at[slab, tile_x, tile_y, block].add(heat_rows)
    source = from_rows(source_rows, TZD, TXD)
    choose = (material[..., None] == jnp.arange(NMAT, dtype=jnp.int32)).astype(jnp.float32)
    shape_rows = (N_GZ, N_GX, N_GY, BPD, ROW)
    k_base = from_rows(jnp.broadcast_to(lax.optimization_barrier(jnp.sum(choose * mat_conductivity, -1))[..., None], shape_rows), TZD, TXD)
    k_soft = from_rows(jnp.broadcast_to(lax.optimization_barrier(jnp.sum(choose * mat_softening, -1))[..., None], shape_rows), TZD, TXD)
    capf = from_rows(jnp.broadcast_to(lax.optimization_barrier(jnp.sum(choose * mat_capacity, -1))[..., None], shape_rows), TZD, TXD)
    cond = k_base / (1.0 + k_soft * thermal_prev)
    weights = [0.5 * (cond + n) for n in neighbours(jnp.pad(cond, 1))]
    diag = capf + sum(weights)
    rhs = capf * thermal_prev + source

    def residual_of(x):
        xn = neighbours(jnp.pad(x, 1))
        applied = capf * x + sum((w * (x - n) for w, n in zip(weights, xn)))
        return rhs - applied
    theta = 1.01
    delta = 0.99
    sigma = theta / delta
    x = thermal_prev
    d = residual_of(x) / (theta * diag)
    x = x + d
    rho = 1.0 / sigma
    for sweep in range(SWEEPS - 1):
        r = residual_of(x)
        rho_new = 1.0 / (2.0 * sigma - rho)
        d = rho_new * rho * d + 2.0 * rho_new / delta * r / diag
        x = x + d
        rho = rho_new
    trows = to_rows(x, N_GZ, N_GX, N_GY)
    back = from_rows(trows[slab, tile_x, tile_y, block], DL, DXD)
    mobility = mobility_prev * jnp.exp(-0.7 * back)
    ionization = jnp.exp(-2.0 * (1.0 + 0.3 * back) / jnp.sqrt(esq + 1.0))
    return (x, mobility, ionization)
```

```python
import jax
import jax.numpy as jnp
from jax import lax
from jax.sharding import PartitionSpec as P

SWEEPS = 6


def with_halo(cells, sides, width):
    for axis, dim in sides:
        count = lax.axis_size(axis)
        ends = count - 1
        head = lax.slice_in_dim(cells, 0, width, axis=dim)
        tail = lax.slice_in_dim(cells, cells.shape[dim] - width, cells.shape[dim], axis=dim)
        cells = jnp.concatenate(
            [
                lax.ppermute(tail, axis, [(i, (i + 1) % count) for i in range(ends)]),
                cells,
                lax.ppermute(head, axis, [((i + 1) % count, i) for i in range(ends)]),
            ],
            axis=dim,
        )
    return cells


def neighbours(padded):
    return [
        padded[2:, 1:-1, 1:-1],
        padded[:-2, 1:-1, 1:-1],
        padded[1:-1, 2:, 1:-1],
        padded[1:-1, :-2, 1:-1],
        padded[1:-1, 1:-1, 2:],
        padded[1:-1, 1:-1, :-2],
    ]


def send_heat(outgoing, labels):
    peers, slots, width = outgoing.shape
    received, ids = (
        lax.all_to_all(outgoing, ("gx", "gy"), split_axis=0, concat_axis=0, tiled=True),
        lax.all_to_all(labels, ("gx", "gy"), split_axis=0, concat_axis=0, tiled=True),
    )
    return (received.reshape(peers * slots, width), ids.reshape(peers * slots))


def send_back(replies):
    peers, slots, width = replies.shape
    returned = lax.all_to_all(replies, ("gx", "gy"), split_axis=0, concat_axis=0, tiled=True)
    return returned.reshape(peers * slots, width)


def per_device(
    efield,
    density,
    mobility_prev,
    thermal_prev,
    owner,
    block,
    live,
    material,
    mat_conductivity,
    mat_softening,
    mat_capacity,
):
    layers, xcells, width = density.shape
    nrows = layers * xcells
    across = lax.axis_size("gx")
    along = lax.axis_size("gy")
    peers = across * along
    slots = max(2, 2 * nrows // peers)
    esq = efield[0] * efield[0] + efield[1] * efield[1] + efield[2] * efield[2]
    heat = 0.2 * density * mobility_prev * esq
    column = lax.broadcasted_iota(jnp.int32, (layers, xcells, width), 2)
    heat = jnp.where(column < live.reshape(layers, xcells, 1), heat, jnp.float32(0.0))
    heat_rows = heat.reshape(nrows, width)
    owners = owner.reshape(nrows)
    targets = block.reshape(nrows)
    order = jnp.arange(nrows, dtype=jnp.int32)
    earlier = (owners[:, None] == owners[None, :]) & (order[None, :] < order[:, None])
    position = jnp.sum(earlier.astype(jnp.int32), axis=1)
    destination = owners * slots + position
    nblocks = material.size
    outgoing = jnp.zeros((peers * slots, width), jnp.float32).at[destination].set(heat_rows)
    labels = jnp.full((peers * slots,), nblocks, jnp.int32).at[destination].set(targets)
    received, ids = send_heat(outgoing.reshape(peers, slots, width), labels.reshape(peers, slots))
    picks = (jnp.arange(nblocks, dtype=jnp.int32)[:, None] == ids[None, :]).astype(jnp.float32)
    source_rows = jnp.dot(
        picks, received, precision=lax.Precision.HIGHEST, preferred_element_type=jnp.float32
    )
    tlayers, txcells, _ = thermal_prev.shape
    source = source_rows.reshape(tlayers, txcells, width)
    choose = (
        material.reshape(tlayers, txcells, 1, 1)
        == jnp.arange(mat_conductivity.shape[0], dtype=jnp.int32)
    ).astype(jnp.float32)
    k_base = jnp.sum(choose * mat_conductivity, -1)
    k_soft = jnp.sum(choose * mat_softening, -1)
    capf = jnp.sum(choose * mat_capacity, -1)
    cond = k_base / (1.0 + k_soft * thermal_prev)
    rhs = capf * thermal_prev + source
    cond_padded = with_halo(cond, (("gx", 1), ("gy", 2), ("gz", 0)), 1)
    fixed_weights = [0.5 * (cond + n) for n in neighbours(cond_padded)]
    fixed_diag = capf + sum(fixed_weights)

    def residual_of(x):
        padded = with_halo(x, (("gx", 1), ("gy", 2), ("gz", 0)), 1)
        applied = capf * x + sum((w * (x - n) for w, n in zip(fixed_weights, neighbours(padded))))
        return (rhs - applied, fixed_diag)

    theta = 1.01
    delta = 0.99
    sigma = theta / delta
    x = thermal_prev
    r, diag = residual_of(x)
    d = r / (theta * diag)
    x = x + d
    rho = 1.0 / sigma
    for sweep in range(SWEEPS - 1):
        r, diag = residual_of(x)
        rho_new = 1.0 / (2.0 * sigma - rho)
        d = rho_new * rho * d + 2.0 * rho_new / delta * r / diag
        x = x + d
        rho = rho_new
    thermal_rows = x.reshape(nblocks, width)
    valid = (ids < nblocks).astype(jnp.float32)
    replies = jnp.take(thermal_rows, jnp.minimum(ids, nblocks - 1), axis=0) * valid[:, None]
    returned = send_back(replies.reshape(peers, slots, width))
    back = returned[destination].reshape(layers, xcells, width)
    mobility = mobility_prev * jnp.exp(-0.7 * back)
    ionization = jnp.exp(-2.0 * (1.0 + 0.3 * back) / jnp.sqrt(esq + 1.0))
    return (x, mobility, ionization)


def solution(mesh):
    placed = (
        P(None, "gz", "gx", "gy"),
        P("gz", "gx", "gy"),
        P("gz", "gx", "gy"),
        P("gz", "gx", "gy"),
        P("gz", "gx", "gy", None, None),
        P("gz", "gx", "gy", None),
        P("gz", "gx", "gy", None),
        P("gz", "gx", "gy", None),
        P(),
        P(),
        P(),
    )
    return jax.shard_map(
        per_device,
        mesh=mesh,
        in_specs=placed,
        out_specs=(P("gz", "gx", "gy"), P("gz", "gx", "gy"), P("gz", "gx", "gy")),
        check_vma=False,
    )
```

```python
import functools

import jax
import jax.numpy as jnp
from jax import lax
from jax.experimental import pallas as pl
from jax.experimental.pallas import tpu as pltpu
from jax.sharding import PartitionSpec as P

SWEEPS = 6
THETA = 1.01
DELTA = 0.99
LANES = 128
EDGE = 8
F32 = jnp.float32
BF16 = jnp.bfloat16
I32 = jnp.int32


def steps():
    sigma = THETA / DELTA
    rho = 1.0 / sigma
    found = [(0.0, 1.0 / THETA)]
    for _ in range(SWEEPS - 1):
        rho_new = 1.0 / (2.0 * sigma - rho)
        found.append((rho_new * rho, 2.0 * rho_new / DELTA))
        rho = rho_new
    return found


def iota(shape, dim):
    return lax.broadcasted_iota(I32, shape, dim)


def dot(a, b, ca, cb):
    return lax.dot_general(a, b, (((ca,), (cb,)), ((), ())), preferred_element_type=F32)


def parts(v):
    high = v.astype(BF16)
    return high, (v - high.astype(F32)).astype(BF16)


def pick_rows(hot, rows):
    high, low = parts(rows)
    got = dot(hot, jnp.concatenate([high, low], axis=1), 1, 0)
    width = rows.shape[1]
    return got[:, :width] + got[:, width:]


def column(row):
    same = iota((LANES, LANES), 0) == iota((LANES, LANES), 1)
    found = []
    for at in range(0, row.shape[1], LANES):
        piece = jnp.broadcast_to(row[:, at : at + LANES], (LANES, LANES))
        found.append(jnp.sum(jnp.where(same, piece, 0), axis=1, keepdims=True))
    return jnp.concatenate(found, axis=0)


def hot_of(cond):
    return jnp.where(cond, F32(1.0), F32(0.0)).astype(BF16)


def edge_lanes():
    r, y = iota((2 * EDGE, LANES), 0), iota((2 * EDGE, LANES), 1)
    return hot_of(y == jnp.where(r < EDGE, r, r + LANES - 2 * EDGE))


def call(kernel, outs, ins, name, scratch=(), limit=32, flops=0, smem=()):
    bytes_of = lambda a: a.size * a.dtype.itemsize
    return pl.pallas_call(
        kernel,
        out_shape=[jax.ShapeDtypeStruct(s, t) for s, t in outs],
        in_specs=[
            pl.BlockSpec(memory_space=pltpu.SMEM if i in smem else pltpu.VMEM)
            for i in range(len(ins))
        ],
        out_specs=[pl.BlockSpec(memory_space=pltpu.VMEM) for _ in outs],
        scratch_shapes=list(scratch),
        compiler_params=pltpu.CompilerParams(vmem_limit_bytes=limit << 20),
        cost_estimate=pl.CostEstimate(
            flops=flops,
            bytes_accessed=sum(bytes_of(a) for a in ins)
            + sum(jax.ShapeDtypeStruct(s, t).size * 4 for s, t in outs),
            transcendentals=0,
        ),
        name=name,
    )(*ins)


def dispatch_kernel(peers, slots, ef, den, mob, owner, block, live, out):
    n = owner.shape[1]
    esq = ef[0] * ef[0] + ef[1] * ef[1] + ef[2] * ef[2]
    heat = 0.2 * den[...] * mob[...] * esq
    heat = jnp.where(iota(heat.shape, 1) < column(live[...]), heat, F32(0.0))
    own = owner[...]
    own_col = column(own)
    pos = jnp.zeros((1, n), I32)
    for at in range(0, n, LANES):
        r = iota((LANES, n), 0) + at
        earlier = (own_col[at : at + LANES] == own) & (r < iota((LANES, n), 1))
        pos = pos + jnp.sum(jnp.where(earlier, 1, 0), axis=0, keepdims=True)
    dest = own * (slots + 1) + pos
    hot = hot_of(iota((peers * (slots + 1), n), 0) == dest)
    out[...] = pick_rows(hot, heat)
    named = hot_of(iota((peers, n), 0) == own)
    at_slot = iota((LANES, n), 0) == pos
    code = block[...] + 1
    high = jnp.where(at_slot, code // 32, 0).astype(F32).astype(BF16)
    low = jnp.where(at_slot, code % 32, 0).astype(F32).astype(BF16)
    out[pl.ds(slots, peers, stride=slots + 1), :] = dot(named, high, 1, 1) * 32.0 + dot(named, low, 1, 1)


def after_kernel(slots, ef, owner, gain, dest):
    n = owner.shape[1]
    esq = ef[0] * ef[0] + ef[1] * ef[1] + ef[2] * ef[2]
    gain[...] = -2.0 * lax.rsqrt(esq + 1.0)
    own = owner[...]
    own_col = column(own)
    for at in range(0, n, LANES):
        r = iota((LANES, n), 0) + at
        piece = own_col[at : at + LANES]
        earlier = (piece == own) & (iota((LANES, n), 1) < r)
        pos = jnp.sum(jnp.where(earlier, 1, 0), axis=1, keepdims=True)
        dest[pl.ds(at, LANES), :] = jnp.broadcast_to(piece * slots + pos, (LANES, LANES))


def labels_of(received, peers, slots):
    got = received[pl.ds(slots, peers, stride=slots + 1), :]
    high = jnp.floor(got * (1.0 / 32.0))
    return high.astype(BF16), (got - 32.0 * high).astype(BF16)


def combine_kernel(peers, slots, far, received, source, first, last):
    n = source.shape[0]
    total = received.shape[0]
    high, low = labels_of(received, peers, slots)
    j = iota((LANES, total), 1)
    spread = hot_of(iota((LANES, total), 0) == j - (slots + 1) * lax.div(j, slots + 1))
    named = dot(high, spread, 1, 0) * 32.0 + dot(low, spread, 1, 0)
    mine = iota((peers, total), 0) == lax.div(iota((peers, total), 1), slots + 1)
    ids = jnp.sum(jnp.where(mine, named, 0.0), axis=0, keepdims=True).astype(I32)
    picks = hot_of(iota((n, total), 0) + 1 == ids)
    source[...] = pick_rows(picks, received[...])
    rows = far * (n // 4)
    first[...] = source[pl.ds(0, rows), :]
    last[...] = source[pl.ds(n - rows, rows), :]


def ids_kernel(peers, slots, received, ids):
    total = peers * slots
    high, low = labels_of(received, peers, slots)
    own = hot_of(lax.div(iota((total, peers), 0), slots) == iota((total, peers), 1))
    named = dot(own, high, 1, 0) * 32.0 + dot(own, low, 1, 0)
    i = iota((total, LANES), 0)
    mine = iota((total, LANES), 1) == i - slots * lax.div(i, slots)
    found = jnp.sum(jnp.where(mine, named, 0.0), axis=1, keepdims=True) - 1.0
    ids[...] = jnp.broadcast_to(found, (total, LANES)).astype(I32)


def start_z_kernel(far, x0, material, near, up, down):
    layers, xcells = material.shape
    n = layers * xcells
    mat = (material[...] + 1).astype(F32)
    rows = far * xcells
    zeros = lambda k: jnp.zeros((k, LANES), F32)
    near[pl.ds(0, n), :] = x0[...]
    near[pl.ds(n, EDGE), :] = jnp.concatenate([mat, zeros(EDGE - layers)], axis=0)
    up[pl.ds(0, rows), :] = x0[pl.ds(n - rows, rows), :]
    up[pl.ds(rows, EDGE), :] = jnp.concatenate([mat[layers - far :], zeros(EDGE - far)], axis=0)
    down[pl.ds(0, rows), :] = x0[pl.ds(0, rows), :]
    down[pl.ds(rows, EDGE), :] = jnp.concatenate([mat[:far], zeros(EDGE - far)], axis=0)


def layers_of(far, pieces):
    low2, low, own, high, high2 = pieces
    found = [(low2, k) for k in range(far)]
    for ref in (low, own, high):
        found += [(ref, k) for k in range(4)]
    return found + [(high2, k) for k in range(far)]


def start_x_kernel(far, low2, low, own, high, high2, xz, mats, xlow, xhigh):
    found = layers_of(far, (low2, low, own, high, high2))
    count = len(found)
    for k, (ref, at) in enumerate(found):
        piece = ref[pl.ds(at * LANES, LANES), :]
        xz[k] = piece
        xlow[pl.ds(k * EDGE, EDGE), :] = piece[:EDGE]
        xhigh[pl.ds(k * EDGE, EDGE), :] = piece[LANES - EDGE :]
        tail = ref.shape[0] - EDGE
        mats[pl.ds(k, 1), :] = ref[pl.ds(tail + at, 1), :]
    xlow[pl.ds(count * EDGE, count), :] = mats[...]
    xhigh[pl.ds(count * EDGE, count), :] = mats[...]


def start_y_kernel(xz, mats, after, before, xm, around, ylow, yhigh):
    count = xz.shape[0]
    for k in range(count):
        xm[k, pl.ds(0, LANES)] = xz[k]
        xm[k, pl.ds(LANES, EDGE)] = after[pl.ds(k * EDGE, EDGE), :]
        xm[k, pl.ds(LANES + EDGE, EDGE)] = before[pl.ds(k * EDGE, EDGE), :]
    around[pl.ds(0, count), :] = mats[...]
    around[pl.ds(count, count), :] = after[pl.ds(count * EDGE, count), :]
    around[pl.ds(2 * count, count), :] = before[pl.ds(count * EDGE, count), :]
    total = count * xm.shape[1]
    high, low = parts(xm[...].reshape(total, LANES))
    edges = edge_lanes()
    sides = dot(edges, high, 1, 1) + dot(edges, low, 1, 1)
    ylow[:, pl.ds(0, total)] = sides[:EDGE]
    yhigh[:, pl.ds(0, total)] = sides[EDGE:]
    for b in range(3 * count // EDGE):
        block = around[pl.ds(b * EDGE, EDGE), :]
        ylow[:, pl.ds(total + b * LANES, LANES)] = block
        yhigh[:, pl.ds(total + b * LANES, LANES)] = block


def turned(v, by, axis):
    return pltpu.roll(v, by % v.shape[axis], axis)


def east(m, s):
    last = iota(m.shape, 1) == LANES - 1
    rm, rs = turned(m, -1, 1), turned(s, -1, 1)
    return jnp.where(last, rs, rm), jnp.where(last, rm, rs)


def west(m, s):
    first = iota(m.shape, 1) == 0
    rm, rs = turned(m, 1, 1), turned(s, 1, 1)
    return jnp.where(first, rs, rm), jnp.where(first, rm, rs)


def weights_kernel(xm, around, left, right, base, soft, heat, xs, wz, wx, wy, inv, b0, cond, capf, flip):
    count, rows, _ = xm.shape
    total = count * rows
    edges = edge_lanes()
    high, low = parts(jnp.concatenate([right[:, :total], left[:, :total]], axis=0))
    xs[...] = (dot(high, edges, 0, 0) + dot(low, edges, 0, 0)).reshape(count, rows, LANES)
    depth = 3 * count

    def table(mat, values):
        found = jnp.zeros(mat.shape, F32)
        for m in range(values.shape[0]):
            found = jnp.where(mat == F32(m + 1), values[m], found)
        return found

    def unpacked(ref):
        return jnp.concatenate(
            [ref[:, pl.ds(total + b * LANES, LANES)] for b in range(depth // EDGE)], axis=0
        )

    pad = jnp.zeros((LANES - depth, LANES), F32)
    for i, mat in enumerate((around[...], unpacked(left), unpacked(right))):
        for j, values in enumerate((base, soft, heat)):
            flip[i, j] = jnp.transpose(jnp.concatenate([table(mat, values), pad], axis=0))

    def col(i, j, k):
        own = flip[i, j, :, pl.ds(k, 1)]
        after = flip[i, j, pl.ds(0, EDGE), pl.ds(count + k, 1)]
        before = flip[i, j, pl.ds(LANES - EDGE, EDGE), pl.ds(2 * count + k, 1)]
        return jnp.broadcast_to(jnp.concatenate([own, after, before], axis=0), (rows, LANES))

    hither = iota((rows, LANES), 1) < LANES // 2
    for k in range(count):
        cond[0, k] = col(0, 0, k) / (1.0 + col(0, 1, k) * xm[k])
        capf[0, k] = col(0, 2, k)
        side = [jnp.where(hither, col(2, j, k), col(1, j, k)) for j in range(3)]
        cond[1, k] = side[0] / (1.0 + side[1] * xs[k])
        capf[1, k] = side[2]

    wz[0, 0] = 0.5 * (cond[0, 0] + cond[0, 1])
    wz[0, 1] = 0.5 * (cond[1, 0] + cond[1, 1])

    @pl.loop(0, count - 2)
    def _(j):
        k = j + 1
        c = (cond[0, k], cond[1, k])
        e = east(*c)
        wyy = tuple(0.5 * (c[t] + e[t]) for t in range(2))
        w = west(*wyy)
        for t in range(2):
            up = 0.5 * (c[t] + cond[t, k + 1])
            wz[k, t] = up
            wxx = 0.5 * (c[t] + turned(c[t], -1, 0))
            wx[j, t] = wxx
            wy[j, t] = wyy[t]
            cf = capf[t, k]
            diag = cf + up + wz[j, t] + wxx + turned(wxx, 1, 0) + wyy[t] + w[t]
            i = jnp.where(cf > 0.0, 1.0 / diag, 0.0)
            inv[j, t] = i
            x = xm[k] if t == 0 else xs[k]
            b0[j, t] = cf * x * i


def source_x_kernel(far, low2, low, own, high, high2, xlow, xhigh):
    for k, (ref, at) in enumerate(layers_of(far, (low2, low, own, high, high2))):
        xlow[pl.ds(k * EDGE, EDGE), :] = ref[pl.ds(at * LANES, EDGE), :]
        xhigh[pl.ds(k * EDGE, EDGE), :] = ref[pl.ds((at + 1) * LANES - EDGE, EDGE), :]


def lay(found, after, before, put):
    for k, (ref, at) in enumerate(found):
        put(k, 0, LANES, ref[pl.ds(at * LANES, LANES), :])
        put(k, LANES, EDGE, after[pl.ds(k * EDGE, EDGE), :])
        put(k, LANES + EDGE, EDGE, before[pl.ds(k * EDGE, EDGE), :])


def source_y_kernel(far, low2, low, own, high, high2, after, before, ylow, yhigh, full):
    rows = LANES + 2 * EDGE

    def put(k, at, size, piece):
        full[pl.ds(k * rows + at, size), :] = piece

    lay(layers_of(far, (low2, low, own, high, high2)), after, before, put)
    big, small = parts(full[...])
    edges = edge_lanes()
    sides = dot(edges, big, 1, 1) + dot(edges, small, 1, 1)
    ylow[...] = sides[:EDGE]
    yhigh[...] = sides[EDGE:]


def sweep_kernel(far, xm, xs, wz, wx, wy, inv, b0, low2, low, own, high, high2, after, before, left, right, ids,
                 out, replies, b, d, xa, xb):
    count, rows, _ = xm.shape
    inner = count - 2

    def put(k, at, size, piece):
        part = pl.ds(at, size)
        b[k, 0, part] = b0[k, 0, part] + piece * inv[k, 0, part]

    lay(layers_of(far, (low2, low, own, high, high2)), after, before, put)
    edges = edge_lanes()
    big, small = parts(jnp.concatenate([right[...], left[...]], axis=0))
    side = dot(big, edges, 0, 0) + dot(small, edges, 0, 0)
    for k in range(inner):
        b[k, 1] = b0[k, 1] + side[k * rows : (k + 1) * rows] * inv[k, 1]

    for s, (keep, add) in enumerate(steps()):
        if s == 0:
            load = lambda k, t: xm[k] if t == 0 else xs[k]
        else:
            load = lambda k, t, src=(xa if s % 2 else xb): src[k, t]
        into = xb if s % 2 else xa

        @pl.loop(1 + s, count - 1 - s)
        def _(k):
            j = k - 1
            x = (load(k, 0), load(k, 1))
            e, w = east(*x), west(*x)
            we = (wy[j, 0], wy[j, 1])
            ww = west(*we)
            for t in range(2):
                wxx = wx[j, t]
                near = wz[k, t] * load(k + 1, t) + wz[k - 1, t] * load(k - 1, t)
                near += wxx * turned(x[t], -1, 0) + turned(wxx, 1, 0) * turned(x[t], 1, 0)
                near += we[t] * e[t] + ww[t] * w[t]
                step = add * (b[j, t] - x[t] + inv[j, t] * near)
                if s > 0:
                    step = step + keep * d[j, t]
                if s < SWEEPS - 1:
                    d[j, t] = step
                into[k, t] = x[t] + step

    final = xb if SWEEPS % 2 == 0 else xa
    for k in range(4):
        out[pl.ds(k * LANES, LANES), :] = final[SWEEPS + k, 0, pl.ds(0, LANES)]
    n = out.shape[0]
    name = ids[...]
    hot = jnp.concatenate([hot_of(name == iota(name.shape, 1) + at) for at in range(0, n, LANES)], axis=1)
    replies[...] = pick_rows(hot, out[...])


def final_kernel(returned, dest, gain, mob, mobility, ionization):
    total = returned.shape[0]
    name = dest[...]
    hot = jnp.concatenate([hot_of(name == iota(name.shape, 1) + at) for at in range(0, total, LANES)], axis=1)
    back = pick_rows(hot, returned[...])
    mobility[...] = mob[...] * jnp.exp(-0.7 * back)
    ionization[...] = jnp.exp(gain[...] * (1.0 + 0.3 * back))


def shifted(v, axis, by):
    count = lax.axis_size(axis)
    pairs = [(i, i + by) for i in range(count) if 0 <= i + by < count]
    return lax.ppermute(v, axis, pairs) if pairs else jnp.zeros_like(v)


def exchanged(v):
    lines = v.reshape(v.shape[0], 1, v.shape[1])
    return lax.all_to_all(lines, ("gx", "gy"), split_axis=0, concat_axis=0, tiled=True).reshape(v.shape)


def per_device(
    efield, density, mobility_prev, thermal_prev, owner, block, live, material,
    mat_conductivity, mat_softening, mat_capacity,
):
    layers, xcells, width = density.shape
    n = layers * xcells
    peers = lax.axis_size("gx") * lax.axis_size("gy")
    slots = max(2, 2 * n // peers)
    line = peers * (slots + 1)
    flat = lambda a: a.reshape(n, width)
    ef = efield.reshape(3, n, width)
    den, mob, x0 = flat(density), flat(mobility_prev), flat(thermal_prev)
    own, blk, liv = owner.reshape(1, n), block.reshape(1, n), live.reshape(1, n)
    mat = material.reshape(layers, xcells)
    sized = lambda *s: (s, F32)

    [sent] = call(functools.partial(dispatch_kernel, peers, slots), [sized(line, width)],
                  [ef, den, mob, own, blk, liv], "dispatch", flops=10**8)
    received = exchanged(sent)

    far = SWEEPS - layers
    count = layers + 2 * SWEEPS
    rows = xcells + 2 * EDGE
    near, up, down = call(
        functools.partial(start_z_kernel, far),
        [sized(n + EDGE, width), sized(far * xcells + EDGE, width), sized(far * xcells + EDGE, width)],
        [x0, mat], "start_z")
    low, high = shifted(near, "gz", 1), shifted(near, "gz", -1)
    low2, high2 = shifted(up, "gz", 2), shifted(down, "gz", -2)
    xz, mats, xlow, xhigh = call(
        functools.partial(start_x_kernel, far),
        [sized(count, xcells, width), sized(count, width)] + [sized(count * (EDGE + 1), width)] * 2,
        [low2, low, near, high, high2], "start_x")
    before, after = shifted(xhigh, "gx", 1), shifted(xlow, "gx", -1)
    long = count * rows + 3 * count * LANES // EDGE
    xm, around, ylow, yhigh = call(
        start_y_kernel,
        [sized(count, rows, width), sized(3 * count, width), sized(EDGE, long), sized(EDGE, long)],
        [xz, mats, after, before], "start_y")
    left, right = shifted(yhigh, "gy", 1), shifted(ylow, "gy", -1)
    pair = lambda k: sized(k, 2, rows, width)
    xs, wz, wx, wy, inv, b0 = call(
        weights_kernel,
        [sized(count, rows, width), pair(count - 1)] + [pair(count - 2)] * 4,
        [xm, around, left, right, mat_conductivity, mat_softening, mat_capacity], "weights",
        scratch=[pltpu.VMEM((2, count, rows, width), F32)] * 2 + [pltpu.VMEM((3, 3, LANES, LANES), F32)],
        limit=56, flops=10**7, smem=(4, 5, 6))
    gain, dest = call(functools.partial(after_kernel, slots), [sized(n, width), ((n, LANES), I32)], [ef, own], "gain")

    received, inv, gain, dest = lax.optimization_barrier((received, inv, gain, dest))
    far -= 1
    source, first, last = call(
        functools.partial(combine_kernel, peers, slots, far),
        [sized(n, width)] + [sized(far * xcells, width)] * 2, [received], "combine", flops=10**8)
    [ids] = call(functools.partial(ids_kernel, peers, slots), [((peers * slots, LANES), I32)], [received], "ids")
    low, high = shifted(source, "gz", 1), shifted(source, "gz", -1)
    low2, high2 = shifted(last, "gz", 2), shifted(first, "gz", -2)
    around_z = [low2, low, source, high, high2]
    inner = count - 2
    xlow, xhigh = call(functools.partial(source_x_kernel, far), [sized(inner * EDGE, width)] * 2, around_z, "source_x")
    before, after = shifted(xhigh, "gx", 1), shifted(xlow, "gx", -1)
    ylow, yhigh = call(
        functools.partial(source_y_kernel, far), [sized(EDGE, inner * rows)] * 2,
        around_z + [after, before], "source_y", scratch=[pltpu.VMEM((inner * rows, width), F32)])
    left, right = shifted(yhigh, "gy", 1), shifted(ylow, "gy", -1)
    x, replies = call(
        functools.partial(sweep_kernel, far), [sized(n, width), sized(peers * slots, width)],
        [xm, xs, wz, wx, wy, inv, b0] + around_z + [after, before, left, right, ids], "sweeps",
        scratch=[pltpu.VMEM((inner, 2, rows, width), F32)] * 2 + [pltpu.VMEM((count, 2, rows, width), F32)] * 2,
        limit=60, flops=10**8)
    returned = exchanged(replies)
    mobility, ionization = call(final_kernel, [sized(n, width)] * 2, [returned, dest, gain, mob], "finish", flops=10**8)
    shape = density.shape
    return x.reshape(shape), mobility.reshape(shape), ionization.reshape(shape)


def solution(mesh):
    tile = P("gz", "gx", "gy")
    rows = P("gz", "gx", "gy", None)
    placed = (
        P(None, "gz", "gx", "gy"), tile, tile, tile,
        P("gz", "gx", "gy", None, None), rows, rows, rows, P(), P(), P(),
    )
    return jax.shard_map(
        per_device, mesh=mesh, in_specs=placed, out_specs=(tile, tile, tile), check_vma=False
    )
```

```python
import functools

import jax
import jax.numpy as jnp
from jax import lax
from jax.experimental import pallas as pl
from jax.experimental.pallas import tpu as pltpu
from jax.sharding import PartitionSpec as P

SWEEPS = 6
THETA = 1.01
DELTA = 0.99
LANES = 128
EDGE = 8
F32 = jnp.float32
BF16 = jnp.bfloat16
I32 = jnp.int32


def steps():
    sigma = THETA / DELTA
    rho = 1.0 / sigma
    found = [(0.0, 1.0 / THETA)]
    for _ in range(SWEEPS - 1):
        rho_new = 1.0 / (2.0 * sigma - rho)
        found.append((rho_new * rho, 2.0 * rho_new / DELTA))
        rho = rho_new
    return found


def iota(shape, dim):
    return lax.broadcasted_iota(I32, shape, dim)


def dot(a, b, ca, cb):
    return lax.dot_general(a, b, (((ca,), (cb,)), ((), ())), preferred_element_type=F32)


def parts(v):
    high = v.astype(BF16)
    return high, (v - high.astype(F32)).astype(BF16)


def pick_rows(hot, rows):
    high, low = parts(rows)
    got = dot(hot, jnp.concatenate([high, low], axis=1), 1, 0)
    width = rows.shape[1]
    return got[:, :width] + got[:, width:]


def column(row):
    same = iota((LANES, LANES), 0) == iota((LANES, LANES), 1)
    found = []
    for at in range(0, row.shape[1], LANES):
        piece = jnp.broadcast_to(row[:, at : at + LANES], (LANES, LANES))
        found.append(jnp.sum(jnp.where(same, piece, 0), axis=1, keepdims=True))
    return jnp.concatenate(found, axis=0)


def hot_of(cond):
    return jnp.where(cond, F32(1.0), F32(0.0)).astype(BF16)


def edge_lanes():
    r, y = iota((2 * EDGE, LANES), 0), iota((2 * EDGE, LANES), 1)
    return hot_of(y == jnp.where(r < EDGE, r, r + LANES - 2 * EDGE))


def call(kernel, outs, ins, name, scratch=(), limit=32, flops=0, smem=()):
    bytes_of = lambda a: a.size * a.dtype.itemsize
    return pl.pallas_call(
        kernel,
        out_shape=[jax.ShapeDtypeStruct(s, t) for s, t in outs],
        in_specs=[
            pl.BlockSpec(memory_space=pltpu.SMEM if i in smem else pltpu.VMEM)
            for i in range(len(ins))
        ],
        out_specs=[pl.BlockSpec(memory_space=pltpu.VMEM) for _ in outs],
        scratch_shapes=list(scratch),
        compiler_params=pltpu.CompilerParams(vmem_limit_bytes=limit << 20),
        cost_estimate=pl.CostEstimate(
            flops=flops,
            bytes_accessed=sum(bytes_of(a) for a in ins)
            + sum(jax.ShapeDtypeStruct(s, t).size * 4 for s, t in outs),
            transcendentals=0,
        ),
        name=name,
    )(*ins)


def dispatch_kernel(peers, slots, ef, den, mob, owner, block, live, out):
    n = owner.shape[1]
    esq = ef[0] * ef[0] + ef[1] * ef[1] + ef[2] * ef[2]
    heat = 0.2 * den[...] * mob[...] * esq
    heat = jnp.where(iota(heat.shape, 1) < column(live[...]), heat, F32(0.0))
    own = owner[...]
    own_col = column(own)
    pos = jnp.zeros((1, n), I32)
    for at in range(0, n, LANES):
        r = iota((LANES, n), 0) + at
        earlier = (own_col[at : at + LANES] == own) & (r < iota((LANES, n), 1))
        pos = pos + jnp.sum(jnp.where(earlier, 1, 0), axis=0, keepdims=True)
    dest = own * (slots + 1) + pos
    hot = hot_of(iota((peers * (slots + 1), n), 0) == dest)
    out[...] = pick_rows(hot, heat)
    named = hot_of(iota((peers, n), 0) == own)
    at_slot = iota((LANES, n), 0) == pos
    code = block[...] + 1
    high = jnp.where(at_slot, code // 32, 0).astype(F32).astype(BF16)
    low = jnp.where(at_slot, code % 32, 0).astype(F32).astype(BF16)
    out[pl.ds(slots, peers, stride=slots + 1), :] = dot(named, high, 1, 1) * 32.0 + dot(named, low, 1, 1)


def after_kernel(slots, ef, owner, gain, dest):
    n = owner.shape[1]
    esq = ef[0] * ef[0] + ef[1] * ef[1] + ef[2] * ef[2]
    gain[...] = -2.0 * lax.rsqrt(esq + 1.0)
    own = owner[...]
    own_col = column(own)
    for at in range(0, n, LANES):
        r = iota((LANES, n), 0) + at
        piece = own_col[at : at + LANES]
        earlier = (piece == own) & (iota((LANES, n), 1) < r)
        pos = jnp.sum(jnp.where(earlier, 1, 0), axis=1, keepdims=True)
        dest[pl.ds(at, LANES), :] = jnp.broadcast_to(piece * slots + pos, (LANES, LANES))


def labels_of(received, peers, slots):
    got = received[pl.ds(slots, peers, stride=slots + 1), :]
    high = jnp.floor(got * (1.0 / 32.0))
    return high.astype(BF16), (got - 32.0 * high).astype(BF16)


def combine_kernel(peers, slots, far, place, received, source, far_a, far_b):
    n = source.shape[0]
    total = received.shape[0]
    high, low = labels_of(received, peers, slots)
    j = iota((LANES, total), 1)
    spread = hot_of(iota((LANES, total), 0) == j - (slots + 1) * lax.div(j, slots + 1))
    named = dot(high, spread, 1, 0) * 32.0 + dot(low, spread, 1, 0)
    mine = iota((peers, total), 0) == lax.div(iota((peers, total), 1), slots + 1)
    ids = jnp.sum(jnp.where(mine, named, 0.0), axis=0, keepdims=True).astype(I32)
    picks = hot_of(iota((n, total), 0) + 1 == ids)
    source[...] = pick_rows(picks, received[...])
    rows = far * (n // 4)
    first, last = source[pl.ds(0, rows), :], source[pl.ds(n - rows, rows), :]
    even = place[3] == 0
    far_a[...] = jnp.where(even, last, first)
    far_b[...] = jnp.where(even, first, last)


def ids_kernel(peers, slots, received, ids):
    total = peers * slots
    high, low = labels_of(received, peers, slots)
    own = hot_of(lax.div(iota((total, peers), 0), slots) == iota((total, peers), 1))
    named = dot(own, high, 1, 0) * 32.0 + dot(own, low, 1, 0)
    i = iota((total, LANES), 0)
    mine = iota((total, LANES), 1) == i - slots * lax.div(i, slots)
    found = jnp.sum(jnp.where(mine, named, 0.0), axis=1, keepdims=True) - 1.0
    ids[...] = jnp.broadcast_to(found, (total, LANES)).astype(I32)


def start_z_kernel(far, place, x0, material, near, far_a, far_b):
    layers, xcells = material.shape
    n = layers * xcells
    mat = (material[...] + 1).astype(F32)
    rows = far * xcells
    zeros = lambda k: jnp.zeros((k, LANES), F32)
    near[pl.ds(0, n), :] = x0[...]
    near[pl.ds(n, EDGE), :] = jnp.concatenate([mat, zeros(EDGE - layers)], axis=0)
    up, down = x0[pl.ds(n - rows, rows), :], x0[pl.ds(0, rows), :]
    mat_up = jnp.concatenate([mat[layers - far :], zeros(EDGE - far)], axis=0)
    mat_down = jnp.concatenate([mat[:far], zeros(EDGE - far)], axis=0)
    even = place[3] == 0
    far_a[pl.ds(0, rows), :] = jnp.where(even, up, down)
    far_b[pl.ds(0, rows), :] = jnp.where(even, down, up)
    far_a[pl.ds(rows, EDGE), :] = jnp.where(even, mat_up, mat_down)
    far_b[pl.ds(rows, EDGE), :] = jnp.where(even, mat_down, mat_up)


def layer_readers(far, place, far_a, far_b, near_a, near_b, own):
    even, even2 = place[2] == 0, place[3] == 0

    def one(k, ref):
        return lambda at, size: ref[pl.ds(k * LANES + at, size), :]

    def either(k, cond, yes, no):
        return lambda at, size: jnp.where(cond, one(k, yes)(at, size), one(k, no)(at, size))

    found = [either(k, even2, far_b, far_a) for k in range(far)]
    found += [either(k, even, near_b, near_a) for k in range(4)]
    found += [one(k, own) for k in range(4)]
    found += [either(k, even, near_a, near_b) for k in range(4)]
    return found + [either(k, even2, far_a, far_b) for k in range(far)]


def start_x_kernel(far, place, far_a, far_b, near_a, near_b, own, xz, mats, xa, xb):
    readers = layer_readers(far, place, far_a, far_b, near_a, near_b, own)
    count = len(readers)
    even = place[0] == 0
    for k, read in enumerate(readers):
        piece = read(0, LANES)
        xz[k] = piece
        low, high = piece[:EDGE], piece[LANES - EDGE :]
        xa[pl.ds(k * EDGE, EDGE), :] = jnp.where(even, high, low)
        xb[pl.ds(k * EDGE, EDGE), :] = jnp.where(even, low, high)
    tail = [far * LANES] * far + [4 * LANES] * 12 + [far * LANES] * far
    at = list(range(far)) + list(range(4)) * 3 + list(range(far))
    for k, read in enumerate(readers):
        mats[pl.ds(k, 1), :] = read(tail[k] + at[k] - at[k] * LANES, 1)
    xa[pl.ds(count * EDGE, count), :] = mats[...]
    xb[pl.ds(count * EDGE, count), :] = mats[...]


def flat_sides(rows):
    high, low = parts(rows)
    edges = edge_lanes()
    return dot(edges, high, 1, 1) + dot(edges, low, 1, 1)


def start_y_kernel(place, xz, mats, xa, xb, xm, sides, flat_mat, ya, yb):
    count = xz.shape[0]
    even = place[0] == 0
    after, before = jnp.where(even, xa[...], xb[...]), jnp.where(even, xb[...], xa[...])
    blank = jnp.zeros((EDGE, LANES), F32)
    for k in range(count):
        part = slice(k * EDGE, (k + 1) * EDGE)
        xm[k, pl.ds(0, EDGE)] = blank
        xm[k, pl.ds(EDGE, EDGE)] = before[part]
        xm[k, pl.ds(2 * EDGE, LANES)] = xz[k]
        xm[k, pl.ds(LANES + 2 * EDGE, EDGE)] = after[part]
        xm[k, pl.ds(LANES + 3 * EDGE, EDGE)] = blank
    rows = LANES + 2 * EDGE
    total = count * rows
    found = flat_sides(xm[:, EDGE : EDGE + rows].reshape(total, LANES))
    sides[...] = found
    around = jnp.concatenate([before[count * EDGE :], mats[...], after[count * EDGE :]], axis=0)
    q = iota((1, total), 1)
    layer = lax.div(q, rows)
    row = q - layer * rows
    tile = jnp.where(row < EDGE, 0, jnp.where(row < LANES + EDGE, 1, 2))
    lane = row - EDGE + LANES * (1 - tile)
    spread = hot_of(iota((LANES, total), 0) == lane)
    named = dot(around.astype(BF16), spread, 1, 0)
    mine = iota((3 * count, total), 0) == tile * count + layer
    mat = jnp.sum(jnp.where(mine, named, 0.0), axis=0, keepdims=True)
    mat = jnp.where(iota((EDGE, total), 0) == 0, mat, 0.0)
    flat_mat[...] = mat
    even = place[1] == 0
    ya[pl.ds(0, EDGE), :] = jnp.where(even, found[EDGE:], found[:EDGE])
    yb[pl.ds(0, EDGE), :] = jnp.where(even, found[:EDGE], found[EDGE:])
    ya[pl.ds(EDGE, EDGE), :] = mat
    yb[pl.ds(EDGE, EDGE), :] = mat


def three_parts(v):
    high = v.astype(BF16)
    rest = v - high.astype(F32)
    mid = rest.astype(BF16)
    return high, mid, (rest - mid.astype(F32)).astype(BF16)


def ends_of(strip):
    return jnp.concatenate([strip[EDGE - 1 : EDGE], strip[3 * EDGE : 3 * EDGE + 1]], axis=0)


def end_lanes(depth, times):
    r, y = iota((depth, times * LANES), 0), iota((depth, times * LANES), 1)
    first = (r % 2 == 0) & (y == (r // 2) * LANES)
    last = (r % 2 == 1) & (y == (r // 2) * LANES + LANES - 1)
    return hot_of(first | last)


def turned(v, by, axis):
    return pltpu.roll(v, by % v.shape[axis], axis)


def strip_of(sides, before, after):
    return jnp.concatenate([before, sides, after], axis=0)


def weights_kernel(place, base, soft, heat, xm, sides, flat_mat, ya, yb, wz, wx, wy, wyw, inv, b0, strips, cond, cols, ends):
    count, rows = inv.shape[0], inv.shape[1]
    total = count * rows
    even = place[1] == 0
    after, before = jnp.where(even, ya[...], yb[...]), jnp.where(even, yb[...], ya[...])
    mat = jnp.concatenate([flat_mat[0:1], before[EDGE : EDGE + 1], after[EDGE : EDGE + 1]], axis=0)
    tables = []
    for values in (base, soft, heat):
        found = jnp.zeros(mat.shape, F32)
        for m in range(values.shape[0]):
            found = jnp.where(mat == F32(m + 1), values[m], found)
        tables.append(found)
    own = [p for t in tables for p in three_parts(t[0:1])]
    r, y = iota((9, 3 * LANES), 0), iota((9, 3 * LANES), 1)
    cols[...] = dot(jnp.concatenate(own, axis=0), hot_of(lax.div(r, 3) == lax.div(y, LANES)), 0, 0)
    wide = lambda t, i: jnp.broadcast_to(t[i : i + 1], (EDGE, total))
    kb, ks, cf = (jnp.concatenate([wide(t, 1), wide(t, 0), wide(t, 0), wide(t, 2)], axis=0) for t in tables)
    sx = strip_of(sides[...], before[:EDGE], after[:EDGE])
    sc = kb / (1.0 + ks * sx)
    down = lambda by, axis: 0.5 * (sc + turned(sc, by, axis))
    around = [down(rows, 1), down(-rows, 1), down(1, 1), down(-1, 1), down(1, 0), down(-1, 0)]
    diag = cf
    for w in around:
        diag = diag + w
    si = jnp.where(cf > 0.0, 1.0 / diag, 0.0)
    for i, w in enumerate(around):
        strips[i] = w * si
    strips[6] = si
    strips[7] = cf * sx * si
    strips[8] = sx
    got = [dot(p, end_lanes(2, 1), 0, 0) for p in three_parts(ends_of(sc))]
    ends[...] = got[0] + got[1] + got[2]

    piece = 16
    blank = jnp.zeros((EDGE, LANES), F32)

    @pl.loop(0, count)
    def _(k):
        cond[k, pl.ds(0, EDGE)] = blank
        cond[k, pl.ds(rows + EDGE, EDGE)] = blank
        wx[k, pl.ds(0, EDGE)] = blank
        wx[k, pl.ds(rows + EDGE, EDGE)] = blank
        for at in range(0, rows, piece):
            part = pl.ds(pl.multiple_of(k * rows + at, 8), piece)
            x = xm[k, pl.ds(EDGE + at, piece)]
            cond[k, pl.ds(EDGE + at, piece)] = cols[part, 0:LANES] / (1.0 + cols[part, LANES : 2 * LANES] * x)

    first, last = iota((piece, LANES), 1) == 0, iota((piece, LANES), 1) == LANES - 1
    wz[0] = 0.5 * (cond[0, pl.ds(EDGE, rows)] + cond[1, pl.ds(EDGE, rows)])

    @pl.loop(1, count - 1)
    def _(k):
        for at in range(0, rows, piece):
            here = pl.ds(EDGE + at, piece)
            part = pl.ds(pl.multiple_of(k * rows + at, 8), piece)
            to = pl.ds(at, piece)
            c, end = cond[k, here], ends[part, :]
            up = 0.5 * (c + cond[k + 1, here])
            low = 0.5 * (c + cond[k - 1, here])
            right = 0.5 * (c + cond[k, pl.ds(EDGE + at + 1, piece)])
            left = 0.5 * (c + cond[k, pl.ds(EDGE + at - 1, piece)])
            e = 0.5 * (c + jnp.where(last, end, turned(c, -1, 1)))
            w = 0.5 * (c + jnp.where(first, end, turned(c, 1, 1)))
            cf = cols[part, 2 * LANES : 3 * LANES]
            diag = cf + up + low + right + left + e + w
            i = jnp.where(cf > 0.0, 1.0 / diag, 0.0)
            wz[k, to] = up
            wx[k, here] = right
            wy[k, to] = e
            wyw[k, to] = w
            inv[k, to] = i
            b0[k, to] = cf * xm[k, here] * i


def source_x_kernel(far, place, far_a, far_b, near_a, near_b, own, xa, xb):
    even = place[0] == 0
    for k, read in enumerate(layer_readers(far, place, far_a, far_b, near_a, near_b, own)):
        low, high = read(0, EDGE), read(LANES - EDGE, EDGE)
        xa[pl.ds(k * EDGE, EDGE), :] = jnp.where(even, high, low)
        xb[pl.ds(k * EDGE, EDGE), :] = jnp.where(even, low, high)


def source_y_kernel(far, place, far_a, far_b, near_a, near_b, own, xa, xb, full, sides, ya, yb):
    count, rows, _ = full.shape
    even = place[0] == 0
    full[0] = jnp.zeros((rows, LANES), F32)
    full[count - 1] = jnp.zeros((rows, LANES), F32)
    for k, read in enumerate(layer_readers(far, place, far_a, far_b, near_a, near_b, own)):
        a, b = xa[pl.ds(k * EDGE, EDGE), :], xb[pl.ds(k * EDGE, EDGE), :]
        full[k + 1, pl.ds(0, EDGE)] = jnp.where(even, b, a)
        full[k + 1, pl.ds(EDGE, LANES)] = read(0, LANES)
        full[k + 1, pl.ds(EDGE + LANES, EDGE)] = jnp.where(even, a, b)
    found = flat_sides(full[...].reshape(count * rows, LANES))
    sides[...] = found
    even = place[1] == 0
    ya[...] = jnp.where(even, found[EDGE:], found[:EDGE])
    yb[...] = jnp.where(even, found[:EDGE], found[EDGE:])


def sweep_kernel(place, xm, wz, wx, wy, wyw, inv, b0, strips, full, sides, ya, yb, ids, out, replies, b, d, xa, xb, ends):
    count, rows, _ = inv.shape
    total = count * rows
    even = place[1] == 0
    after, before = jnp.where(even, ya[...], yb[...]), jnp.where(even, yb[...], ya[...])
    factors = steps()

    sb = strips[7] + strip_of(sides[...], before, after) * strips[6]
    sx, sd = strips[8], None
    kept = [ends_of(sx)]
    for keep, add in factors[:-1]:
        near = strips[0] * turned(sx, rows, 1) + strips[1] * turned(sx, -rows, 1)
        near += strips[2] * turned(sx, 1, 1) + strips[3] * turned(sx, -1, 1)
        near += strips[4] * turned(sx, 1, 0) + strips[5] * turned(sx, -1, 0)
        step = add * (sb - sx + near)
        sd = step if sd is None else step + keep * sd
        sx = sx + sd
        kept.append(ends_of(sx))
    place_in = end_lanes(2 * SWEEPS, SWEEPS)
    big, small = parts(jnp.concatenate(kept, axis=0))
    ends[...] = dot(big, place_in, 0, 0) + dot(small, place_in, 0, 0)

    piece = 24
    first, last = iota((piece, LANES), 1) == 0, iota((piece, LANES), 1) == LANES - 1
    blank = jnp.zeros((EDGE, LANES), F32)

    @pl.loop(0, count)
    def _(k):
        for ref in (xa, xb):
            ref[k, pl.ds(0, EDGE)] = blank
            ref[k, pl.ds(rows + EDGE, EDGE)] = blank

    for s, (keep, add) in enumerate(factors):
        src, into = (xm if s == 0 else (xa if s % 2 else xb)), (xb if s % 2 else xa)

        @pl.loop(1 + s, count - 1 - s)
        def _(k):
            for at in range(0, rows, piece):
                here, to = pl.ds(EDGE + at, piece), pl.ds(at, piece)
                x = src[k, here]
                end = ends[pl.ds(pl.multiple_of(k * rows + at, 8), piece), s * LANES : (s + 1) * LANES]
                e = jnp.where(last, end, turned(x, -1, 1))
                w = jnp.where(first, end, turned(x, 1, 1))
                near = wz[k, to] * src[k + 1, here] + wz[k - 1, to] * src[k - 1, here]
                near += wx[k, here] * src[k, pl.ds(EDGE + at + 1, piece)]
                near += wx[k, pl.ds(EDGE + at - 1, piece)] * src[k, pl.ds(EDGE + at - 1, piece)]
                near += wy[k, to] * e + wyw[k, to] * w
                if s == 0:
                    rhs = b0[k, to] + full[k, to] * inv[k, to]
                    b[k, to] = rhs
                else:
                    rhs = b[k, to]
                step = add * (rhs - x + inv[k, to] * near)
                if s > 0:
                    step = step + keep * d[k, to]
                if s < SWEEPS - 1:
                    d[k, to] = step
                into[k, here] = x + step

    final = xb if SWEEPS % 2 == 0 else xa
    for k in range(4):
        out[pl.ds(k * LANES, LANES), :] = final[SWEEPS + k, pl.ds(2 * EDGE, LANES)]
    n = out.shape[0]
    name = ids[...]
    hot = jnp.concatenate([hot_of(name == iota(name.shape, 1) + at) for at in range(0, n, LANES)], axis=1)
    replies[...] = pick_rows(hot, out[...])


def final_kernel(returned, dest, gain, mob, mobility, ionization):
    total = returned.shape[0]
    name = dest[...]
    hot = jnp.concatenate([hot_of(name == iota(name.shape, 1) + at) for at in range(0, total, LANES)], axis=1)
    back = pick_rows(hot, returned[...])
    mobility[...] = mob[...] * jnp.exp(-0.7 * back)
    ionization[...] = jnp.exp(gain[...] * (1.0 + 0.3 * back))


def swapped(a, b, axis, apart=1):
    count = lax.axis_size(axis)
    found = []
    for v, odd in ((a, 0), (b, 1)):
        pairs = []
        for i in range(count - apart):
            if (i // apart) % 2 == odd:
                pairs += [(i, i + apart), (i + apart, i)]
        found.append(lax.ppermute(v, axis, pairs) if pairs else jnp.zeros_like(v))
    return found


def exchanged(v):
    lines = v.reshape(v.shape[0], 1, v.shape[1])
    return lax.all_to_all(lines, ("gx", "gy"), split_axis=0, concat_axis=0, tiled=True).reshape(v.shape)


def per_device(
    efield, density, mobility_prev, thermal_prev, owner, block, live, material,
    mat_conductivity, mat_softening, mat_capacity,
):
    layers, xcells, width = density.shape
    n = layers * xcells
    peers = lax.axis_size("gx") * lax.axis_size("gy")
    slots = max(2, 2 * n // peers)
    line = peers * (slots + 1)
    flat = lambda a: a.reshape(n, width)
    ef = efield.reshape(3, n, width)
    den, mob, x0 = flat(density), flat(mobility_prev), flat(thermal_prev)
    own, blk, liv = owner.reshape(1, n), block.reshape(1, n), live.reshape(1, n)
    mat = material.reshape(layers, xcells)
    sized = lambda *s: (s, F32)

    [sent] = call(functools.partial(dispatch_kernel, peers, slots), [sized(line, width)],
                  [ef, den, mob, own, blk, liv], "dispatch", flops=10**8)
    received = exchanged(sent)

    spot = [lax.axis_index(a) for a in ("gx", "gy", "gz")]
    place = jnp.stack([spot[0] % 2, spot[1] % 2, spot[2] % 2, spot[2] // 2 % 2])
    far = SWEEPS - layers
    count = layers + 2 * SWEEPS
    rows = xcells + 2 * EDGE
    total = count * rows
    aside = sized(far * xcells + EDGE, width)
    near, far_a, far_b = call(
        functools.partial(start_z_kernel, far), [sized(n + EDGE, width), aside, aside],
        [place, x0, mat], "start_z", smem=(0,))
    far_a, far_b = swapped(far_a, far_b, "gz", 2)
    near_a, near_b = swapped(near, near, "gz")
    xz, mats, xa, xb = call(
        functools.partial(start_x_kernel, far),
        [sized(count, xcells, width), sized(count, width)] + [sized(count * (EDGE + 1), width)] * 2,
        [place, far_a, far_b, near_a, near_b, near], "start_x", smem=(0,))
    xa, xb = swapped(xa, xb, "gx")
    tall = sized(count, rows + 2 * EDGE, width)
    xm, sides, flat_mat, ya, yb = call(
        start_y_kernel,
        [tall, sized(2 * EDGE, total), sized(EDGE, total), sized(2 * EDGE, total), sized(2 * EDGE, total)],
        [place, xz, mats, xa, xb], "start_y", smem=(0,))
    ya, yb = swapped(ya, yb, "gy")
    gain, dest = call(functools.partial(after_kernel, slots), [sized(n, width), ((n, LANES), I32)], [ef, own], "gain")
    received, ya, yb, gain, dest = lax.optimization_barrier((received, ya, yb, gain, dest))
    tile = sized(count, rows, width)
    weights = call(
        weights_kernel, [tile, tall, tile, tile, tile, tile, sized(9, 4 * EDGE, total)],
        [place, mat_conductivity, mat_softening, mat_capacity, xm, sides, flat_mat, ya, yb], "weights",
        scratch=[pltpu.VMEM((count, rows + 2 * EDGE, width), F32), pltpu.VMEM((total, 3 * width), F32),
                 pltpu.VMEM((total, width), F32)],
        limit=32, flops=10**9, smem=(0, 1, 2, 3))

    far -= 1
    source, far_a, far_b = call(
        functools.partial(combine_kernel, peers, slots, far),
        [sized(n, width)] + [sized(far * xcells, width)] * 2, [place, received], "combine", flops=10**8, smem=(0,))
    [ids] = call(functools.partial(ids_kernel, peers, slots), [((peers * slots, LANES), I32)], [received], "ids")
    far_a, far_b = swapped(far_a, far_b, "gz", 2)
    near_a, near_b = swapped(source, source, "gz")
    above = [place, far_a, far_b, near_a, near_b, source]
    xa, xb = call(functools.partial(source_x_kernel, far), [sized((count - 2) * EDGE, width)] * 2, above, "source_x", smem=(0,))
    xa, xb = swapped(xa, xb, "gx")
    full, sides, ya, yb = call(
        functools.partial(source_y_kernel, far),
        [tile, sized(2 * EDGE, total), sized(EDGE, total), sized(EDGE, total)], above + [xa, xb], "source_y", smem=(0,))
    ya, yb = swapped(ya, yb, "gy")
    x, replies = call(
        sweep_kernel, [sized(n, width), sized(peers * slots, width)],
        [place, xm] + list(weights) + [full, sides, ya, yb, ids], "sweeps",
        scratch=[pltpu.VMEM((count, rows, width), F32)] * 2 + [pltpu.VMEM((count, rows + 2 * EDGE, width), F32)] * 2
        + [pltpu.VMEM((total, SWEEPS * width), F32)],
        limit=36, flops=10**8, smem=(0,))
    returned = exchanged(replies)
    mobility, ionization = call(final_kernel, [sized(n, width)] * 2, [returned, dest, gain, mob], "finish", flops=10**8)
    shape = density.shape
    return x.reshape(shape), mobility.reshape(shape), ionization.reshape(shape)


def solution(mesh):
    tile = P("gz", "gx", "gy")
    rows = P("gz", "gx", "gy", None)
    placed = (
        P(None, "gz", "gx", "gy"), tile, tile, tile,
        P("gz", "gx", "gy", None, None), rows, rows, rows, P(), P(), P(),
    )
    return jax.shard_map(
        per_device, mesh=mesh, in_specs=placed, out_specs=(tile, tile, tile), check_vma=False
    )
```

```python
import functools

import jax
import jax.numpy as jnp
from jax import lax
from jax.experimental import pallas as pl
from jax.experimental.pallas import tpu as pltpu
from jax.sharding import PartitionSpec as P

SWEEPS = 6
THETA = 1.01
DELTA = 0.99
LANES = 128
EDGE = 8
F32 = jnp.float32
BF16 = jnp.bfloat16
I32 = jnp.int32


def steps():
    sigma = THETA / DELTA
    rho = 1.0 / sigma
    found = [(0.0, 1.0 / THETA)]
    for _ in range(SWEEPS - 1):
        rho_new = 1.0 / (2.0 * sigma - rho)
        found.append((rho_new * rho, 2.0 * rho_new / DELTA))
        rho = rho_new
    return found


def iota(shape, dim):
    return lax.broadcasted_iota(I32, shape, dim)


def dot(a, b, ca, cb):
    return lax.dot_general(a, b, (((ca,), (cb,)), ((), ())), preferred_element_type=F32)


def parts(v):
    high = v.astype(BF16)
    return high, (v - high.astype(F32)).astype(BF16)


def pick_rows(hot, rows):
    high, low = parts(rows)
    got = dot(hot, jnp.concatenate([high, low], axis=1), 1, 0)
    width = rows.shape[1]
    return got[:, :width] + got[:, width:]


def column(row):
    same = iota((LANES, LANES), 0) == iota((LANES, LANES), 1)
    found = []
    for at in range(0, row.shape[1], LANES):
        piece = jnp.broadcast_to(row[:, at : at + LANES], (LANES, LANES))
        found.append(jnp.sum(jnp.where(same, piece, 0), axis=1, keepdims=True))
    return jnp.concatenate(found, axis=0)


def hot_of(cond):
    return jnp.where(cond, F32(1.0), F32(0.0)).astype(BF16)


def edge_lanes():
    r, y = iota((2 * EDGE, LANES), 0), iota((2 * EDGE, LANES), 1)
    return hot_of(y == jnp.where(r < EDGE, r, r + LANES - 2 * EDGE))


def call(kernel, outs, ins, name, scratch=(), limit=32, flops=0, smem=(), hbm=False):
    bytes_of = lambda a: a.size * a.dtype.itemsize
    return pl.pallas_call(
        kernel,
        out_shape=[jax.ShapeDtypeStruct(s, t) for s, t in outs],
        in_specs=[
            pl.BlockSpec(memory_space=pltpu.SMEM if i in smem else pltpu.HBM if hbm else pltpu.VMEM)
            for i in range(len(ins))
        ],
        out_specs=[pl.BlockSpec(memory_space=pltpu.VMEM) for _ in outs],
        scratch_shapes=list(scratch),
        compiler_params=pltpu.CompilerParams(vmem_limit_bytes=limit << 20),
        cost_estimate=pl.CostEstimate(
            flops=flops,
            bytes_accessed=sum(bytes_of(a) for a in ins)
            + sum(jax.ShapeDtypeStruct(s, t).size * 4 for s, t in outs),
            transcendentals=0,
        ),
        name=name,
    )(*ins)


def dispatch_kernel(peers, slots, *refs):
    far, out, near, sems = refs[:6], refs[6], refs[7:13], refs[13]
    copies = [pltpu.make_async_copy(a, b, sems.at[i]) for i, (a, b) in enumerate(zip(far, near))]
    for copy in copies:
        copy.start()
    for copy in copies:
        copy.wait()
    ef, den, mob, owner, block, live = near
    n = owner.shape[1]
    esq = ef[0] * ef[0] + ef[1] * ef[1] + ef[2] * ef[2]
    heat = 0.2 * den[...] * mob[...] * esq
    heat = jnp.where(iota(heat.shape, 1) < column(live[...]), heat, F32(0.0))
    own = owner[...]
    own_col = column(own)
    pos = jnp.zeros((1, n), I32)
    for at in range(0, n, LANES):
        r = iota((LANES, n), 0) + at
        earlier = (own_col[at : at + LANES] == own) & (r < iota((LANES, n), 1))
        pos = pos + jnp.sum(jnp.where(earlier, 1, 0), axis=0, keepdims=True)
    dest = own * (slots + 1) + pos
    hot = hot_of(iota((peers * (slots + 1), n), 0) == dest)
    out[...] = pick_rows(hot, heat)
    named = hot_of(iota((peers, n), 0) == own)
    at_slot = iota((LANES, n), 0) == pos
    code = block[...] + 1
    high = jnp.where(at_slot, code // 32, 0).astype(F32).astype(BF16)
    low = jnp.where(at_slot, code % 32, 0).astype(F32).astype(BF16)
    out[pl.ds(slots, peers, stride=slots + 1), :] = dot(named, high, 1, 1) * 32.0 + dot(named, low, 1, 1)


def after_kernel(slots, ef, owner, gain, dest):
    n = owner.shape[1]
    esq = ef[0] * ef[0] + ef[1] * ef[1] + ef[2] * ef[2]
    gain[...] = -2.0 * lax.rsqrt(esq + 1.0)
    own = owner[...]
    own_col = column(own)
    for at in range(0, n, LANES):
        r = iota((LANES, n), 0) + at
        piece = own_col[at : at + LANES]
        earlier = (piece == own) & (iota((LANES, n), 1) < r)
        pos = jnp.sum(jnp.where(earlier, 1, 0), axis=1, keepdims=True)
        dest[pl.ds(at, LANES), :] = jnp.broadcast_to(piece * slots + pos, (LANES, LANES))


def labels_of(received, peers, slots):
    got = received[pl.ds(slots, peers, stride=slots + 1), :]
    high = jnp.floor(got * (1.0 / 32.0))
    return high.astype(BF16), (got - 32.0 * high).astype(BF16)


def combine_kernel(peers, slots, far, place, received, source, far_a, far_b):
    n = source.shape[0]
    total = received.shape[0]
    high, low = labels_of(received, peers, slots)
    j = iota((LANES, total), 1)
    spread = hot_of(iota((LANES, total), 0) == j - (slots + 1) * lax.div(j, slots + 1))
    named = dot(high, spread, 1, 0) * 32.0 + dot(low, spread, 1, 0)
    mine = iota((peers, total), 0) == lax.div(iota((peers, total), 1), slots + 1)
    ids = jnp.sum(jnp.where(mine, named, 0.0), axis=0, keepdims=True).astype(I32)
    picks = hot_of(iota((n, total), 0) + 1 == ids)
    source[...] = pick_rows(picks, received[...])
    rows = far * (n // 4)
    first, last = source[pl.ds(0, rows), :], source[pl.ds(n - rows, rows), :]
    even = place[3] == 0
    far_a[...] = jnp.where(even, last, first)
    far_b[...] = jnp.where(even, first, last)


def ids_kernel(peers, slots, received, ids):
    total = peers * slots
    high, low = labels_of(received, peers, slots)
    own = hot_of(lax.div(iota((total, peers), 0), slots) == iota((total, peers), 1))
    named = dot(own, high, 1, 0) * 32.0 + dot(own, low, 1, 0)
    i = iota((total, LANES), 0)
    mine = iota((total, LANES), 1) == i - slots * lax.div(i, slots)
    found = jnp.sum(jnp.where(mine, named, 0.0), axis=1, keepdims=True) - 1.0
    ids[...] = jnp.broadcast_to(found, (total, LANES)).astype(I32)


def start_z_kernel(far, place, x0, material, near, far_a, far_b):
    layers, xcells = material.shape
    n = layers * xcells
    mat = (material[...] + 1).astype(F32)
    rows = far * xcells
    zeros = lambda k: jnp.zeros((k, LANES), F32)
    near[pl.ds(0, n), :] = x0[...]
    near[pl.ds(n, EDGE), :] = jnp.concatenate([mat, zeros(EDGE - layers)], axis=0)
    up, down = x0[pl.ds(n - rows, rows), :], x0[pl.ds(0, rows), :]
    mat_up = jnp.concatenate([mat[layers - far :], zeros(EDGE - far)], axis=0)
    mat_down = jnp.concatenate([mat[:far], zeros(EDGE - far)], axis=0)
    even = place[3] == 0
    far_a[pl.ds(0, rows), :] = jnp.where(even, up, down)
    far_b[pl.ds(0, rows), :] = jnp.where(even, down, up)
    far_a[pl.ds(rows, EDGE), :] = jnp.where(even, mat_up, mat_down)
    far_b[pl.ds(rows, EDGE), :] = jnp.where(even, mat_down, mat_up)


def layer_readers(far, place, far_a, far_b, near_a, near_b, own):
    even, even2 = place[2] == 0, place[3] == 0

    def one(k, ref):
        return lambda at, size: ref[pl.ds(k * LANES + at, size), :]

    def either(k, cond, yes, no):
        return lambda at, size: jnp.where(cond, one(k, yes)(at, size), one(k, no)(at, size))

    found = [either(k, even2, far_b, far_a) for k in range(far)]
    found += [either(k, even, near_b, near_a) for k in range(4)]
    found += [one(k, own) for k in range(4)]
    found += [either(k, even, near_a, near_b) for k in range(4)]
    return found + [either(k, even2, far_a, far_b) for k in range(far)]


def start_x_kernel(far, place, far_a, far_b, near_a, near_b, own, xz, mats, xa, xb):
    readers = layer_readers(far, place, far_a, far_b, near_a, near_b, own)
    count = len(readers)
    even = place[0] == 0
    for k, read in enumerate(readers):
        piece = read(0, LANES)
        xz[k] = piece
        low, high = piece[:EDGE], piece[LANES - EDGE :]
        xa[pl.ds(k * EDGE, EDGE), :] = jnp.where(even, high, low)
        xb[pl.ds(k * EDGE, EDGE), :] = jnp.where(even, low, high)
    tail = [far * LANES] * far + [4 * LANES] * 12 + [far * LANES] * far
    at = list(range(far)) + list(range(4)) * 3 + list(range(far))
    for k, read in enumerate(readers):
        mats[pl.ds(k, 1), :] = read(tail[k] + at[k] - at[k] * LANES, 1)
    xa[pl.ds(count * EDGE, count), :] = mats[...]
    xb[pl.ds(count * EDGE, count), :] = mats[...]


def flat_sides(rows):
    high, low = parts(rows)
    edges = edge_lanes()
    return dot(edges, high, 1, 1) + dot(edges, low, 1, 1)


def start_y_kernel(place, xz, mats, xa, xb, xm, sides, flat_mat, ya, yb):
    count = xz.shape[0]
    even = place[0] == 0
    after, before = jnp.where(even, xa[...], xb[...]), jnp.where(even, xb[...], xa[...])
    blank = jnp.zeros((EDGE, LANES), F32)
    for k in range(count):
        part = slice(k * EDGE, (k + 1) * EDGE)
        xm[k, pl.ds(0, EDGE)] = blank
        xm[k, pl.ds(EDGE, EDGE)] = before[part]
        xm[k, pl.ds(2 * EDGE, LANES)] = xz[k]
        xm[k, pl.ds(LANES + 2 * EDGE, EDGE)] = after[part]
        xm[k, pl.ds(LANES + 3 * EDGE, EDGE)] = blank
    rows = LANES + 2 * EDGE
    total = count * rows
    found = flat_sides(xm[:, EDGE : EDGE + rows].reshape(total, LANES))
    sides[...] = found
    around = jnp.concatenate([before[count * EDGE :], mats[...], after[count * EDGE :]], axis=0)
    q = iota((1, total), 1)
    layer = lax.div(q, rows)
    row = q - layer * rows
    tile = jnp.where(row < EDGE, 0, jnp.where(row < LANES + EDGE, 1, 2))
    lane = row - EDGE + LANES * (1 - tile)
    spread = hot_of(iota((LANES, total), 0) == lane)
    named = dot(around.astype(BF16), spread, 1, 0)
    mine = iota((3 * count, total), 0) == tile * count + layer
    mat = jnp.sum(jnp.where(mine, named, 0.0), axis=0, keepdims=True)
    mat = jnp.where(iota((EDGE, total), 0) == 0, mat, 0.0)
    flat_mat[...] = mat
    even = place[1] == 0
    ya[pl.ds(0, EDGE), :] = jnp.where(even, found[EDGE:], found[:EDGE])
    yb[pl.ds(0, EDGE), :] = jnp.where(even, found[:EDGE], found[EDGE:])
    ya[pl.ds(EDGE, EDGE), :] = mat
    yb[pl.ds(EDGE, EDGE), :] = mat


def three_parts(v):
    high = v.astype(BF16)
    rest = v - high.astype(F32)
    mid = rest.astype(BF16)
    return high, mid, (rest - mid.astype(F32)).astype(BF16)


def ends_of(strip):
    return jnp.concatenate([strip[EDGE - 1 : EDGE], strip[3 * EDGE : 3 * EDGE + 1]], axis=0)


def end_lanes(depth, times):
    r, y = iota((depth, times * LANES), 0), iota((depth, times * LANES), 1)
    first = (r % 2 == 0) & (y == (r // 2) * LANES)
    last = (r % 2 == 1) & (y == (r // 2) * LANES + LANES - 1)
    return hot_of(first | last)


def turned(v, by, axis):
    return pltpu.roll(v, by % v.shape[axis], axis)


def strip_of(sides, before, after):
    return jnp.concatenate([before, sides, after], axis=0)


def weights_kernel(place, base, soft, heat, xm, sides, flat_mat, ya, yb, wz, wx, wy, wyw, inv, b0, strips, cond, cols, ends):
    count, rows = inv.shape[0], inv.shape[1]
    total = count * rows
    even = place[1] == 0
    after, before = jnp.where(even, ya[...], yb[...]), jnp.where(even, yb[...], ya[...])
    mat = jnp.concatenate([flat_mat[0:1], before[EDGE : EDGE + 1], after[EDGE : EDGE + 1]], axis=0)
    tables = []
    for values in (base, soft, heat):
        found = jnp.zeros(mat.shape, F32)
        for m in range(values.shape[0]):
            found = jnp.where(mat == F32(m + 1), values[m], found)
        tables.append(found)
    own = [p for t in tables for p in three_parts(t[0:1])]
    r, y = iota((9, 3 * LANES), 0), iota((9, 3 * LANES), 1)
    cols[...] = dot(jnp.concatenate(own, axis=0), hot_of(lax.div(r, 3) == lax.div(y, LANES)), 0, 0)
    wide = lambda t, i: jnp.broadcast_to(t[i : i + 1], (EDGE, total))
    kb, ks, cf = (jnp.concatenate([wide(t, 1), wide(t, 0), wide(t, 0), wide(t, 2)], axis=0) for t in tables)
    sx = strip_of(sides[...], before[:EDGE], after[:EDGE])
    sc = kb / (1.0 + ks * sx)
    down = lambda by, axis: 0.5 * (sc + turned(sc, by, axis))
    around = [down(rows, 1), down(-rows, 1), down(1, 1), down(-1, 1), down(1, 0), down(-1, 0)]
    diag = cf
    for w in around:
        diag = diag + w
    si = jnp.where(cf > 0.0, 1.0 / diag, 0.0)
    for i, w in enumerate(around):
        strips[i] = w * si
    strips[6] = si
    strips[7] = cf * sx * si
    strips[8] = sx
    got = [dot(p, end_lanes(2, 1), 0, 0) for p in three_parts(ends_of(sc))]
    ends[...] = got[0] + got[1] + got[2]

    piece = 16
    blank = jnp.zeros((EDGE, LANES), F32)

    @pl.loop(0, count)
    def _(k):
        cond[k, pl.ds(0, EDGE)] = blank
        cond[k, pl.ds(rows + EDGE, EDGE)] = blank
        wx[k, pl.ds(0, EDGE)] = blank
        wx[k, pl.ds(rows + EDGE, EDGE)] = blank
        for at in range(0, rows, piece):
            part = pl.ds(pl.multiple_of(k * rows + at, 8), piece)
            x = xm[k, pl.ds(EDGE + at, piece)]
            cond[k, pl.ds(EDGE + at, piece)] = cols[part, 0:LANES] / (1.0 + cols[part, LANES : 2 * LANES] * x)

    first, last = iota((piece, LANES), 1) == 0, iota((piece, LANES), 1) == LANES - 1
    wz[0] = 0.5 * (cond[0, pl.ds(EDGE, rows)] + cond[1, pl.ds(EDGE, rows)])

    @pl.loop(1, count - 1)
    def _(k):
        for at in range(0, rows, piece):
            here = pl.ds(EDGE + at, piece)
            part = pl.ds(pl.multiple_of(k * rows + at, 8), piece)
            to = pl.ds(at, piece)
            c, end = cond[k, here], ends[part, :]
            up = 0.5 * (c + cond[k + 1, here])
            low = 0.5 * (c + cond[k - 1, here])
            right = 0.5 * (c + cond[k, pl.ds(EDGE + at + 1, piece)])
            left = 0.5 * (c + cond[k, pl.ds(EDGE + at - 1, piece)])
            e = 0.5 * (c + jnp.where(last, end, turned(c, -1, 1)))
            w = 0.5 * (c + jnp.where(first, end, turned(c, 1, 1)))
            cf = cols[part, 2 * LANES : 3 * LANES]
            diag = cf + up + low + right + left + e + w
            i = jnp.where(cf > 0.0, 1.0 / diag, 0.0)
            wz[k, to] = up
            wx[k, here] = right
            wy[k, to] = e
            wyw[k, to] = w
            inv[k, to] = i
            b0[k, to] = cf * xm[k, here] * i


def source_x_kernel(far, place, far_a, far_b, near_a, near_b, own, xa, xb):
    even = place[0] == 0
    for k, read in enumerate(layer_readers(far, place, far_a, far_b, near_a, near_b, own)):
        low, high = read(0, EDGE), read(LANES - EDGE, EDGE)
        xa[pl.ds(k * EDGE, EDGE), :] = jnp.where(even, high, low)
        xb[pl.ds(k * EDGE, EDGE), :] = jnp.where(even, low, high)


def source_y_kernel(far, place, far_a, far_b, near_a, near_b, own, xa, xb, full, sides, ya, yb):
    count, rows, _ = full.shape
    even = place[0] == 0
    full[0] = jnp.zeros((rows, LANES), F32)
    full[count - 1] = jnp.zeros((rows, LANES), F32)
    for k, read in enumerate(layer_readers(far, place, far_a, far_b, near_a, near_b, own)):
        a, b = xa[pl.ds(k * EDGE, EDGE), :], xb[pl.ds(k * EDGE, EDGE), :]
        full[k + 1, pl.ds(0, EDGE)] = jnp.where(even, b, a)
        full[k + 1, pl.ds(EDGE, LANES)] = read(0, LANES)
        full[k + 1, pl.ds(EDGE + LANES, EDGE)] = jnp.where(even, a, b)
    found = flat_sides(full[...].reshape(count * rows, LANES))
    sides[...] = found
    even = place[1] == 0
    ya[...] = jnp.where(even, found[EDGE:], found[:EDGE])
    yb[...] = jnp.where(even, found[:EDGE], found[EDGE:])


def sweep_kernel(place, xm, wz, wx, wy, wyw, inv, b0, strips, full, sides, ya, yb, ids, out, replies, b, d, xa, xb, ends):
    count, rows, _ = inv.shape
    total = count * rows
    even = place[1] == 0
    after, before = jnp.where(even, ya[...], yb[...]), jnp.where(even, yb[...], ya[...])
    factors = steps()

    sb = strips[7] + strip_of(sides[...], before, after) * strips[6]
    sx, sd = strips[8], None
    kept = [ends_of(sx)]
    for keep, add in factors[:-1]:
        near = strips[0] * turned(sx, rows, 1) + strips[1] * turned(sx, -rows, 1)
        near += strips[2] * turned(sx, 1, 1) + strips[3] * turned(sx, -1, 1)
        near += strips[4] * turned(sx, 1, 0) + strips[5] * turned(sx, -1, 0)
        step = add * (sb - sx + near)
        sd = step if sd is None else step + keep * sd
        sx = sx + sd
        kept.append(ends_of(sx))
    place_in = end_lanes(2 * SWEEPS, SWEEPS)
    kept = jnp.concatenate(parts(jnp.concatenate(kept, axis=0)), axis=0)
    ends[...] = dot(kept, jnp.concatenate([place_in, place_in], axis=0), 0, 0)

    piece = 24
    first, last = iota((piece, LANES), 1) == 0, iota((piece, LANES), 1) == LANES - 1
    blank = jnp.zeros((EDGE, LANES), F32)

    @pl.loop(0, count)
    def _(k):
        for ref in (xa, xb):
            ref[k, pl.ds(0, EDGE)] = blank
            ref[k, pl.ds(rows + EDGE, EDGE)] = blank

    for s, (keep, add) in enumerate(factors):
        src, into = (xm if s == 0 else (xa if s % 2 else xb)), (xb if s % 2 else xa)

        @pl.loop(1 + s, count - 1 - s)
        def _(k):
            for at in range(0, rows, piece):
                here, to = pl.ds(EDGE + at, piece), pl.ds(at, piece)
                x = src[k, here]
                end = ends[pl.ds(pl.multiple_of(k * rows + at, 8), piece), s * LANES : (s + 1) * LANES]
                e = jnp.where(last, end, turned(x, -1, 1))
                w = jnp.where(first, end, turned(x, 1, 1))
                near = wz[k, to] * src[k + 1, here] + wz[k - 1, to] * src[k - 1, here]
                near += wx[k, here] * src[k, pl.ds(EDGE + at + 1, piece)]
                near += wx[k, pl.ds(EDGE + at - 1, piece)] * src[k, pl.ds(EDGE + at - 1, piece)]
                near += wy[k, to] * e + wyw[k, to] * w
                if s == 0:
                    rhs = b0[k, to] + full[k, to] * inv[k, to]
                    b[k, to] = rhs
                else:
                    rhs = b[k, to]
                step = add * (rhs - x + inv[k, to] * near)
                if s > 0:
                    step = step + keep * d[k, to]
                if s < SWEEPS - 1:
                    d[k, to] = step
                into[k, here] = x + step

    final = xb if SWEEPS % 2 == 0 else xa
    for k in range(4):
        out[pl.ds(k * LANES, LANES), :] = final[SWEEPS + k, pl.ds(2 * EDGE, LANES)]
    n = out.shape[0]
    name = ids[...]
    hot = jnp.concatenate([hot_of(name == iota(name.shape, 1) + at) for at in range(0, n, LANES)], axis=1)
    replies[...] = pick_rows(hot, out[...])


def final_kernel(returned, dest, gain, mob, mobility, ionization):
    total = returned.shape[0]
    name = dest[...]
    hot = jnp.concatenate([hot_of(name == iota(name.shape, 1) + at) for at in range(0, total, LANES)], axis=1)
    back = pick_rows(hot, returned[...])
    mobility[...] = mob[...] * jnp.exp(-0.7 * back)
    ionization[...] = jnp.exp(gain[...] * (1.0 + 0.3 * back))


def swapped(a, b, axis, apart=1):
    count = lax.axis_size(axis)
    found = []
    for v, odd in ((a, 0), (b, 1)):
        pairs = []
        for i in range(count - apart):
            if (i // apart) % 2 == odd:
                pairs += [(i, i + apart), (i + apart, i)]
        found.append(lax.ppermute(v, axis, pairs) if pairs else jnp.zeros_like(v))
    return found


def exchanged(v):
    lines = v.reshape(v.shape[0], 1, v.shape[1])
    return lax.all_to_all(lines, ("gx", "gy"), split_axis=0, concat_axis=0, tiled=True).reshape(v.shape)


def per_device(
    efield, density, mobility_prev, thermal_prev, owner, block, live, material,
    mat_conductivity, mat_softening, mat_capacity,
):
    layers, xcells, width = density.shape
    n = layers * xcells
    peers = lax.axis_size("gx") * lax.axis_size("gy")
    slots = max(2, 2 * n // peers)
    line = peers * (slots + 1)
    flat = lambda a: a.reshape(n, width)
    ef = efield.reshape(3, n, width)
    den, mob, x0 = flat(density), flat(mobility_prev), flat(thermal_prev)
    own, blk, liv = owner.reshape(1, n), block.reshape(1, n), live.reshape(1, n)
    mat = material.reshape(layers, xcells)
    sized = lambda *s: (s, F32)

    given = [ef, den, mob, own, blk, liv]
    [sent] = call(
        functools.partial(dispatch_kernel, peers, slots), [sized(line, width)], given, "dispatch", flops=10**8, hbm=True, limit=60,
        scratch=[pltpu.VMEM(a.shape, a.dtype) for a in given] + [pltpu.SemaphoreType.DMA((len(given),))])
    received = exchanged(sent)

    spot = [lax.axis_index(a) for a in ("gx", "gy", "gz")]
    place = jnp.stack([spot[0] % 2, spot[1] % 2, spot[2] % 2, spot[2] // 2 % 2])
    far = SWEEPS - layers
    count = layers + 2 * SWEEPS
    rows = xcells + 2 * EDGE
    total = count * rows
    aside = sized(far * xcells + EDGE, width)
    near, far_a, far_b = call(
        functools.partial(start_z_kernel, far), [sized(n + EDGE, width), aside, aside],
        [place, x0, mat], "start_z", smem=(0,))
    far_a, far_b = swapped(far_a, far_b, "gz", 2)
    near, far_a, far_b = lax.optimization_barrier((near, far_a, far_b))
    near_a, near_b = swapped(near, near, "gz")
    xz, mats, xa, xb = call(
        functools.partial(start_x_kernel, far),
        [sized(count, xcells, width), sized(count, width)] + [sized(count * (EDGE + 1), width)] * 2,
        [place, far_a, far_b, near_a, near_b, near], "start_x", smem=(0,))
    xa, xb = swapped(xa, xb, "gx")
    received, xa, xb = lax.optimization_barrier((received, xa, xb))
    tall = sized(count, rows + 2 * EDGE, width)
    xm, sides, flat_mat, ya, yb = call(
        start_y_kernel,
        [tall, sized(2 * EDGE, total), sized(EDGE, total), sized(2 * EDGE, total), sized(2 * EDGE, total)],
        [place, xz, mats, xa, xb], "start_y", smem=(0,))
    ya, yb = swapped(ya, yb, "gy")
    gain, dest = call(functools.partial(after_kernel, slots), [sized(n, width), ((n, LANES), I32)], [ef, own], "gain")
    far -= 1
    source, far_a, far_b = call(
        functools.partial(combine_kernel, peers, slots, far),
        [sized(n, width)] + [sized(far * xcells, width)] * 2, [place, received], "combine", flops=10**8, smem=(0,))
    [ids] = call(functools.partial(ids_kernel, peers, slots), [((peers * slots, LANES), I32)], [received], "ids")
    far_a, far_b = swapped(far_a, far_b, "gz", 2)
    source, far_a, far_b = lax.optimization_barrier((source, far_a, far_b))
    near_a, near_b = swapped(source, source, "gz")
    near_a, near_b, ya, yb = lax.optimization_barrier((near_a, near_b, ya, yb))
    tile = sized(count, rows, width)
    weights = call(
        weights_kernel, [tile, tall, tile, tile, tile, tile, sized(9, 4 * EDGE, total)],
        [place, mat_conductivity, mat_softening, mat_capacity, xm, sides, flat_mat, ya, yb], "weights",
        scratch=[pltpu.VMEM((count, rows + 2 * EDGE, width), F32), pltpu.VMEM((total, 3 * width), F32),
                 pltpu.VMEM((total, width), F32)],
        limit=32, flops=10**9, smem=(0, 1, 2, 3))
    above = [place, far_a, far_b, near_a, near_b, source]
    xa, xb = call(functools.partial(source_x_kernel, far), [sized((count - 2) * EDGE, width)] * 2, above, "source_x", smem=(0,))
    xa, xb = swapped(xa, xb, "gx")
    xa, xb, weights, ids, gain, dest = lax.optimization_barrier((xa, xb, weights, ids, gain, dest))
    full, sides, ya, yb = call(
        functools.partial(source_y_kernel, far),
        [tile, sized(2 * EDGE, total), sized(EDGE, total), sized(EDGE, total)], above + [xa, xb], "source_y", smem=(0,))
    ya, yb = swapped(ya, yb, "gy")
    x, replies = call(
        sweep_kernel, [sized(n, width), sized(peers * slots, width)],
        [place, xm] + list(weights) + [full, sides, ya, yb, ids], "sweeps",
        scratch=[pltpu.VMEM((count, rows, width), F32)] * 2 + [pltpu.VMEM((count, rows + 2 * EDGE, width), F32)] * 2
        + [pltpu.VMEM((total, SWEEPS * width), F32)],
        limit=36, flops=10**8, smem=(0,))
    returned = exchanged(replies)
    mobility, ionization = call(final_kernel, [sized(n, width)] * 2, [returned, dest, gain, mob], "finish", flops=10**8)
    shape = density.shape
    return x.reshape(shape), mobility.reshape(shape), ionization.reshape(shape)


def solution(mesh):
    tile = P("gz", "gx", "gy")
    rows = P("gz", "gx", "gy", None)
    placed = (
        P(None, "gz", "gx", "gy"), tile, tile, tile,
        P("gz", "gx", "gy", None, None), rows, rows, rows, P(), P(), P(),
    )
    return jax.shard_map(
        per_device, mesh=mesh, in_specs=placed, out_specs=(tile, tile, tile), check_vma=False
    )
```

```python
import functools

import jax
import jax.numpy as jnp
from jax import lax
from jax.experimental import pallas as pl
from jax.experimental.pallas import tpu as pltpu
from jax.sharding import PartitionSpec as P

SWEEPS = 6
THETA = 1.01
DELTA = 0.99
LANES = 128
EDGE = 8
F32 = jnp.float32
BF16 = jnp.bfloat16
I32 = jnp.int32


def steps():
    sigma = THETA / DELTA
    rho = 1.0 / sigma
    found = [(0.0, 1.0 / THETA)]
    for _ in range(SWEEPS - 1):
        rho_new = 1.0 / (2.0 * sigma - rho)
        found.append((rho_new * rho, 2.0 * rho_new / DELTA))
        rho = rho_new
    return found


def iota(shape, dim):
    return lax.broadcasted_iota(I32, shape, dim)


def dot(a, b, ca, cb):
    return lax.dot_general(a, b, (((ca,), (cb,)), ((), ())), preferred_element_type=F32)


def parts(v):
    high = v.astype(BF16)
    return high, (v - high.astype(F32)).astype(BF16)


def pick_rows(hot, rows):
    high, low = parts(rows)
    got = dot(hot, jnp.concatenate([high, low], axis=1), 1, 0)
    width = rows.shape[1]
    return got[:, :width] + got[:, width:]


def column(row):
    same = iota((LANES, LANES), 0) == iota((LANES, LANES), 1)
    found = []
    for at in range(0, row.shape[1], LANES):
        piece = jnp.broadcast_to(row[:, at : at + LANES], (LANES, LANES))
        found.append(jnp.sum(jnp.where(same, piece, 0), axis=1, keepdims=True))
    return jnp.concatenate(found, axis=0)


def hot_of(cond):
    return jnp.where(cond, F32(1.0), F32(0.0)).astype(BF16)


def edge_lanes():
    r, y = iota((2 * EDGE, LANES), 0), iota((2 * EDGE, LANES), 1)
    return hot_of(y == jnp.where(r < EDGE, r, r + LANES - 2 * EDGE))


def call(kernel, outs, ins, name, scratch=(), limit=32, flops=0, smem=(), hbm=False):
    bytes_of = lambda a: a.size * a.dtype.itemsize
    return pl.pallas_call(
        kernel,
        out_shape=[jax.ShapeDtypeStruct(s, t) for s, t in outs],
        in_specs=[
            pl.BlockSpec(memory_space=pltpu.SMEM if i in smem else pltpu.HBM if hbm else pltpu.VMEM)
            for i in range(len(ins))
        ],
        out_specs=[pl.BlockSpec(memory_space=pltpu.VMEM) for _ in outs],
        scratch_shapes=list(scratch),
        compiler_params=pltpu.CompilerParams(vmem_limit_bytes=limit << 20),
        cost_estimate=pl.CostEstimate(
            flops=flops,
            bytes_accessed=sum(bytes_of(a) for a in ins)
            + sum(jax.ShapeDtypeStruct(s, t).size * 4 for s, t in outs),
            transcendentals=0,
        ),
        name=name,
    )(*ins)


def dispatch_kernel(peers, slots, *refs):
    far, out, near, sems = refs[:6], refs[6], refs[7:13], refs[13]
    copies = [pltpu.make_async_copy(a, b, sems.at[i]) for i, (a, b) in enumerate(zip(far, near))]
    for copy in copies:
        copy.start()
    for copy in copies:
        copy.wait()
    ef, den, mob, owner, block, live = near
    n = owner.shape[1]
    esq = ef[0] * ef[0] + ef[1] * ef[1] + ef[2] * ef[2]
    heat = 0.2 * den[...] * mob[...] * esq
    heat = jnp.where(iota(heat.shape, 1) < column(live[...]), heat, F32(0.0))
    own = owner[...]
    own_col = column(own)
    pos = jnp.zeros((1, n), I32)
    for at in range(0, n, LANES):
        r = iota((LANES, n), 0) + at
        earlier = (own_col[at : at + LANES] == own) & (r < iota((LANES, n), 1))
        pos = pos + jnp.sum(jnp.where(earlier, 1, 0), axis=0, keepdims=True)
    dest = own * (slots + 1) + pos
    hot = hot_of(iota((peers * (slots + 1), n), 0) == dest)
    out[...] = pick_rows(hot, heat)
    named = hot_of(iota((peers, n), 0) == own)
    at_slot = iota((LANES, n), 0) == pos
    code = block[...] + 1
    high = jnp.where(at_slot, code // 32, 0).astype(F32).astype(BF16)
    low = jnp.where(at_slot, code % 32, 0).astype(F32).astype(BF16)
    out[pl.ds(slots, peers, stride=slots + 1), :] = dot(named, high, 1, 1) * 32.0 + dot(named, low, 1, 1)


def after_kernel(slots, ef, owner, gain, dest):
    n = owner.shape[1]
    esq = ef[0] * ef[0] + ef[1] * ef[1] + ef[2] * ef[2]
    gain[...] = -2.0 * lax.rsqrt(esq + 1.0)
    own = owner[...]
    own_col = column(own)
    for at in range(0, n, LANES):
        r = iota((LANES, n), 0) + at
        piece = own_col[at : at + LANES]
        earlier = (piece == own) & (iota((LANES, n), 1) < r)
        pos = jnp.sum(jnp.where(earlier, 1, 0), axis=1, keepdims=True)
        dest[pl.ds(at, LANES), :] = jnp.broadcast_to(piece * slots + pos, (LANES, LANES))


def labels_of(received, peers, slots):
    got = received[pl.ds(slots, peers, stride=slots + 1), :]
    high = jnp.floor(got * (1.0 / 32.0))
    return high.astype(BF16), (got - 32.0 * high).astype(BF16)


def combine_kernel(peers, slots, received, source, first, last):
    n = source.shape[0]
    total = received.shape[0]
    high, low = labels_of(received, peers, slots)
    j = iota((LANES, total), 1)
    spread = hot_of(iota((LANES, total), 0) == j - (slots + 1) * lax.div(j, slots + 1))
    named = dot(high, spread, 1, 0) * 32.0 + dot(low, spread, 1, 0)
    mine = iota((peers, total), 0) == lax.div(iota((peers, total), 1), slots + 1)
    ids = jnp.sum(jnp.where(mine, named, 0.0), axis=0, keepdims=True).astype(I32)
    picks = hot_of(iota((n, total), 0) + 1 == ids)
    source[...] = pick_rows(picks, received[...])
    first[...] = source[pl.ds(0, LANES), :]
    last[...] = source[pl.ds(n - LANES, LANES), :]


def ids_kernel(peers, slots, received, ids):
    total = peers * slots
    high, low = labels_of(received, peers, slots)
    own = hot_of(lax.div(iota((total, peers), 0), slots) == iota((total, peers), 1))
    named = dot(own, high, 1, 0) * 32.0 + dot(own, low, 1, 0)
    i = iota((total, LANES), 0)
    mine = iota((total, LANES), 1) == i - slots * lax.div(i, slots)
    found = jnp.sum(jnp.where(mine, named, 0.0), axis=1, keepdims=True) - 1.0
    ids[...] = jnp.broadcast_to(found, (total, LANES)).astype(I32)


def start_z_kernel(far, x0, material, near, up, down):
    layers, xcells = material.shape
    n = layers * xcells
    mat = (material[...] + 1).astype(F32)
    rows = far * xcells
    zeros = lambda k: jnp.zeros((k, LANES), F32)
    near[pl.ds(0, n), :] = x0[...]
    near[pl.ds(n, EDGE), :] = jnp.concatenate([mat, zeros(EDGE - layers)], axis=0)
    up[pl.ds(0, rows), :] = x0[pl.ds(n - rows, rows), :]
    up[pl.ds(rows, EDGE), :] = jnp.concatenate([mat[layers - far :], zeros(EDGE - far)], axis=0)
    down[pl.ds(0, rows), :] = x0[pl.ds(0, rows), :]
    down[pl.ds(rows, EDGE), :] = jnp.concatenate([mat[:far], zeros(EDGE - far)], axis=0)


def start_x_kernel(far, low2, low, own, high, high2, xz, mats, xlow, xhigh):
    found = [(low2, k) for k in range(far)]
    for ref in (low, own, high):
        found += [(ref, k) for k in range(4)]
    found += [(high2, k) for k in range(far)]
    count = len(found)
    for k, (ref, at) in enumerate(found):
        piece = ref[pl.ds(at * LANES, LANES), :]
        xz[k] = piece
        xlow[pl.ds(k * EDGE, EDGE), :] = piece[:EDGE]
        xhigh[pl.ds(k * EDGE, EDGE), :] = piece[LANES - EDGE :]
        mats[pl.ds(k, 1), :] = ref[pl.ds(ref.shape[0] - EDGE + at, 1), :]
    xlow[pl.ds(count * EDGE, count), :] = mats[...]
    xhigh[pl.ds(count * EDGE, count), :] = mats[...]


def near_layers(low, own, high):
    return [(ref, k) for ref in (low, own, high) for k in range(4)]


def pack_x_kernel(low, own, high, start_low, start_high, xlow, xhigh):
    top = start_low.shape[0]
    xlow[pl.ds(0, top), :] = start_low[...]
    xhigh[pl.ds(0, top), :] = start_high[...]
    for k, (ref, at) in enumerate(near_layers(low, own, high)):
        to = pl.ds(top + k * EDGE, EDGE)
        xlow[to, :] = ref[pl.ds(at * LANES, EDGE), :]
        xhigh[to, :] = ref[pl.ds((at + 1) * LANES - EDGE, EDGE), :]


def flat_sides(rows):
    high, low = parts(rows)
    edges = edge_lanes()
    return dot(edges, high, 1, 1) + dot(edges, low, 1, 1)


def pack_y_kernel(xz, mats, low, own, high, after, before, xm, full, sides, heat_sides, flat_mat, ylow, yhigh):
    count = xz.shape[0]
    blank = jnp.zeros((EDGE, LANES), F32)
    for k in range(count):
        part = pl.ds(k * EDGE, EDGE)
        xm[k, pl.ds(0, EDGE)] = blank
        xm[k, pl.ds(EDGE, EDGE)] = before[part, :]
        xm[k, pl.ds(2 * EDGE, LANES)] = xz[k]
        xm[k, pl.ds(LANES + 2 * EDGE, EDGE)] = after[part, :]
        xm[k, pl.ds(LANES + 3 * EDGE, EDGE)] = blank
    found = near_layers(low, own, high)
    skip = (count - len(found)) // 2
    top = count * (EDGE + 1)
    for k in range(skip):
        full[k] = jnp.zeros(full.shape[1:], F32)
        full[count - 1 - k] = jnp.zeros(full.shape[1:], F32)
    for k, (ref, at) in enumerate(found):
        part = pl.ds(top + k * EDGE, EDGE)
        full[skip + k, pl.ds(0, EDGE)] = before[part, :]
        full[skip + k, pl.ds(EDGE, LANES)] = ref[pl.ds(at * LANES, LANES), :]
        full[skip + k, pl.ds(EDGE + LANES, EDGE)] = after[part, :]
    rows = LANES + 2 * EDGE
    total = count * rows
    found = flat_sides(xm[:, EDGE : EDGE + rows].reshape(total, LANES))
    sides[...] = found
    beside = pl.ds(count * EDGE, count)
    around = jnp.concatenate([before[beside, :], mats[...], after[beside, :]], axis=0)
    q = iota((1, total), 1)
    layer = lax.div(q, rows)
    row = q - layer * rows
    tile = jnp.where(row < EDGE, 0, jnp.where(row < LANES + EDGE, 1, 2))
    lane = row - EDGE + LANES * (1 - tile)
    spread = hot_of(iota((LANES, total), 0) == lane)
    named = dot(around.astype(BF16), spread, 1, 0)
    mine = iota((3 * count, total), 0) == tile * count + layer
    mat = jnp.sum(jnp.where(mine, named, 0.0), axis=0, keepdims=True)
    flat_mat[...] = jnp.broadcast_to(mat, (EDGE, total))
    heat_found = flat_sides(full[...].reshape(total, LANES))
    heat_sides[...] = heat_found
    ylow[pl.ds(0, EDGE), :] = found[:EDGE]
    yhigh[pl.ds(0, EDGE), :] = found[EDGE:]
    ylow[pl.ds(EDGE, EDGE), :] = heat_found[:EDGE]
    yhigh[pl.ds(EDGE, EDGE), :] = heat_found[EDGE:]
    ylow[pl.ds(2 * EDGE - 1, 1), :] = mat
    yhigh[pl.ds(EDGE, 1), :] = mat


def three_parts(v):
    high = v.astype(BF16)
    rest = v - high.astype(F32)
    mid = rest.astype(BF16)
    return high, mid, (rest - mid.astype(F32)).astype(BF16)


def ends_of(strip):
    return jnp.concatenate([strip[EDGE - 1 : EDGE], strip[3 * EDGE : 3 * EDGE + 1]], axis=0)


def end_lanes(depth, times):
    r, y = iota((depth, times * LANES), 0), iota((depth, times * LANES), 1)
    first = (r % 2 == 0) & (y == (r // 2) * LANES)
    last = (r % 2 == 1) & (y == (r // 2) * LANES + LANES - 1)
    return hot_of(first | last)


def turned(v, by, axis):
    return pltpu.roll(v, by % v.shape[axis], axis)


def strip_of(sides, before, after):
    return jnp.concatenate([before, sides, after], axis=0)


def weights_kernel(base, soft, heat, xm, sides, flat_mat, before, after, wz, wx, wy, wyw, inv, b0, strips, cond, cols, ends):
    count, rows = inv.shape[0], inv.shape[1]
    total = count * rows
    mat = jnp.concatenate(
        [flat_mat[0:1], before[pl.ds(EDGE, 1), :], after[pl.ds(2 * EDGE - 1, 1), :]], axis=0
    )
    tables = []
    for values in (base, soft, heat):
        found = jnp.zeros(mat.shape, F32)
        for m in range(values.shape[0]):
            found = jnp.where(mat == F32(m + 1), values[m], found)
        tables.append(found)
    own = [p for t in tables for p in three_parts(t[0:1])]
    r, y = iota((9, 3 * LANES), 0), iota((9, 3 * LANES), 1)
    cols[...] = dot(jnp.concatenate(own, axis=0), hot_of(lax.div(r, 3) == lax.div(y, LANES)), 0, 0)
    wide = lambda t, i: jnp.broadcast_to(t[i : i + 1], (EDGE, total))
    kb, ks, cf = (jnp.concatenate([wide(t, 1), wide(t, 0), wide(t, 0), wide(t, 2)], axis=0) for t in tables)
    sx = strip_of(sides[...], before[:EDGE], after[:EDGE])
    sc = kb / (1.0 + ks * sx)
    down = lambda by, axis: 0.5 * (sc + turned(sc, by, axis))
    around = [down(rows, 1), down(-rows, 1), down(1, 1), down(-1, 1), down(1, 0), down(-1, 0)]
    diag = cf
    for w in around:
        diag = diag + w
    si = jnp.where(cf > 0.0, 1.0 / diag, 0.0)
    for i, w in enumerate(around):
        strips[i] = w * si
    strips[6] = si
    strips[7] = cf * sx * si
    strips[8] = sx
    got = [dot(p, end_lanes(2, 1), 0, 0) for p in three_parts(ends_of(sc))]
    ends[...] = got[0] + got[1] + got[2]

    piece = 16
    blank = jnp.zeros((EDGE, LANES), F32)

    @pl.loop(0, count)
    def _(k):
        cond[k, pl.ds(0, EDGE)] = blank
        cond[k, pl.ds(rows + EDGE, EDGE)] = blank
        wx[k, pl.ds(0, EDGE)] = blank
        wx[k, pl.ds(rows + EDGE, EDGE)] = blank
        for at in range(0, rows, piece):
            part = pl.ds(pl.multiple_of(k * rows + at, 8), piece)
            x = xm[k, pl.ds(EDGE + at, piece)]
            cond[k, pl.ds(EDGE + at, piece)] = cols[part, 0:LANES] / (1.0 + cols[part, LANES : 2 * LANES] * x)

    first, last = iota((piece, LANES), 1) == 0, iota((piece, LANES), 1) == LANES - 1
    wz[0] = 0.5 * (cond[0, pl.ds(EDGE, rows)] + cond[1, pl.ds(EDGE, rows)])

    @pl.loop(1, count - 1)
    def _(k):
        for at in range(0, rows, piece):
            here = pl.ds(EDGE + at, piece)
            part = pl.ds(pl.multiple_of(k * rows + at, 8), piece)
            to = pl.ds(at, piece)
            c, end = cond[k, here], ends[part, :]
            up = 0.5 * (c + cond[k + 1, here])
            low = 0.5 * (c + cond[k - 1, here])
            right = 0.5 * (c + cond[k, pl.ds(EDGE + at + 1, piece)])
            left = 0.5 * (c + cond[k, pl.ds(EDGE + at - 1, piece)])
            e = 0.5 * (c + jnp.where(last, end, turned(c, -1, 1)))
            w = 0.5 * (c + jnp.where(first, end, turned(c, 1, 1)))
            cf = cols[part, 2 * LANES : 3 * LANES]
            diag = cf + up + low + right + left + e + w
            i = jnp.where(cf > 0.0, 1.0 / diag, 0.0)
            wz[k, to] = up
            wx[k, here] = right
            wy[k, to] = e
            wyw[k, to] = w
            inv[k, to] = i
            b0[k, to] = cf * xm[k, here] * i


def sweep_kernel(xm, wz, wx, wy, wyw, inv, b0, strips, full, sides, before, after, low2, high2, ids,
                 out, replies, b, d, xa, xb, ends):
    count, rows, _ = inv.shape
    total = count * rows
    factors = steps()

    sb = strips[7] + strip_of(sides[...], before[EDGE:], after[EDGE:]) * strips[6]
    sx, sd = strips[8], None
    kept = [ends_of(sx)]
    for keep, add in factors[:-1]:
        near = strips[0] * turned(sx, rows, 1) + strips[1] * turned(sx, -rows, 1)
        near += strips[2] * turned(sx, 1, 1) + strips[3] * turned(sx, -1, 1)
        near += strips[4] * turned(sx, 1, 0) + strips[5] * turned(sx, -1, 0)
        step = add * (sb - sx + near)
        sd = step if sd is None else step + keep * sd
        sx = sx + sd
        kept.append(ends_of(sx))
    place_in = end_lanes(2 * SWEEPS, SWEEPS)
    kept = jnp.concatenate(parts(jnp.concatenate(kept, axis=0)), axis=0)
    ends[...] = dot(kept, jnp.concatenate([place_in, place_in], axis=0), 0, 0)

    piece = 24
    first, last = iota((piece, LANES), 1) == 0, iota((piece, LANES), 1) == LANES - 1
    blank = jnp.zeros((EDGE, LANES), F32)

    @pl.loop(0, count)
    def _(k):
        for ref in (xa, xb):
            ref[k, pl.ds(0, EDGE)] = blank
            ref[k, pl.ds(rows + EDGE, EDGE)] = blank

    for s, (keep, add) in enumerate(factors):
        src, into = (xm if s == 0 else (xa if s % 2 else xb)), (xb if s % 2 else xa)

        @pl.loop(1 + s, count - 1 - s)
        def _(k):
            for at in range(0, rows, piece):
                here, to = pl.ds(EDGE + at, piece), pl.ds(at, piece)
                x = src[k, here]
                end = ends[pl.ds(pl.multiple_of(k * rows + at, 8), piece), s * LANES : (s + 1) * LANES]
                e = jnp.where(last, end, turned(x, -1, 1))
                w = jnp.where(first, end, turned(x, 1, 1))
                near = wz[k, to] * src[k + 1, here] + wz[k - 1, to] * src[k - 1, here]
                near += wx[k, here] * src[k, pl.ds(EDGE + at + 1, piece)]
                near += wx[k, pl.ds(EDGE + at - 1, piece)] * src[k, pl.ds(EDGE + at - 1, piece)]
                near += wy[k, to] * e + wyw[k, to] * w
                if s == 0:
                    rhs = b0[k, to] + full[k, to] * inv[k, to]
                    b[k, to] = rhs
                else:
                    rhs = b[k, to]
                step = add * (rhs - x + inv[k, to] * near)
                if s > 0:
                    step = step + keep * d[k, to]
                if s < SWEEPS - 1:
                    d[k, to] = step
                into[k, here] = x + step

    final = xb if SWEEPS % 2 == 0 else xa
    for k in range(4):
        out[pl.ds(k * LANES, LANES), :] = final[SWEEPS + k, pl.ds(2 * EDGE, LANES)]
    scale = 1.0
    for _, add in factors:
        scale = scale * add
    tile = pl.ds(EDGE, LANES)
    for ref, start, way, k in ((low2, 1, 1, 0), (high2, count - 2, -1, 3)):
        gain = scale * inv[start, tile] * ref[...]
        for j in range(1, SWEEPS):
            at = start + way * j
            gain = gain * inv[at, tile] * wz[at - 1 if way > 0 else at, tile]
        to = pl.ds(k * LANES, LANES)
        out[to, :] = out[to, :] + gain
    n = out.shape[0]
    name = ids[...]
    hot = jnp.concatenate([hot_of(name == iota(name.shape, 1) + at) for at in range(0, n, LANES)], axis=1)
    replies[...] = pick_rows(hot, out[...])


def final_kernel(returned, dest, gain, mob, mobility, ionization):
    total = returned.shape[0]
    name = dest[...]
    hot = jnp.concatenate([hot_of(name == iota(name.shape, 1) + at) for at in range(0, total, LANES)], axis=1)
    back = pick_rows(hot, returned[...])
    mobility[...] = mob[...] * jnp.exp(-0.7 * back)
    ionization[...] = jnp.exp(gain[...] * (1.0 + 0.3 * back))


def shifted(v, axis, by):
    count = lax.axis_size(axis)
    pairs = [(i, i + by) for i in range(count) if 0 <= i + by < count]
    return lax.ppermute(v, axis, pairs) if pairs else jnp.zeros_like(v)


def exchanged(v):
    lines = v.reshape(v.shape[0], 1, v.shape[1])
    return lax.all_to_all(lines, ("gx", "gy"), split_axis=0, concat_axis=0, tiled=True).reshape(v.shape)


def per_device(
    efield, density, mobility_prev, thermal_prev, owner, block, live, material,
    mat_conductivity, mat_softening, mat_capacity,
):
    layers, xcells, width = density.shape
    n = layers * xcells
    peers = lax.axis_size("gx") * lax.axis_size("gy")
    slots = max(2, 2 * n // peers)
    line = peers * (slots + 1)
    flat = lambda a: a.reshape(n, width)
    ef = efield.reshape(3, n, width)
    den, mob, x0 = flat(density), flat(mobility_prev), flat(thermal_prev)
    own, blk, liv = owner.reshape(1, n), block.reshape(1, n), live.reshape(1, n)
    mat = material.reshape(layers, xcells)
    sized = lambda *s: (s, F32)

    given = [ef, den, mob, own, blk, liv]
    [sent] = call(
        functools.partial(dispatch_kernel, peers, slots), [sized(line, width)], given, "dispatch", flops=10**8, hbm=True, limit=60,
        scratch=[pltpu.VMEM(a.shape, a.dtype) for a in given] + [pltpu.SemaphoreType.DMA((len(given),))])
    received = exchanged(sent)

    far = SWEEPS - layers
    count = layers + 2 * SWEEPS
    rows = xcells + 2 * EDGE
    total = count * rows
    aside = sized(far * xcells + EDGE, width)
    near, up, down = call(
        functools.partial(start_z_kernel, far), [sized(n + EDGE, width), aside, aside], [x0, mat], "start_z")
    low, high = shifted(near, "gz", 1), shifted(near, "gz", -1)
    low2, high2 = shifted(up, "gz", 2), shifted(down, "gz", -2)
    received, low, high, low2, high2 = lax.optimization_barrier((received, low, high, low2, high2))
    edge = sized(count * (EDGE + 1), width)
    xz, mats, start_low, start_high = call(
        functools.partial(start_x_kernel, far), [sized(count, xcells, width), sized(count, width), edge, edge],
        [low2, low, near, high, high2], "start_x")
    gain, dest = call(functools.partial(after_kernel, slots), [sized(n, width), ((n, LANES), I32)], [ef, own], "gain")

    source, first, last = call(
        functools.partial(combine_kernel, peers, slots), [sized(n, width)] + [sized(xcells, width)] * 2,
        [received], "combine", flops=10**8)
    [ids] = call(functools.partial(ids_kernel, peers, slots), [((peers * slots, LANES), I32)], [received], "ids")
    low, high = shifted(source, "gz", 1), shifted(source, "gz", -1)
    low, high, start_low, start_high = lax.optimization_barrier((low, high, start_low, start_high))
    edge = sized(count * (EDGE + 1) + 3 * layers * EDGE, width)
    xlow, xhigh = call(pack_x_kernel, [edge, edge], [low, source, high, start_low, start_high], "pack_x")
    before, after = shifted(xhigh, "gx", 1), shifted(xlow, "gx", -1)
    before, after, ids, gain, dest = lax.optimization_barrier((before, after, ids, gain, dest))
    tall, tile, flat_edge = sized(count, rows + 2 * EDGE, width), sized(count, rows, width), sized(2 * EDGE, total)
    xm, full, sides, heat_sides, flat_mat, ylow, yhigh = call(
        pack_y_kernel, [tall, tile, flat_edge, flat_edge, sized(EDGE, total), flat_edge, flat_edge],
        [xz, mats, low, source, high, after, before], "pack_y")
    ylow, yhigh, first, last = lax.optimization_barrier((ylow, yhigh, first, last))
    before, after = shifted(yhigh, "gy", 1), shifted(ylow, "gy", -1)
    low2, high2 = shifted(last, "gz", 2), shifted(first, "gz", -2)
    weights = call(
        weights_kernel, [tile, tall, tile, tile, tile, tile, sized(9, 4 * EDGE, total)],
        [mat_conductivity, mat_softening, mat_capacity, xm, sides, flat_mat, before, after], "weights",
        scratch=[pltpu.VMEM((count, rows + 2 * EDGE, width), F32), pltpu.VMEM((total, 3 * width), F32),
                 pltpu.VMEM((total, width), F32)],
        limit=32, flops=10**9, smem=(0, 1, 2))
    x, replies = call(
        sweep_kernel, [sized(n, width), sized(peers * slots, width)],
        [xm] + list(weights) + [full, heat_sides, before, after, low2, high2, ids], "sweeps",
        scratch=[pltpu.VMEM((count, rows, width), F32)] * 2 + [pltpu.VMEM((count, rows + 2 * EDGE, width), F32)] * 2
        + [pltpu.VMEM((total, SWEEPS * width), F32)],
        limit=36, flops=10**8)
    returned = exchanged(replies)
    mobility, ionization = call(final_kernel, [sized(n, width)] * 2, [returned, dest, gain, mob], "finish", flops=10**8)
    shape = density.shape
    return x.reshape(shape), mobility.reshape(shape), ionization.reshape(shape)


def solution(mesh):
    tile = P("gz", "gx", "gy")
    rows = P("gz", "gx", "gy", None)
    placed = (
        P(None, "gz", "gx", "gy"), tile, tile, tile,
        P("gz", "gx", "gy", None, None), rows, rows, rows, P(), P(), P(),
    )
    return jax.shard_map(
        per_device, mesh=mesh, in_specs=placed, out_specs=(tile, tile, tile), check_vma=False
    )
```

```python
import functools

import jax
import jax.numpy as jnp
from jax import lax
from jax.experimental import pallas as pl
from jax.experimental.pallas import tpu as pltpu
from jax.sharding import PartitionSpec as P

SWEEPS = 6
THETA = 1.01
DELTA = 0.99
LANES = 128
EDGE = 8
F32 = jnp.float32
BF16 = jnp.bfloat16
I32 = jnp.int32


def steps():
    sigma = THETA / DELTA
    rho = 1.0 / sigma
    found = [(0.0, 1.0 / THETA)]
    for _ in range(SWEEPS - 1):
        rho_new = 1.0 / (2.0 * sigma - rho)
        found.append((rho_new * rho, 2.0 * rho_new / DELTA))
        rho = rho_new
    return found


def iota(shape, dim):
    return lax.broadcasted_iota(I32, shape, dim)


def dot(a, b, ca, cb):
    return lax.dot_general(a, b, (((ca,), (cb,)), ((), ())), preferred_element_type=F32)


def parts(v):
    high = v.astype(BF16)
    return high, (v - high.astype(F32)).astype(BF16)


def pick_rows(hot, rows):
    high, low = parts(rows)
    got = dot(hot, jnp.concatenate([high, low], axis=1), 1, 0)
    width = rows.shape[1]
    return got[:, :width] + got[:, width:]


def column(row):
    same = iota((LANES, LANES), 0) == iota((LANES, LANES), 1)
    found = []
    for at in range(0, row.shape[1], LANES):
        piece = jnp.broadcast_to(row[:, at : at + LANES], (LANES, LANES))
        found.append(jnp.sum(jnp.where(same, piece, 0), axis=1, keepdims=True))
    return jnp.concatenate(found, axis=0)


def hot_of(cond):
    return jnp.where(cond, F32(1.0), F32(0.0)).astype(BF16)


def edge_lanes():
    r, y = iota((2 * EDGE, LANES), 0), iota((2 * EDGE, LANES), 1)
    return hot_of(y == jnp.where(r < EDGE, r, r + LANES - 2 * EDGE))


def call(kernel, outs, ins, name, scratch=(), limit=32, flops=0, smem=(), hbm=False):
    bytes_of = lambda a: a.size * a.dtype.itemsize
    return pl.pallas_call(
        kernel,
        out_shape=[jax.ShapeDtypeStruct(s, t) for s, t in outs],
        in_specs=[
            pl.BlockSpec(memory_space=pltpu.SMEM if i in smem else pltpu.HBM if hbm else pltpu.VMEM)
            for i in range(len(ins))
        ],
        out_specs=[pl.BlockSpec(memory_space=pltpu.VMEM) for _ in outs],
        scratch_shapes=list(scratch),
        compiler_params=pltpu.CompilerParams(vmem_limit_bytes=limit << 20),
        cost_estimate=pl.CostEstimate(
            flops=flops,
            bytes_accessed=sum(bytes_of(a) for a in ins)
            + sum(jax.ShapeDtypeStruct(s, t).size * 4 for s, t in outs),
            transcendentals=0,
        ),
        name=name,
    )(*ins)


def dispatch_kernel(peers, slots, *refs):
    far, out, near, sems = refs[:6], refs[6], refs[7:13], refs[13]
    copies = [pltpu.make_async_copy(a, b, sems.at[i]) for i, (a, b) in enumerate(zip(far, near))]
    for copy in copies:
        copy.start()
    for copy in copies:
        copy.wait()
    ef, den, mob, owner, block, live = near
    n = owner.shape[1]
    esq = ef[0] * ef[0] + ef[1] * ef[1] + ef[2] * ef[2]
    heat = 0.2 * den[...] * mob[...] * esq
    heat = jnp.where(iota(heat.shape, 1) < column(live[...]), heat, F32(0.0))
    own = owner[...]
    own_col = column(own)
    pos = jnp.zeros((1, n), I32)
    for at in range(0, n, LANES):
        r = iota((LANES, n), 0) + at
        earlier = (own_col[at : at + LANES] == own) & (r < iota((LANES, n), 1))
        pos = pos + jnp.sum(jnp.where(earlier, 1, 0), axis=0, keepdims=True)
    dest = own * (slots + 1) + pos
    hot = hot_of(iota((peers * (slots + 1), n), 0) == dest)
    out[...] = pick_rows(hot, heat)
    named = hot_of(iota((peers, n), 0) == own)
    at_slot = iota((LANES, n), 0) == pos
    code = block[...] + 1
    high = jnp.where(at_slot, code // 32, 0).astype(F32).astype(BF16)
    low = jnp.where(at_slot, code % 32, 0).astype(F32).astype(BF16)
    out[pl.ds(slots, peers, stride=slots + 1), :] = dot(named, high, 1, 1) * 32.0 + dot(named, low, 1, 1)


def after_kernel(slots, ef, owner, gain, dest):
    n = owner.shape[1]
    esq = ef[0] * ef[0] + ef[1] * ef[1] + ef[2] * ef[2]
    gain[...] = -2.0 * lax.rsqrt(esq + 1.0)
    own = owner[...]
    own_col = column(own)
    for at in range(0, n, LANES):
        r = iota((LANES, n), 0) + at
        piece = own_col[at : at + LANES]
        earlier = (piece == own) & (iota((LANES, n), 1) < r)
        pos = jnp.sum(jnp.where(earlier, 1, 0), axis=1, keepdims=True)
        dest[pl.ds(at, LANES), :] = jnp.broadcast_to(piece * slots + pos, (LANES, LANES))


def labels_of(received, peers, slots):
    got = received[pl.ds(slots, peers, stride=slots + 1), :]
    high = jnp.floor(got * (1.0 / 32.0))
    return high.astype(BF16), (got - 32.0 * high).astype(BF16)


def combine_kernel(peers, slots, received, source, first, last):
    n = source.shape[0]
    total = received.shape[0]
    high, low = labels_of(received, peers, slots)
    j = iota((LANES, total), 1)
    spread = hot_of(iota((LANES, total), 0) == j - (slots + 1) * lax.div(j, slots + 1))
    named = dot(high, spread, 1, 0) * 32.0 + dot(low, spread, 1, 0)
    mine = iota((peers, total), 0) == lax.div(iota((peers, total), 1), slots + 1)
    ids = jnp.sum(jnp.where(mine, named, 0.0), axis=0, keepdims=True).astype(I32)
    picks = hot_of(iota((n, total), 0) + 1 == ids)
    source[...] = pick_rows(picks, received[...])
    first[...] = source[pl.ds(0, LANES), :]
    last[...] = source[pl.ds(n - LANES, LANES), :]


def ids_kernel(peers, slots, received, ids):
    total = peers * slots
    high, low = labels_of(received, peers, slots)
    own = hot_of(lax.div(iota((total, peers), 0), slots) == iota((total, peers), 1))
    named = dot(own, high, 1, 0) * 32.0 + dot(own, low, 1, 0)
    i = iota((total, LANES), 0)
    mine = iota((total, LANES), 1) == i - slots * lax.div(i, slots)
    found = jnp.sum(jnp.where(mine, named, 0.0), axis=1, keepdims=True) - 1.0
    ids[...] = jnp.broadcast_to(found, (total, LANES)).astype(I32)


def start_z_kernel(far, x0, material, near, up, down):
    layers, xcells = material.shape
    n = layers * xcells
    mat = (material[...] + 1).astype(F32)
    rows = far * xcells
    zeros = lambda k: jnp.zeros((k, LANES), F32)
    near[pl.ds(0, n), :] = x0[...]
    near[pl.ds(n, EDGE), :] = jnp.concatenate([mat, zeros(EDGE - layers)], axis=0)
    up[pl.ds(0, rows), :] = x0[pl.ds(n - rows, rows), :]
    up[pl.ds(rows, EDGE), :] = jnp.concatenate([mat[layers - far :], zeros(EDGE - far)], axis=0)
    down[pl.ds(0, rows), :] = x0[pl.ds(0, rows), :]
    down[pl.ds(rows, EDGE), :] = jnp.concatenate([mat[:far], zeros(EDGE - far)], axis=0)


def start_x_kernel(far, low2, low, own, high, high2, xz, mats, xlow, xhigh):
    found = [(low2, k) for k in range(far)]
    for ref in (low, own, high):
        found += [(ref, k) for k in range(4)]
    found += [(high2, k) for k in range(far)]
    count = len(found)
    for k, (ref, at) in enumerate(found):
        piece = ref[pl.ds(at * LANES, LANES), :]
        xz[k] = piece
        xlow[pl.ds(k * EDGE, EDGE), :] = piece[:EDGE]
        xhigh[pl.ds(k * EDGE, EDGE), :] = piece[LANES - EDGE :]
        mats[pl.ds(k, 1), :] = ref[pl.ds(ref.shape[0] - EDGE + at, 1), :]
    xlow[pl.ds(count * EDGE, count), :] = mats[...]
    xhigh[pl.ds(count * EDGE, count), :] = mats[...]


def near_layers(low, own, high):
    return [(ref, k) for ref in (low, own, high) for k in range(4)]


def pack_x_kernel(low, own, high, start_low, start_high, xlow, xhigh):
    top = start_low.shape[0]
    xlow[pl.ds(0, top), :] = start_low[...]
    xhigh[pl.ds(0, top), :] = start_high[...]
    for k, (ref, at) in enumerate(near_layers(low, own, high)):
        to = pl.ds(top + k * EDGE, EDGE)
        xlow[to, :] = ref[pl.ds(at * LANES, EDGE), :]
        xhigh[to, :] = ref[pl.ds((at + 1) * LANES - EDGE, EDGE), :]


def flat_sides(rows):
    high, low = parts(rows)
    edges = edge_lanes()
    return dot(edges, high, 1, 1) + dot(edges, low, 1, 1)


def pack_y_kernel(xz, mats, low, own, high, after, before, xm, full, sides, heat_sides, flat_mat, ylow, yhigh):
    count = xz.shape[0]
    blank = jnp.zeros((EDGE, LANES), F32)
    for k in range(count):
        part = pl.ds(k * EDGE, EDGE)
        xm[k, pl.ds(0, EDGE)] = blank
        xm[k, pl.ds(EDGE, EDGE)] = before[part, :]
        xm[k, pl.ds(2 * EDGE, LANES)] = xz[k]
        xm[k, pl.ds(LANES + 2 * EDGE, EDGE)] = after[part, :]
        xm[k, pl.ds(LANES + 3 * EDGE, EDGE)] = blank
    found = near_layers(low, own, high)
    skip = (count - len(found)) // 2
    top = count * (EDGE + 1)
    for k in range(skip):
        full[k] = jnp.zeros(full.shape[1:], F32)
        full[count - 1 - k] = jnp.zeros(full.shape[1:], F32)
    for k, (ref, at) in enumerate(found):
        part = pl.ds(top + k * EDGE, EDGE)
        full[skip + k, pl.ds(0, EDGE)] = before[part, :]
        full[skip + k, pl.ds(EDGE, LANES)] = ref[pl.ds(at * LANES, LANES), :]
        full[skip + k, pl.ds(EDGE + LANES, EDGE)] = after[part, :]
    rows = LANES + 2 * EDGE
    total = count * rows
    found = flat_sides(xm[:, EDGE : EDGE + rows].reshape(total, LANES))
    sides[...] = found
    beside = pl.ds(count * EDGE, count)
    around = jnp.concatenate([before[beside, :], mats[...], after[beside, :]], axis=0)
    q = iota((1, total), 1)
    layer = lax.div(q, rows)
    row = q - layer * rows
    tile = jnp.where(row < EDGE, 0, jnp.where(row < LANES + EDGE, 1, 2))
    lane = row - EDGE + LANES * (1 - tile)
    spread = hot_of(iota((LANES, total), 0) == lane)
    named = dot(around.astype(BF16), spread, 1, 0)
    mine = iota((3 * count, total), 0) == tile * count + layer
    mat = jnp.sum(jnp.where(mine, named, 0.0), axis=0, keepdims=True)
    flat_mat[...] = jnp.broadcast_to(mat, (EDGE, total))
    heat_found = flat_sides(full[...].reshape(total, LANES))
    heat_sides[...] = heat_found
    ylow[pl.ds(0, EDGE), :] = found[:EDGE]
    yhigh[pl.ds(0, EDGE), :] = found[EDGE:]
    ylow[pl.ds(EDGE, EDGE), :] = heat_found[:EDGE]
    yhigh[pl.ds(EDGE, EDGE), :] = heat_found[EDGE:]
    ylow[pl.ds(2 * EDGE - 1, 1), :] = mat
    yhigh[pl.ds(EDGE, 1), :] = mat


def three_parts(v):
    high = v.astype(BF16)
    rest = v - high.astype(F32)
    mid = rest.astype(BF16)
    return high, mid, (rest - mid.astype(F32)).astype(BF16)


def ends_of(strip):
    return jnp.concatenate([strip[EDGE - 1 : EDGE], strip[3 * EDGE : 3 * EDGE + 1]], axis=0)


def end_lanes(depth, times):
    r, y = iota((depth, times * LANES), 0), iota((depth, times * LANES), 1)
    first = (r % 2 == 0) & (y == (r // 2) * LANES)
    last = (r % 2 == 1) & (y == (r // 2) * LANES + LANES - 1)
    return hot_of(first | last)


def turned(v, by, axis):
    return pltpu.roll(v, by % v.shape[axis], axis)


def strip_of(sides, before, after):
    return jnp.concatenate([before, sides, after], axis=0)


def weights_kernel(base, soft, heat, xm, sides, flat_mat, before, after, wz, wx, wy, wyw, inv, b0, strips, cond, cols, ends):
    count, rows = inv.shape[0], inv.shape[1]
    total = count * rows
    mat = jnp.concatenate(
        [flat_mat[0:1], before[pl.ds(EDGE, 1), :], after[pl.ds(2 * EDGE - 1, 1), :]], axis=0
    )
    tables = []
    for values in (base, soft, heat):
        found = jnp.zeros(mat.shape, F32)
        for m in range(values.shape[0]):
            found = jnp.where(mat == F32(m + 1), values[m], found)
        tables.append(found)
    own = [p for t in tables for p in three_parts(t[0:1])]
    r, y = iota((9, 3 * LANES), 0), iota((9, 3 * LANES), 1)
    cols[...] = dot(jnp.concatenate(own, axis=0), hot_of(lax.div(r, 3) == lax.div(y, LANES)), 0, 0)
    wide = lambda t, i: jnp.broadcast_to(t[i : i + 1], (EDGE, total))
    kb, ks, cf = (jnp.concatenate([wide(t, 1), wide(t, 0), wide(t, 0), wide(t, 2)], axis=0) for t in tables)
    sx = strip_of(sides[...], before[:EDGE], after[:EDGE])
    sc = kb / (1.0 + ks * sx)
    down = lambda by, axis: 0.5 * (sc + turned(sc, by, axis))
    around = [down(rows, 1), down(-rows, 1), down(1, 1), down(-1, 1), down(1, 0), down(-1, 0)]
    diag = cf
    for w in around:
        diag = diag + w
    si = jnp.where(cf > 0.0, 1.0 / diag, 0.0)
    for i, w in enumerate(around):
        strips[i] = w * si
    strips[6] = si
    strips[7] = cf * sx * si
    strips[8] = sx
    got = [dot(p, end_lanes(2, 1), 0, 0) for p in three_parts(ends_of(sc))]
    ends[...] = got[0] + got[1] + got[2]

    piece = 16
    blank = jnp.zeros((EDGE, LANES), F32)

    @pl.loop(0, count)
    def _(k):
        cond[k, pl.ds(0, EDGE)] = blank
        cond[k, pl.ds(rows + EDGE, EDGE)] = blank
        wx[k, pl.ds(0, EDGE)] = blank
        wx[k, pl.ds(rows + EDGE, EDGE)] = blank
        for at in range(0, rows, piece):
            part = pl.ds(pl.multiple_of(k * rows + at, 8), piece)
            x = xm[k, pl.ds(EDGE + at, piece)]
            cond[k, pl.ds(EDGE + at, piece)] = cols[part, 0:LANES] / (1.0 + cols[part, LANES : 2 * LANES] * x)

    first, last = iota((piece, LANES), 1) == 0, iota((piece, LANES), 1) == LANES - 1
    wz[0] = 0.5 * (cond[0, pl.ds(EDGE, rows)] + cond[1, pl.ds(EDGE, rows)])

    @pl.loop(1, count - 1)
    def _(k):
        for at in range(0, rows, piece):
            here = pl.ds(EDGE + at, piece)
            part = pl.ds(pl.multiple_of(k * rows + at, 8), piece)
            to = pl.ds(at, piece)
            c, end = cond[k, here], ends[part, :]
            up = 0.5 * (c + cond[k + 1, here])
            low = 0.5 * (c + cond[k - 1, here])
            right = 0.5 * (c + cond[k, pl.ds(EDGE + at + 1, piece)])
            left = 0.5 * (c + cond[k, pl.ds(EDGE + at - 1, piece)])
            e = 0.5 * (c + jnp.where(last, end, turned(c, -1, 1)))
            w = 0.5 * (c + jnp.where(first, end, turned(c, 1, 1)))
            cf = cols[part, 2 * LANES : 3 * LANES]
            diag = cf + up + low + right + left + e + w
            i = jnp.where(cf > 0.0, 1.0 / diag, 0.0)
            wz[k, to] = up
            wx[k, here] = right
            wy[k, to] = e
            wyw[k, to] = w
            inv[k, to] = i
            b0[k, to] = cf * xm[k, here] * i


def sweep_kernel(xm, wz, wx, wy, wyw, inv, b0, strips, full, sides, before, after,
                 out, pull, b, d, xa, xb, ends):
    count, rows, _ = inv.shape
    total = count * rows
    factors = steps()

    sb = strips[7] + strip_of(sides[...], before[EDGE:], after[EDGE:]) * strips[6]
    sx, sd = strips[8], None
    kept = [ends_of(sx)]
    for keep, add in factors[:-1]:
        near = strips[0] * turned(sx, rows, 1) + strips[1] * turned(sx, -rows, 1)
        near += strips[2] * turned(sx, 1, 1) + strips[3] * turned(sx, -1, 1)
        near += strips[4] * turned(sx, 1, 0) + strips[5] * turned(sx, -1, 0)
        step = add * (sb - sx + near)
        sd = step if sd is None else step + keep * sd
        sx = sx + sd
        kept.append(ends_of(sx))
    place_in = end_lanes(2, 1)
    place_in = jnp.concatenate([place_in, place_in], axis=0)
    for s, pair in enumerate(kept):
        start = (1 + s) * rows // LANES * LANES
        stop = -(-(count - 1 - s) * rows // LANES) * LANES
        ends[start:stop, s * LANES : (s + 1) * LANES] = dot(
            jnp.concatenate(parts(pair[:, start:stop]), axis=0), place_in, 0, 0)

    piece = 24
    first, last = iota((piece, LANES), 1) == 0, iota((piece, LANES), 1) == LANES - 1
    blank = jnp.zeros((EDGE, LANES), F32)

    @pl.loop(0, count)
    def _(k):
        for ref in (xa, xb):
            ref[k, pl.ds(0, EDGE)] = blank
            ref[k, pl.ds(rows + EDGE, EDGE)] = blank

    for s, (keep, add) in enumerate(factors):
        src, into = (xm if s == 0 else (xa if s % 2 else xb)), (xb if s % 2 else xa)

        @pl.loop(1 + s, count - 1 - s)
        def _(k):
            for at in range(0, rows, piece):
                here, to = pl.ds(EDGE + at, piece), pl.ds(at, piece)
                x = src[k, here]
                end = ends[pl.ds(pl.multiple_of(k * rows + at, 8), piece), s * LANES : (s + 1) * LANES]
                e = jnp.where(last, end, turned(x, -1, 1))
                w = jnp.where(first, end, turned(x, 1, 1))
                near = wz[k, to] * src[k + 1, here] + wz[k - 1, to] * src[k - 1, here]
                near += wx[k, here] * src[k, pl.ds(EDGE + at + 1, piece)]
                near += wx[k, pl.ds(EDGE + at - 1, piece)] * src[k, pl.ds(EDGE + at - 1, piece)]
                near += wy[k, to] * e + wyw[k, to] * w
                if s == 0:
                    rhs = b0[k, to] + full[k, to] * inv[k, to]
                    b[k, to] = rhs
                else:
                    rhs = b[k, to]
                step = add * (rhs - x + inv[k, to] * near)
                if s > 0:
                    step = step + keep * d[k, to]
                if s < SWEEPS - 1:
                    d[k, to] = step
                into[k, here] = x + step

    final = xb if SWEEPS % 2 == 0 else xa
    for k in range(4):
        out[pl.ds(k * LANES, LANES), :] = final[SWEEPS + k, pl.ds(2 * EDGE, LANES)]
    scale = 1.0
    for _, add in factors:
        scale = scale * add
    tile = pl.ds(EDGE, LANES)
    for i, (start, way) in enumerate(((1, 1), (count - 2, -1))):
        gain = scale * inv[start, tile]
        for j in range(1, SWEEPS):
            at = start + way * j
            gain = gain * inv[at, tile] * wz[at - 1 if way > 0 else at, tile]
        pull[pl.ds(i * LANES, LANES), :] = gain


def reply_kernel(x, pull, low2, high2, ids, out, replies):
    n = out.shape[0]
    first, last = pl.ds(0, LANES), pl.ds(n - LANES, LANES)
    out[...] = x[...]
    out[first, :] = x[first, :] + pull[pl.ds(0, LANES), :] * low2[...]
    out[last, :] = x[last, :] + pull[pl.ds(LANES, LANES), :] * high2[...]
    name = ids[...]
    hot = jnp.concatenate([hot_of(name == iota(name.shape, 1) + at) for at in range(0, n, LANES)], axis=1)
    replies[...] = pick_rows(hot, out[...])


def final_kernel(returned, dest, gain, mob, mobility, ionization):
    total = returned.shape[0]
    name = dest[...]
    hot = jnp.concatenate([hot_of(name == iota(name.shape, 1) + at) for at in range(0, total, LANES)], axis=1)
    back = pick_rows(hot, returned[...])
    mobility[...] = mob[...] * jnp.exp(-0.7 * back)
    ionization[...] = jnp.exp(gain[...] * (1.0 + 0.3 * back))


def shifted(v, axis, by):
    count = lax.axis_size(axis)
    pairs = [(i, i + by) for i in range(count) if 0 <= i + by < count]
    return lax.ppermute(v, axis, pairs) if pairs else jnp.zeros_like(v)


def exchanged(v):
    lines = v.reshape(v.shape[0], 1, v.shape[1])
    return lax.all_to_all(lines, ("gx", "gy"), split_axis=0, concat_axis=0, tiled=True).reshape(v.shape)


def per_device(
    efield, density, mobility_prev, thermal_prev, owner, block, live, material,
    mat_conductivity, mat_softening, mat_capacity,
):
    layers, xcells, width = density.shape
    n = layers * xcells
    peers = lax.axis_size("gx") * lax.axis_size("gy")
    slots = max(2, 2 * n // peers)
    line = peers * (slots + 1)
    flat = lambda a: a.reshape(n, width)
    ef = efield.reshape(3, n, width)
    den, mob, x0 = flat(density), flat(mobility_prev), flat(thermal_prev)
    own, blk, liv = owner.reshape(1, n), block.reshape(1, n), live.reshape(1, n)
    mat = material.reshape(layers, xcells)
    sized = lambda *s: (s, F32)

    given = [ef, den, mob, own, blk, liv]
    [sent] = call(
        functools.partial(dispatch_kernel, peers, slots), [sized(line, width)], given, "dispatch", flops=10**8, hbm=True, limit=60,
        scratch=[pltpu.VMEM(a.shape, a.dtype) for a in given] + [pltpu.SemaphoreType.DMA((len(given),))])
    received = exchanged(sent)

    far = SWEEPS - layers
    count = layers + 2 * SWEEPS
    rows = xcells + 2 * EDGE
    total = count * rows
    aside = sized(far * xcells + EDGE, width)
    near, up, down = call(
        functools.partial(start_z_kernel, far), [sized(n + EDGE, width), aside, aside], [x0, mat], "start_z")
    low, high = shifted(near, "gz", 1), shifted(near, "gz", -1)
    low2, high2 = shifted(up, "gz", 2), shifted(down, "gz", -2)
    received, low, high, low2, high2 = lax.optimization_barrier((received, low, high, low2, high2))
    edge = sized(count * (EDGE + 1), width)
    xz, mats, start_low, start_high = call(
        functools.partial(start_x_kernel, far), [sized(count, xcells, width), sized(count, width), edge, edge],
        [low2, low, near, high, high2], "start_x")
    gain, dest = call(functools.partial(after_kernel, slots), [sized(n, width), ((n, LANES), I32)], [ef, own], "gain")

    source, first, last = call(
        functools.partial(combine_kernel, peers, slots), [sized(n, width)] + [sized(xcells, width)] * 2,
        [received], "combine", flops=10**8)
    [ids] = call(functools.partial(ids_kernel, peers, slots), [((peers * slots, LANES), I32)], [received], "ids")
    low, high = shifted(source, "gz", 1), shifted(source, "gz", -1)
    low, high, start_low, start_high = lax.optimization_barrier((low, high, start_low, start_high))
    edge = sized(count * (EDGE + 1) + 3 * layers * EDGE, width)
    xlow, xhigh = call(pack_x_kernel, [edge, edge], [low, source, high, start_low, start_high], "pack_x")
    before, after = shifted(xhigh, "gx", 1), shifted(xlow, "gx", -1)
    before, after, ids, gain, dest = lax.optimization_barrier((before, after, ids, gain, dest))
    tall, tile, flat_edge = sized(count, rows + 2 * EDGE, width), sized(count, rows, width), sized(2 * EDGE, total)
    xm, full, sides, heat_sides, flat_mat, ylow, yhigh = call(
        pack_y_kernel, [tall, tile, flat_edge, flat_edge, sized(EDGE, total), flat_edge, flat_edge],
        [xz, mats, low, source, high, after, before], "pack_y")
    ylow, yhigh, first, last = lax.optimization_barrier((ylow, yhigh, first, last))
    before, after = shifted(yhigh, "gy", 1), shifted(ylow, "gy", -1)
    low2, high2 = shifted(last, "gz", 2), shifted(first, "gz", -2)
    weights = call(
        weights_kernel, [tile, tall, tile, tile, tile, tile, sized(9, 4 * EDGE, total)],
        [mat_conductivity, mat_softening, mat_capacity, xm, sides, flat_mat, before, after], "weights",
        scratch=[pltpu.VMEM((count, rows + 2 * EDGE, width), F32), pltpu.VMEM((total, 3 * width), F32),
                 pltpu.VMEM((total, width), F32)],
        limit=32, flops=10**9, smem=(0, 1, 2))
    x, pull = call(
        sweep_kernel, [sized(n, width), sized(2 * xcells, width)],
        [xm] + list(weights) + [full, heat_sides, before, after], "sweeps",
        scratch=[pltpu.VMEM((count, rows, width), F32)] * 2 + [pltpu.VMEM((count, rows + 2 * EDGE, width), F32)] * 2
        + [pltpu.VMEM((total, SWEEPS * width), F32)],
        limit=36, flops=10**8)
    x, pull, low2, high2 = lax.optimization_barrier((x, pull, low2, high2))
    x, replies = call(
        reply_kernel, [sized(n, width), sized(peers * slots, width)], [x, pull, low2, high2, ids], "reply", flops=10**8)
    returned = exchanged(replies)
    mobility, ionization = call(final_kernel, [sized(n, width)] * 2, [returned, dest, gain, mob], "finish", flops=10**8)
    shape = density.shape
    return x.reshape(shape), mobility.reshape(shape), ionization.reshape(shape)


def solution(mesh):
    tile = P("gz", "gx", "gy")
    rows = P("gz", "gx", "gy", None)
    placed = (
        P(None, "gz", "gx", "gy"), tile, tile, tile,
        P("gz", "gx", "gy", None, None), rows, rows, rows, P(), P(), P(),
    )
    return jax.shard_map(
        per_device, mesh=mesh, in_specs=placed, out_specs=(tile, tile, tile), check_vma=False
    )
```

```python
import functools

import jax
import jax.numpy as jnp
from jax import lax
from jax.experimental import pallas as pl
from jax.experimental.pallas import tpu as pltpu
from jax.sharding import PartitionSpec as P

SWEEPS = 6
THETA = 1.01
DELTA = 0.99
LANES = 128
EDGE = 8
F32 = jnp.float32
BF16 = jnp.bfloat16
I32 = jnp.int32


def steps():
    sigma = THETA / DELTA
    rho = 1.0 / sigma
    found = [(0.0, 1.0 / THETA)]
    for _ in range(SWEEPS - 1):
        rho_new = 1.0 / (2.0 * sigma - rho)
        found.append((rho_new * rho, 2.0 * rho_new / DELTA))
        rho = rho_new
    return found


def iota(shape, dim):
    return lax.broadcasted_iota(I32, shape, dim)


def dot(a, b, ca, cb):
    return lax.dot_general(a, b, (((ca,), (cb,)), ((), ())), preferred_element_type=F32)


def parts(v):
    high = v.astype(BF16)
    return high, (v - high.astype(F32)).astype(BF16)


def pick_rows(hot, rows):
    high, low = parts(rows)
    got = dot(hot, jnp.concatenate([high, low], axis=1), 1, 0)
    width = rows.shape[1]
    return got[:, :width] + got[:, width:]


def column(row):
    same = iota((LANES, LANES), 0) == iota((LANES, LANES), 1)
    found = []
    for at in range(0, row.shape[1], LANES):
        piece = jnp.broadcast_to(row[:, at : at + LANES], (LANES, LANES))
        found.append(jnp.sum(jnp.where(same, piece, 0), axis=1, keepdims=True))
    return jnp.concatenate(found, axis=0)


def hot_of(cond):
    return jnp.where(cond, F32(1.0), F32(0.0)).astype(BF16)


def edge_lanes():
    r, y = iota((2 * EDGE, LANES), 0), iota((2 * EDGE, LANES), 1)
    return hot_of(y == jnp.where(r < EDGE, r, r + LANES - 2 * EDGE))


def call(kernel, outs, ins, name, scratch=(), limit=32, flops=0, smem=(), hbm=False):
    bytes_of = lambda a: a.size * a.dtype.itemsize
    return pl.pallas_call(
        kernel,
        out_shape=[jax.ShapeDtypeStruct(s, t) for s, t in outs],
        in_specs=[
            pl.BlockSpec(memory_space=pltpu.SMEM if i in smem else pltpu.HBM if hbm else pltpu.VMEM)
            for i in range(len(ins))
        ],
        out_specs=[pl.BlockSpec(memory_space=pltpu.VMEM) for _ in outs],
        scratch_shapes=list(scratch),
        compiler_params=pltpu.CompilerParams(vmem_limit_bytes=limit << 20),
        cost_estimate=pl.CostEstimate(
            flops=flops,
            bytes_accessed=sum(bytes_of(a) for a in ins)
            + sum(jax.ShapeDtypeStruct(s, t).size * 4 for s, t in outs),
            transcendentals=0,
        ),
        name=name,
    )(*ins)


def dispatch_kernel(peers, slots, *refs):
    far, out, near, sems = refs[:6], refs[6], refs[7:13], refs[13]
    copies = [pltpu.make_async_copy(a, b, sems.at[i]) for i, (a, b) in enumerate(zip(far, near))]
    for copy in copies[3:] + copies[:3]:
        copy.start()
    for copy in copies[3:]:
        copy.wait()
    ef, den, mob, owner, block, live = near
    n = owner.shape[1]
    own = owner[...]
    own_col = column(own)
    pos = jnp.zeros((1, n), I32)
    for at in range(0, n, LANES):
        r = iota((LANES, n), 0) + at
        earlier = (own_col[at : at + LANES] == own) & (r < iota((LANES, n), 1))
        pos = pos + jnp.sum(jnp.where(earlier, 1, 0), axis=0, keepdims=True)
    dest = own * (slots + 1) + pos
    hot = hot_of(iota((peers * (slots + 1), n), 0) == dest)
    named = hot_of(iota((peers, n), 0) == own)
    at_slot = iota((LANES, n), 0) == pos
    code = block[...] + 1
    high = jnp.where(at_slot, code // 32, 0).astype(F32).astype(BF16)
    low = jnp.where(at_slot, code % 32, 0).astype(F32).astype(BF16)
    labels = dot(named, high, 1, 1) * 32.0 + dot(named, low, 1, 1)
    live_col = column(live[...])
    for copy in copies[:3]:
        copy.wait()
    esq = ef[0] * ef[0] + ef[1] * ef[1] + ef[2] * ef[2]
    heat = 0.2 * den[...] * mob[...] * esq
    heat = jnp.where(iota(heat.shape, 1) < live_col, heat, F32(0.0))
    out[...] = pick_rows(hot, heat)
    out[pl.ds(slots, peers, stride=slots + 1), :] = labels


def after_kernel(slots, ef, owner, gain, hot):
    n = owner.shape[1]
    esq = ef[0] * ef[0] + ef[1] * ef[1] + ef[2] * ef[2]
    gain[...] = -2.0 * lax.rsqrt(esq + 1.0)
    own = owner[...]
    own_col = column(own)
    for at in range(0, n, LANES):
        r = iota((LANES, n), 0) + at
        piece = own_col[at : at + LANES]
        earlier = (piece == own) & (iota((LANES, n), 1) < r)
        pos = jnp.sum(jnp.where(earlier, 1, 0), axis=1, keepdims=True)
        size = (LANES, hot.shape[1])
        hot[pl.ds(at, LANES), :] = hot_of(jnp.broadcast_to(piece * slots + pos, size) == iota(size, 1))


def labels_of(received, peers, slots):
    got = received[pl.ds(slots, peers, stride=slots + 1), :]
    high = jnp.floor(got * (1.0 / 32.0))
    return high.astype(BF16), (got - 32.0 * high).astype(BF16)


def combine_kernel(peers, slots, received, source, first, last):
    n = source.shape[0]
    total = received.shape[0]
    high, low = labels_of(received, peers, slots)
    j = iota((LANES, total), 1)
    spread = hot_of(iota((LANES, total), 0) == j - (slots + 1) * lax.div(j, slots + 1))
    named = dot(high, spread, 1, 0) * 32.0 + dot(low, spread, 1, 0)
    mine = iota((peers, total), 0) == lax.div(iota((peers, total), 1), slots + 1)
    ids = jnp.sum(jnp.where(mine, named, 0.0), axis=0, keepdims=True).astype(I32)
    picks = hot_of(iota((n, total), 0) + 1 == ids)
    source[...] = pick_rows(picks, received[...])
    first[...] = source[pl.ds(0, LANES), :]
    last[...] = source[pl.ds(n - LANES, LANES), :]


def ids_kernel(peers, slots, received, hot):
    total = peers * slots
    high, low = labels_of(received, peers, slots)
    own = hot_of(lax.div(iota((total, peers), 0), slots) == iota((total, peers), 1))
    named = dot(own, high, 1, 0) * 32.0 + dot(own, low, 1, 0)
    i = iota((total, LANES), 0)
    mine = iota((total, LANES), 1) == i - slots * lax.div(i, slots)
    found = jnp.sum(jnp.where(mine, named, 0.0), axis=1, keepdims=True) - 1.0
    hot[...] = hot_of(jnp.broadcast_to(found.astype(I32), hot.shape) == iota(hot.shape, 1))


def start_z_kernel(far, x0, material, near, up, down):
    layers, xcells = material.shape
    n = layers * xcells
    mat = (material[...] + 1).astype(F32)
    rows = far * xcells
    zeros = lambda k: jnp.zeros((k, LANES), F32)
    near[pl.ds(0, n), :] = x0[...]
    near[pl.ds(n, EDGE), :] = jnp.concatenate([mat, zeros(EDGE - layers)], axis=0)
    up[pl.ds(0, rows), :] = x0[pl.ds(n - rows, rows), :]
    up[pl.ds(rows, EDGE), :] = jnp.concatenate([mat[layers - far :], zeros(EDGE - far)], axis=0)
    down[pl.ds(0, rows), :] = x0[pl.ds(0, rows), :]
    down[pl.ds(rows, EDGE), :] = jnp.concatenate([mat[:far], zeros(EDGE - far)], axis=0)


def start_x_kernel(far, low2, low, own, high, high2, xz, mats, xlow, xhigh):
    found = [(low2, k) for k in range(far)]
    for ref in (low, own, high):
        found += [(ref, k) for k in range(4)]
    found += [(high2, k) for k in range(far)]
    count = len(found)
    for k, (ref, at) in enumerate(found):
        piece = ref[pl.ds(at * LANES, LANES), :]
        xz[k] = piece
        xlow[pl.ds(k * EDGE, EDGE), :] = piece[:EDGE]
        xhigh[pl.ds(k * EDGE, EDGE), :] = piece[LANES - EDGE :]
        mats[pl.ds(k, 1), :] = ref[pl.ds(ref.shape[0] - EDGE + at, 1), :]
    xlow[pl.ds(count * EDGE, count), :] = mats[...]
    xhigh[pl.ds(count * EDGE, count), :] = mats[...]


def near_layers(low, own, high):
    return [(ref, k) for ref in (low, own, high) for k in range(4)]


def pack_x_kernel(low, own, high, start_low, start_high, xlow, xhigh):
    top = start_low.shape[0]
    xlow[pl.ds(0, top), :] = start_low[...]
    xhigh[pl.ds(0, top), :] = start_high[...]
    for k, (ref, at) in enumerate(near_layers(low, own, high)):
        to = pl.ds(top + k * EDGE, EDGE)
        xlow[to, :] = ref[pl.ds(at * LANES, EDGE), :]
        xhigh[to, :] = ref[pl.ds((at + 1) * LANES - EDGE, EDGE), :]


def flat_sides(rows):
    high, low = parts(rows)
    edges = edge_lanes()
    return dot(edges, high, 1, 1) + dot(edges, low, 1, 1)


def pack_y_kernel(xz, mats, low, own, high, after, before, xm, full, sides, heat_sides, flat_mat, ylow, yhigh):
    count = xz.shape[0]
    blank = jnp.zeros((EDGE, LANES), F32)
    for k in range(count):
        part = pl.ds(k * EDGE, EDGE)
        xm[k, pl.ds(0, EDGE)] = blank
        xm[k, pl.ds(EDGE, EDGE)] = before[part, :]
        xm[k, pl.ds(2 * EDGE, LANES)] = xz[k]
        xm[k, pl.ds(LANES + 2 * EDGE, EDGE)] = after[part, :]
        xm[k, pl.ds(LANES + 3 * EDGE, EDGE)] = blank
    found = near_layers(low, own, high)
    skip = (count - len(found)) // 2
    top = count * (EDGE + 1)
    for k in range(skip):
        full[k] = jnp.zeros(full.shape[1:], F32)
        full[count - 1 - k] = jnp.zeros(full.shape[1:], F32)
    for k, (ref, at) in enumerate(found):
        part = pl.ds(top + k * EDGE, EDGE)
        full[skip + k, pl.ds(0, EDGE)] = before[part, :]
        full[skip + k, pl.ds(EDGE, LANES)] = ref[pl.ds(at * LANES, LANES), :]
        full[skip + k, pl.ds(EDGE + LANES, EDGE)] = after[part, :]
    rows = LANES + 2 * EDGE
    total = count * rows
    found = flat_sides(xm[:, EDGE : EDGE + rows].reshape(total, LANES))
    sides[...] = found
    beside = pl.ds(count * EDGE, count)
    around = jnp.concatenate([before[beside, :], mats[...], after[beside, :]], axis=0)
    q = iota((1, total), 1)
    layer = lax.div(q, rows)
    row = q - layer * rows
    tile = jnp.where(row < EDGE, 0, jnp.where(row < LANES + EDGE, 1, 2))
    lane = row - EDGE + LANES * (1 - tile)
    spread = hot_of(iota((LANES, total), 0) == lane)
    named = dot(around.astype(BF16), spread, 1, 0)
    mine = iota((3 * count, total), 0) == tile * count + layer
    mat = jnp.sum(jnp.where(mine, named, 0.0), axis=0, keepdims=True)
    flat_mat[...] = jnp.broadcast_to(mat, (EDGE, total))
    heat_found = flat_sides(full[...].reshape(total, LANES))
    heat_sides[...] = heat_found
    ylow[pl.ds(0, EDGE), :] = found[:EDGE]
    yhigh[pl.ds(0, EDGE), :] = found[EDGE:]
    ylow[pl.ds(EDGE, EDGE), :] = heat_found[:EDGE]
    yhigh[pl.ds(EDGE, EDGE), :] = heat_found[EDGE:]
    ylow[pl.ds(2 * EDGE - 1, 1), :] = mat
    yhigh[pl.ds(EDGE, 1), :] = mat


def inverse(v):
    guess = pl.reciprocal(v, approx=True)
    guess = guess * (2.0 - v * guess)
    return guess * (2.0 - v * guess)


def three_parts(v):
    high = v.astype(BF16)
    rest = v - high.astype(F32)
    mid = rest.astype(BF16)
    return high, mid, (rest - mid.astype(F32)).astype(BF16)


def ends_of(strip):
    return jnp.concatenate([strip[EDGE - 1 : EDGE], strip[3 * EDGE : 3 * EDGE + 1]], axis=0)


def end_lanes(depth, times):
    r, y = iota((depth, times * LANES), 0), iota((depth, times * LANES), 1)
    first = (r % 2 == 0) & (y == (r // 2) * LANES)
    last = (r % 2 == 1) & (y == (r // 2) * LANES + LANES - 1)
    return hot_of(first | last)


def turned(v, by, axis):
    return pltpu.roll(v, by % v.shape[axis], axis)


def strip_of(sides, before, after):
    return jnp.concatenate([before, sides, after], axis=0)


def weights_kernel(base, soft, heat, xm, sides, flat_mat, before, after, wz, wx, wxl, wy, wyw, inv, b0, strips, cond, cols, ends):
    count, rows = inv.shape[0], inv.shape[1]
    total = count * rows
    mat = jnp.concatenate(
        [flat_mat[0:1], before[pl.ds(EDGE, 1), :], after[pl.ds(2 * EDGE - 1, 1), :]], axis=0
    )
    tables = []
    for values in (base, soft, heat):
        found = jnp.zeros(mat.shape, F32)
        for m in range(values.shape[0]):
            found = jnp.where(mat == F32(m + 1), values[m], found)
        tables.append(found)
    own = [p for t in tables for p in three_parts(t[0:1])]
    r, y = iota((9, 3 * LANES), 0), iota((9, 3 * LANES), 1)
    cols[...] = dot(jnp.concatenate(own, axis=0), hot_of(lax.div(r, 3) == lax.div(y, LANES)), 0, 0)
    wide = lambda t, i: jnp.broadcast_to(t[i : i + 1], (EDGE, total))
    kb, ks, cf = (jnp.concatenate([wide(t, 1), wide(t, 0), wide(t, 0), wide(t, 2)], axis=0) for t in tables)
    sx = strip_of(sides[...], before[:EDGE], after[:EDGE])
    sc = kb * inverse(1.0 + ks * sx)
    down = lambda by, axis: 0.5 * (sc + turned(sc, by, axis))
    around = [down(rows, 1), down(-rows, 1), down(1, 1), down(-1, 1), down(1, 0), down(-1, 0)]
    diag = cf
    for w in around:
        diag = diag + w
    si = jnp.where(cf > 0.0, inverse(diag), 0.0)
    for i, w in enumerate(around):
        strips[i] = w * si
    strips[6] = si
    strips[7] = cf * sx * si
    strips[8] = sx
    got = [dot(p, end_lanes(2, 1), 0, 0) for p in three_parts(ends_of(sc))]
    ends[...] = got[0] + got[1] + got[2]

    piece = 16
    blank = jnp.zeros((EDGE, LANES), F32)

    @pl.loop(0, count)
    def _(k):
        cond[k, pl.ds(0, EDGE)] = blank
        cond[k, pl.ds(rows + EDGE, EDGE)] = blank
        for at in range(0, rows, piece):
            part = pl.ds(pl.multiple_of(k * rows + at, 8), piece)
            x = xm[k, pl.ds(EDGE + at, piece)]
            cond[k, pl.ds(EDGE + at, piece)] = cols[part, 0:LANES] * inverse(1.0 + cols[part, LANES : 2 * LANES] * x)

    first, last = iota((piece, LANES), 1) == 0, iota((piece, LANES), 1) == LANES - 1
    wz[0] = 0.5 * (cond[0, pl.ds(EDGE, rows)] + cond[1, pl.ds(EDGE, rows)])

    @pl.loop(1, count - 1)
    def _(k):
        for at in range(0, rows, piece):
            here = pl.ds(EDGE + at, piece)
            part = pl.ds(pl.multiple_of(k * rows + at, 8), piece)
            to = pl.ds(at, piece)
            c, end = cond[k, here], ends[part, :]
            up = 0.5 * (c + cond[k + 1, here])
            low = 0.5 * (c + cond[k - 1, here])
            right = 0.5 * (c + cond[k, pl.ds(EDGE + at + 1, piece)])
            left = 0.5 * (c + cond[k, pl.ds(EDGE + at - 1, piece)])
            e = 0.5 * (c + jnp.where(last, end, turned(c, -1, 1)))
            w = 0.5 * (c + jnp.where(first, end, turned(c, 1, 1)))
            cf = cols[part, 2 * LANES : 3 * LANES]
            diag = cf + up + low + right + left + e + w
            i = jnp.where(cf > 0.0, inverse(diag), 0.0)
            wz[k, to] = up
            wx[k, to] = right
            wxl[k, to] = left
            wy[k, to] = e
            wyw[k, to] = w
            inv[k, to] = i
            b0[k, to] = cf * xm[k, here] * i


def sweep_kernel(xm, wz, wx, wxl, wy, wyw, inv, b0, strips, full, sides, before, after,
                 out, pull, b, d, xa, xb, ends):
    count, rows, _ = inv.shape
    total = count * rows
    factors = steps()

    sb = strips[7] + strip_of(sides[...], before[EDGE:], after[EDGE:]) * strips[6]
    sx, sd = strips[8], None
    kept = [ends_of(sx)]
    for keep, add in factors[:-1]:
        near = strips[0] * turned(sx, rows, 1) + strips[1] * turned(sx, -rows, 1)
        near += strips[2] * turned(sx, 1, 1) + strips[3] * turned(sx, -1, 1)
        near += strips[4] * turned(sx, 1, 0) + strips[5] * turned(sx, -1, 0)
        step = add * (sb - sx + near)
        sd = step if sd is None else step + keep * sd
        sx = sx + sd
        kept.append(ends_of(sx))
    place_in = end_lanes(2, 1)
    place_in = jnp.concatenate([place_in, place_in], axis=0)
    for s, pair in enumerate(kept):
        start = (1 + s) * rows // LANES * LANES
        stop = -(-(count - 1 - s) * rows // LANES) * LANES
        ends[start:stop, s * LANES : (s + 1) * LANES] = dot(
            jnp.concatenate(parts(pair[:, start:stop]), axis=0), place_in, 0, 0)

    piece = 24
    first, last = iota((piece, LANES), 1) == 0, iota((piece, LANES), 1) == LANES - 1
    blank = jnp.zeros((EDGE, LANES), F32)

    @pl.loop(0, count)
    def _(k):
        for ref in (xa, xb):
            ref[k, pl.ds(0, EDGE)] = blank
            ref[k, pl.ds(rows + EDGE, EDGE)] = blank

    for s, (keep, add) in enumerate(factors):
        src, into = (xm if s == 0 else (xa if s % 2 else xb)), (xb if s % 2 else xa)

        @pl.loop(1 + s, count - 1 - s)
        def _(k):
            for at in range(0, rows, piece):
                here, to = pl.ds(EDGE + at, piece), pl.ds(at, piece)
                x = src[k, here]
                end = ends[pl.ds(pl.multiple_of(k * rows + at, 8), piece), s * LANES : (s + 1) * LANES]
                e = jnp.where(last, end, turned(x, -1, 1))
                w = jnp.where(first, end, turned(x, 1, 1))
                near = wz[k, to] * src[k + 1, here] + wz[k - 1, to] * src[k - 1, here]
                near += wx[k, to] * src[k, pl.ds(EDGE + at + 1, piece)]
                near += wxl[k, to] * src[k, pl.ds(EDGE + at - 1, piece)]
                near += wy[k, to] * e + wyw[k, to] * w
                if s == 0:
                    rhs = b0[k, to] + full[k, to] * inv[k, to]
                    b[k, to] = rhs
                else:
                    rhs = b[k, to]
                step = add * (rhs - x + inv[k, to] * near)
                if s > 0:
                    step = step + keep * d[k, to]
                if s < SWEEPS - 1:
                    d[k, to] = step
                into[k, here] = x + step

    final = xb if SWEEPS % 2 == 0 else xa
    for k in range(4):
        out[pl.ds(k * LANES, LANES), :] = final[SWEEPS + k, pl.ds(2 * EDGE, LANES)]
    scale = 1.0
    for _, add in factors:
        scale = scale * add
    tile = pl.ds(EDGE, LANES)
    for i, (start, way) in enumerate(((1, 1), (count - 2, -1))):
        gain = scale * inv[start, tile]
        for j in range(1, SWEEPS):
            at = start + way * j
            gain = gain * inv[at, tile] * wz[at - 1 if way > 0 else at, tile]
        pull[pl.ds(i * LANES, LANES), :] = gain


def reply_kernel(x, pull, low2, high2, hot, out, replies):
    n = out.shape[0]
    first, last = pl.ds(0, LANES), pl.ds(n - LANES, LANES)
    out[...] = x[...]
    out[first, :] = x[first, :] + pull[pl.ds(0, LANES), :] * low2[...]
    out[last, :] = x[last, :] + pull[pl.ds(LANES, LANES), :] * high2[...]
    replies[...] = pick_rows(hot[...], out[...])


def final_kernel(returned, hot, gain, mob, mobility, ionization):
    back = pick_rows(hot[...], returned[...])
    mobility[...] = mob[...] * jnp.exp(-0.7 * back)
    ionization[...] = jnp.exp(gain[...] * (1.0 + 0.3 * back))


def shifted(v, axis, by):
    count = lax.axis_size(axis)
    pairs = [(i, i + by) for i in range(count) if 0 <= i + by < count]
    return lax.ppermute(v, axis, pairs) if pairs else jnp.zeros_like(v)


def exchanged(v):
    lines = v.reshape(v.shape[0], 1, v.shape[1])
    return lax.all_to_all(lines, ("gx", "gy"), split_axis=0, concat_axis=0, tiled=True).reshape(v.shape)


def per_device(
    efield, density, mobility_prev, thermal_prev, owner, block, live, material,
    mat_conductivity, mat_softening, mat_capacity,
):
    layers, xcells, width = density.shape
    n = layers * xcells
    peers = lax.axis_size("gx") * lax.axis_size("gy")
    slots = max(2, 2 * n // peers)
    line = peers * (slots + 1)
    flat = lambda a: a.reshape(n, width)
    ef = efield.reshape(3, n, width)
    den, mob, x0 = flat(density), flat(mobility_prev), flat(thermal_prev)
    own, blk, liv = owner.reshape(1, n), block.reshape(1, n), live.reshape(1, n)
    mat = material.reshape(layers, xcells)
    sized = lambda *s: (s, F32)

    given = [ef, den, mob, own, blk, liv]
    [sent] = call(
        functools.partial(dispatch_kernel, peers, slots), [sized(line, width)], given, "dispatch", flops=10**8, hbm=True, limit=60,
        scratch=[pltpu.VMEM(a.shape, a.dtype) for a in given] + [pltpu.SemaphoreType.DMA((len(given),))])
    received = exchanged(sent)

    far = SWEEPS - layers
    count = layers + 2 * SWEEPS
    rows = xcells + 2 * EDGE
    total = count * rows
    aside = sized(far * xcells + EDGE, width)
    near, up, down = call(
        functools.partial(start_z_kernel, far), [sized(n + EDGE, width), aside, aside], [x0, mat], "start_z")
    low, high = shifted(near, "gz", 1), shifted(near, "gz", -1)
    low2, high2 = shifted(up, "gz", 2), shifted(down, "gz", -2)
    gain, dest = call(functools.partial(after_kernel, slots), [sized(n, width), ((n, peers * slots), BF16)], [ef, own], "gain")
    received, low, high, low2, high2, gain, dest = lax.optimization_barrier(
        (received, low, high, low2, high2, gain, dest))
    edge = sized(count * (EDGE + 1), width)
    xz, mats, start_low, start_high = call(
        functools.partial(start_x_kernel, far), [sized(count, xcells, width), sized(count, width), edge, edge],
        [low2, low, near, high, high2], "start_x")

    source, first, last = call(
        functools.partial(combine_kernel, peers, slots), [sized(n, width)] + [sized(xcells, width)] * 2,
        [received], "combine", flops=10**8)
    [ids] = call(functools.partial(ids_kernel, peers, slots), [((peers * slots, n), BF16)], [received], "ids")
    low, high = shifted(source, "gz", 1), shifted(source, "gz", -1)
    low, high, start_low, start_high, ids = lax.optimization_barrier((low, high, start_low, start_high, ids))
    edge = sized(count * (EDGE + 1) + 3 * layers * EDGE, width)
    xlow, xhigh = call(pack_x_kernel, [edge, edge], [low, source, high, start_low, start_high], "pack_x")
    before, after = shifted(xhigh, "gx", 1), shifted(xlow, "gx", -1)
    tall, tile, flat_edge = sized(count, rows + 2 * EDGE, width), sized(count, rows, width), sized(2 * EDGE, total)
    xm, full, sides, heat_sides, flat_mat, ylow, yhigh = call(
        pack_y_kernel, [tall, tile, flat_edge, flat_edge, sized(EDGE, total), flat_edge, flat_edge],
        [xz, mats, low, source, high, after, before], "pack_y")
    ylow, yhigh, first, last = lax.optimization_barrier((ylow, yhigh, first, last))
    before, after = shifted(yhigh, "gy", 1), shifted(ylow, "gy", -1)
    low2, high2 = shifted(last, "gz", 2), shifted(first, "gz", -2)
    weights = call(
        weights_kernel, [tile] * 7 + [sized(9, 4 * EDGE, total)],
        [mat_conductivity, mat_softening, mat_capacity, xm, sides, flat_mat, before, after], "weights",
        scratch=[pltpu.VMEM((count, rows + 2 * EDGE, width), F32), pltpu.VMEM((total, 3 * width), F32),
                 pltpu.VMEM((total, width), F32)],
        limit=32, flops=10**9, smem=(0, 1, 2))
    x, pull = call(
        sweep_kernel, [sized(n, width), sized(2 * xcells, width)],
        [xm] + list(weights) + [full, heat_sides, before, after], "sweeps",
        scratch=[pltpu.VMEM((count, rows, width), F32)] * 2 + [pltpu.VMEM((count, rows + 2 * EDGE, width), F32)] * 2
        + [pltpu.VMEM((total, SWEEPS * width), F32)],
        limit=36, flops=10**8)
    x, pull, low2, high2 = lax.optimization_barrier((x, pull, low2, high2))
    x, replies = call(
        reply_kernel, [sized(n, width), sized(peers * slots, width)], [x, pull, low2, high2, ids], "reply", flops=10**8)
    returned = exchanged(replies)
    mobility, ionization = call(final_kernel, [sized(n, width)] * 2, [returned, dest, gain, mob], "finish", flops=10**8)
    shape = density.shape
    return x.reshape(shape), mobility.reshape(shape), ionization.reshape(shape)


def solution(mesh):
    tile = P("gz", "gx", "gy")
    rows = P("gz", "gx", "gy", None)
    placed = (
        P(None, "gz", "gx", "gy"), tile, tile, tile,
        P("gz", "gx", "gy", None, None), rows, rows, rows, P(), P(), P(),
    )
    return jax.shard_map(
        per_device, mesh=mesh, in_specs=placed, out_specs=(tile, tile, tile), check_vma=False
    )
```

```python
import functools

import jax
import jax.numpy as jnp
from jax import lax
from jax.experimental import pallas as pl
from jax.experimental.pallas import tpu as pltpu
from jax.sharding import PartitionSpec as P

SWEEPS = 6
THETA = 1.01
DELTA = 0.99
LANES = 128
EDGE = 8
F32 = jnp.float32
BF16 = jnp.bfloat16
I32 = jnp.int32


def steps():
    sigma = THETA / DELTA
    rho = 1.0 / sigma
    found = [(0.0, 1.0 / THETA)]
    for _ in range(SWEEPS - 1):
        rho_new = 1.0 / (2.0 * sigma - rho)
        found.append((rho_new * rho, 2.0 * rho_new / DELTA))
        rho = rho_new
    return found


def iota(shape, dim):
    return lax.broadcasted_iota(I32, shape, dim)


def dot(a, b, ca, cb):
    return lax.dot_general(a, b, (((ca,), (cb,)), ((), ())), preferred_element_type=F32)


def parts(v):
    high = v.astype(BF16)
    return high, (v - high.astype(F32)).astype(BF16)


def pick_rows(hot, rows):
    high, low = parts(rows)
    got = dot(hot, jnp.concatenate([high, low], axis=1), 1, 0)
    width = rows.shape[1]
    return got[:, :width] + got[:, width:]


def column(row):
    same = iota((LANES, LANES), 0) == iota((LANES, LANES), 1)
    found = []
    for at in range(0, row.shape[1], LANES):
        piece = jnp.broadcast_to(row[:, at : at + LANES], (LANES, LANES))
        found.append(jnp.sum(jnp.where(same, piece, 0), axis=1, keepdims=True))
    return jnp.concatenate(found, axis=0)


def hot_of(cond):
    return jnp.where(cond, F32(1.0), F32(0.0)).astype(BF16)


def edge_lanes():
    r, y = iota((2 * EDGE, LANES), 0), iota((2 * EDGE, LANES), 1)
    return hot_of(y == jnp.where(r < EDGE, r, r + LANES - 2 * EDGE))


def call(kernel, outs, ins, name, scratch=(), limit=32, flops=0, smem=(), hbm=False):
    bytes_of = lambda a: a.size * a.dtype.itemsize
    return pl.pallas_call(
        kernel,
        out_shape=[jax.ShapeDtypeStruct(s, t) for s, t in outs],
        in_specs=[
            pl.BlockSpec(memory_space=pltpu.SMEM if i in smem else pltpu.HBM if hbm else pltpu.VMEM)
            for i in range(len(ins))
        ],
        out_specs=[pl.BlockSpec(memory_space=pltpu.VMEM) for _ in outs],
        scratch_shapes=list(scratch),
        compiler_params=pltpu.CompilerParams(vmem_limit_bytes=limit << 20),
        cost_estimate=pl.CostEstimate(
            flops=flops,
            bytes_accessed=sum(bytes_of(a) for a in ins)
            + sum(jax.ShapeDtypeStruct(s, t).size * 4 for s, t in outs),
            transcendentals=0,
        ),
        name=name,
    )(*ins)


def dispatch_kernel(peers, slots, *refs):
    far, out, near, sems = refs[:6], refs[6], refs[7:13], refs[13]
    copies = [pltpu.make_async_copy(a, b, sems.at[i]) for i, (a, b) in enumerate(zip(far, near))]
    for copy in copies[3:] + copies[:3]:
        copy.start()
    for copy in copies[3:]:
        copy.wait()
    ef, den, mob, owner, block, live = near
    n = owner.shape[1]
    own = owner[...]
    own_col = column(own)
    pos = jnp.zeros((1, n), I32)
    for at in range(0, n, LANES):
        r = iota((LANES, n), 0) + at
        earlier = (own_col[at : at + LANES] == own) & (r < iota((LANES, n), 1))
        pos = pos + jnp.sum(jnp.where(earlier, 1, 0), axis=0, keepdims=True)
    dest = own * (slots + 1) + pos
    hot = hot_of(iota((peers * (slots + 1), n), 0) == dest)
    named = hot_of(iota((peers, n), 0) == own)
    at_slot = iota((LANES, n), 0) == pos
    code = block[...] + 1
    high = jnp.where(at_slot, code // 32, 0).astype(F32).astype(BF16)
    low = jnp.where(at_slot, code % 32, 0).astype(F32).astype(BF16)
    labels = dot(named, high, 1, 1) * 32.0 + dot(named, low, 1, 1)
    live_col = column(live[...])
    for copy in copies[:3]:
        copy.wait()
    esq = ef[0] * ef[0] + ef[1] * ef[1] + ef[2] * ef[2]
    heat = 0.2 * den[...] * mob[...] * esq
    heat = jnp.where(iota(heat.shape, 1) < live_col, heat, F32(0.0))
    out[...] = pick_rows(hot, heat)
    out[pl.ds(slots, peers, stride=slots + 1), :] = labels


def after_kernel(slots, ef, owner, gain, hot):
    n = owner.shape[1]
    esq = ef[0] * ef[0] + ef[1] * ef[1] + ef[2] * ef[2]
    gain[...] = -2.0 * lax.rsqrt(esq + 1.0)
    own = owner[...]
    own_col = column(own)
    for at in range(0, n, LANES):
        r = iota((LANES, n), 0) + at
        piece = own_col[at : at + LANES]
        earlier = (piece == own) & (iota((LANES, n), 1) < r)
        pos = jnp.sum(jnp.where(earlier, 1, 0), axis=1, keepdims=True)
        size = (LANES, hot.shape[1])
        hot[pl.ds(at, LANES), :] = hot_of(jnp.broadcast_to(piece * slots + pos, size) == iota(size, 1))


def labels_of(received, peers, slots):
    got = received[pl.ds(slots, peers, stride=slots + 1), :]
    high = jnp.floor(got * (1.0 / 32.0))
    return high.astype(BF16), (got - 32.0 * high).astype(BF16)


def combine_kernel(peers, slots, received, source, first, last):
    n = source.shape[0]
    total = received.shape[0]
    high, low = labels_of(received, peers, slots)
    j = iota((LANES, total), 1)
    spread = hot_of(iota((LANES, total), 0) == j - (slots + 1) * lax.div(j, slots + 1))
    named = dot(high, spread, 1, 0) * 32.0 + dot(low, spread, 1, 0)
    mine = iota((peers, total), 0) == lax.div(iota((peers, total), 1), slots + 1)
    ids = jnp.sum(jnp.where(mine, named, 0.0), axis=0, keepdims=True).astype(I32)
    picks = hot_of(iota((n, total), 0) + 1 == ids)
    source[...] = pick_rows(picks, received[...])
    first[...] = source[pl.ds(0, LANES), :]
    last[...] = source[pl.ds(n - LANES, LANES), :]


def ids_kernel(peers, slots, received, hot):
    total = peers * slots
    high, low = labels_of(received, peers, slots)
    own = hot_of(lax.div(iota((total, peers), 0), slots) == iota((total, peers), 1))
    named = dot(own, high, 1, 0) * 32.0 + dot(own, low, 1, 0)
    i = iota((total, LANES), 0)
    mine = iota((total, LANES), 1) == i - slots * lax.div(i, slots)
    found = jnp.sum(jnp.where(mine, named, 0.0), axis=1, keepdims=True) - 1.0
    hot[...] = hot_of(jnp.broadcast_to(found.astype(I32), hot.shape) == iota(hot.shape, 1))


def start_z_kernel(far, x0, material, near, up, down):
    layers, xcells = material.shape
    n = layers * xcells
    mat = (material[...] + 1).astype(F32)
    rows = far * xcells
    zeros = lambda k: jnp.zeros((k, LANES), F32)
    near[pl.ds(0, n), :] = x0[...]
    near[pl.ds(n, EDGE), :] = jnp.concatenate([mat, zeros(EDGE - layers)], axis=0)
    up[pl.ds(0, rows), :] = x0[pl.ds(n - rows, rows), :]
    up[pl.ds(rows, EDGE), :] = jnp.concatenate([mat[layers - far :], zeros(EDGE - far)], axis=0)
    down[pl.ds(0, rows), :] = x0[pl.ds(0, rows), :]
    down[pl.ds(rows, EDGE), :] = jnp.concatenate([mat[:far], zeros(EDGE - far)], axis=0)


def start_x_kernel(far, low2, low, own, high, high2, xz, mats, xlow, xhigh):
    found = [(low2, k) for k in range(far)]
    for ref in (low, own, high):
        found += [(ref, k) for k in range(4)]
    found += [(high2, k) for k in range(far)]
    count = len(found)
    for k, (ref, at) in enumerate(found):
        piece = ref[pl.ds(at * LANES, LANES), :]
        xz[k] = piece
        xlow[pl.ds(k * EDGE, EDGE), :] = piece[:EDGE]
        xhigh[pl.ds(k * EDGE, EDGE), :] = piece[LANES - EDGE :]
        mats[pl.ds(k, 1), :] = ref[pl.ds(ref.shape[0] - EDGE + at, 1), :]
    xlow[pl.ds(count * EDGE, count), :] = mats[...]
    xhigh[pl.ds(count * EDGE, count), :] = mats[...]


def pack_x_kernel(source, start_low, start_high, xlow, xhigh):
    top = start_low.shape[0]
    xlow[pl.ds(0, top), :] = start_low[...]
    xhigh[pl.ds(0, top), :] = start_high[...]
    for k in range(source.shape[0] // LANES):
        to = pl.ds(top + k * EDGE, EDGE)
        xlow[to, :] = source[pl.ds(k * LANES, EDGE), :]
        xhigh[to, :] = source[pl.ds((k + 1) * LANES - EDGE, EDGE), :]


def flat_sides(rows):
    high, low = parts(rows)
    edges = edge_lanes()
    return dot(edges, high, 1, 1) + dot(edges, low, 1, 1)


def pack_y_kernel(xz, mats, own, after, before, xm, full, sides, heat_sides, flat_mat, ylow, yhigh):
    count = xz.shape[0]
    blank = jnp.zeros((EDGE, LANES), F32)
    for k in range(count):
        part = pl.ds(k * EDGE, EDGE)
        xm[k, pl.ds(0, EDGE)] = blank
        xm[k, pl.ds(EDGE, EDGE)] = before[part, :]
        xm[k, pl.ds(2 * EDGE, LANES)] = xz[k]
        xm[k, pl.ds(LANES + 2 * EDGE, EDGE)] = after[part, :]
        xm[k, pl.ds(LANES + 3 * EDGE, EDGE)] = blank
    top = count * (EDGE + 1)
    size = LANES + 2 * EDGE
    layers = own.shape[0] // LANES
    for k in range(layers):
        part = pl.ds(top + k * EDGE, EDGE)
        full[pl.ds(k * size, EDGE), :] = before[part, :]
        full[pl.ds(k * size + EDGE, LANES), :] = own[pl.ds(k * LANES, LANES), :]
        full[pl.ds(k * size + EDGE + LANES, EDGE), :] = after[part, :]
    rows = LANES + 2 * EDGE
    total = count * rows
    found = flat_sides(xm[:, EDGE : EDGE + rows].reshape(total, LANES))
    sides[...] = found
    beside = pl.ds(count * EDGE, count)
    around = jnp.concatenate([before[beside, :], mats[...], after[beside, :]], axis=0)
    q = iota((1, total), 1)
    layer = lax.div(q, rows)
    row = q - layer * rows
    tile = jnp.where(row < EDGE, 0, jnp.where(row < LANES + EDGE, 1, 2))
    lane = row - EDGE + LANES * (1 - tile)
    spread = hot_of(iota((LANES, total), 0) == lane)
    named = dot(around.astype(BF16), spread, 1, 0)
    mine = iota((3 * count, total), 0) == tile * count + layer
    mat = jnp.sum(jnp.where(mine, named, 0.0), axis=0, keepdims=True)
    flat_mat[...] = jnp.broadcast_to(mat, (EDGE, total))
    heat_found = flat_sides(full[...])
    inner = pl.ds(0, layers * rows)
    beyond = jnp.zeros((EDGE, total), F32)
    heat_sides[...] = heat_found
    ylow[pl.ds(0, EDGE), :] = found[:EDGE]
    yhigh[pl.ds(0, EDGE), :] = found[EDGE:]
    ylow[pl.ds(EDGE, EDGE), :] = beyond
    yhigh[pl.ds(EDGE, EDGE), :] = beyond
    ylow[pl.ds(EDGE, EDGE), inner] = heat_found[:EDGE]
    yhigh[pl.ds(EDGE, EDGE), inner] = heat_found[EDGE:]
    ylow[pl.ds(2 * EDGE - 1, 1), :] = mat
    yhigh[pl.ds(EDGE, 1), :] = mat


def three_parts(v):
    high = v.astype(BF16)
    rest = v - high.astype(F32)
    mid = rest.astype(BF16)
    return high, mid, (rest - mid.astype(F32)).astype(BF16)


def ends_of(strip):
    return jnp.concatenate([strip[EDGE - 1 : EDGE], strip[3 * EDGE : 3 * EDGE + 1]], axis=0)


def end_lanes(depth, times):
    r, y = iota((depth, times * LANES), 0), iota((depth, times * LANES), 1)
    first = (r % 2 == 0) & (y == (r // 2) * LANES)
    last = (r % 2 == 1) & (y == (r // 2) * LANES + LANES - 1)
    return hot_of(first | last)


def turned(v, by, axis):
    return pltpu.roll(v, by % v.shape[axis], axis)


def strip_of(sides, before, after):
    return jnp.concatenate([before, sides, after], axis=0)


def pack_z_kernel(full, sides, before, after, out):
    n = full.shape[0]
    out[pl.ds(0, n), :] = full[...]
    strip = strip_of(sides[...], before[pl.ds(EDGE, EDGE), 0:n], after[pl.ds(EDGE, EDGE), 0:n])
    blocks = -(-n // LANES)
    strip = jnp.concatenate([strip, jnp.zeros((4 * EDGE, blocks * LANES - n), F32)], axis=1)
    for i in range(blocks):
        out[pl.ds(n + 4 * EDGE * i, 4 * EDGE), :] = strip[:, i * LANES : (i + 1) * LANES]


def weights_kernel(base, soft, heat, xm, sides, flat_mat, before, after, wz, wx, wy, wyw, inv, b0, strips, cond, cols, ends):
    count, rows = inv.shape[0], inv.shape[1]
    total = count * rows
    mat = jnp.concatenate(
        [flat_mat[0:1], before[pl.ds(EDGE, 1), :], after[pl.ds(2 * EDGE - 1, 1), :]], axis=0
    )
    tables = []
    for values in (base, soft, heat):
        found = jnp.zeros(mat.shape, F32)
        for m in range(values.shape[0]):
            found = jnp.where(mat == F32(m + 1), values[m], found)
        tables.append(found)
    own = [p for t in tables for p in three_parts(t[0:1])]
    r, y = iota((9, 3 * LANES), 0), iota((9, 3 * LANES), 1)
    cols[...] = dot(jnp.concatenate(own, axis=0), hot_of(lax.div(r, 3) == lax.div(y, LANES)), 0, 0)
    wide = lambda t, i: jnp.broadcast_to(t[i : i + 1], (EDGE, total))
    kb, ks, cf = (jnp.concatenate([wide(t, 1), wide(t, 0), wide(t, 0), wide(t, 2)], axis=0) for t in tables)
    sx = strip_of(sides[...], before[:EDGE], after[:EDGE])
    sc = kb / (1.0 + ks * sx)
    down = lambda by, axis: 0.5 * (sc + turned(sc, by, axis))
    around = [down(rows, 1), down(-rows, 1), down(1, 1), down(-1, 1), down(1, 0), down(-1, 0)]
    diag = cf
    for w in around:
        diag = diag + w
    si = jnp.where(cf > 0.0, 1.0 / diag, 0.0)
    for i, w in enumerate(around):
        strips[i] = w * si
    strips[6] = si
    strips[7] = cf * sx * si
    strips[8] = sx
    got = [dot(p, end_lanes(2, 1), 0, 0) for p in three_parts(ends_of(sc))]
    ends[...] = got[0] + got[1] + got[2]

    piece = 16
    blank = jnp.zeros((EDGE, LANES), F32)

    @pl.loop(0, count)
    def _(k):
        cond[k, pl.ds(0, EDGE)] = blank
        cond[k, pl.ds(rows + EDGE, EDGE)] = blank
        wx[k, pl.ds(0, EDGE)] = blank
        wx[k, pl.ds(rows + EDGE, EDGE)] = blank
        for at in range(0, rows, piece):
            part = pl.ds(pl.multiple_of(k * rows + at, 8), piece)
            x = xm[k, pl.ds(EDGE + at, piece)]
            cond[k, pl.ds(EDGE + at, piece)] = cols[part, 0:LANES] / (1.0 + cols[part, LANES : 2 * LANES] * x)

    first, last = iota((piece, LANES), 1) == 0, iota((piece, LANES), 1) == LANES - 1
    wz[0] = 0.5 * (cond[0, pl.ds(EDGE, rows)] + cond[1, pl.ds(EDGE, rows)])

    @pl.loop(1, count - 1)
    def _(k):
        for at in range(0, rows, piece):
            here = pl.ds(EDGE + at, piece)
            part = pl.ds(pl.multiple_of(k * rows + at, 8), piece)
            to = pl.ds(at, piece)
            c, end = cond[k, here], ends[part, :]
            up = 0.5 * (c + cond[k + 1, here])
            low = 0.5 * (c + cond[k - 1, here])
            right = 0.5 * (c + cond[k, pl.ds(EDGE + at + 1, piece)])
            left = 0.5 * (c + cond[k, pl.ds(EDGE + at - 1, piece)])
            e = 0.5 * (c + jnp.where(last, end, turned(c, -1, 1)))
            w = 0.5 * (c + jnp.where(first, end, turned(c, 1, 1)))
            cf = cols[part, 2 * LANES : 3 * LANES]
            diag = cf + up + low + right + left + e + w
            i = jnp.where(cf > 0.0, 1.0 / diag, 0.0)
            wz[k, to] = up
            wx[k, here] = right
            wy[k, to] = e
            wyw[k, to] = w
            inv[k, to] = i
            b0[k, to] = cf * xm[k, here] * i


def sweep_kernel(xm, wz, wx, wy, wyw, inv, b0, strips, low, own, high,
                 out, pull, full, b, d, xa, xb, ends):
    count, rows, _ = inv.shape
    total = count * rows
    factors = steps()

    layers = out.shape[0] // LANES
    n = layers * rows
    skip = (count - 3 * layers) // 2
    sb = jnp.zeros((4 * EDGE, total), F32)
    blocks = -(-n // LANES)
    blank = jnp.zeros((4 * EDGE, total - blocks * LANES), F32)
    for i, ref in enumerate((low, own, high)):
        start = skip + i * layers
        for k in range(layers):
            full[start + k] = ref[pl.ds(k * rows, rows), :]
        cells = [ref[pl.ds(n + 4 * EDGE * j, 4 * EDGE), :] for j in range(blocks)]
        sb = sb + turned(jnp.concatenate(cells + [blank], axis=1), start * rows, 1)
    for k in range(skip):
        full[k] = jnp.zeros((rows, LANES), F32)
        full[count - 1 - k] = jnp.zeros((rows, LANES), F32)
    sb = strips[7] + sb * strips[6]
    sx, sd = strips[8], None
    kept = [ends_of(sx)]
    for keep, add in factors[:-1]:
        near = strips[0] * turned(sx, rows, 1) + strips[1] * turned(sx, -rows, 1)
        near += strips[2] * turned(sx, 1, 1) + strips[3] * turned(sx, -1, 1)
        near += strips[4] * turned(sx, 1, 0) + strips[5] * turned(sx, -1, 0)
        step = add * (sb - sx + near)
        sd = step if sd is None else step + keep * sd
        sx = sx + sd
        kept.append(ends_of(sx))
    place_in = end_lanes(2, 1)
    place_in = jnp.concatenate([place_in, place_in], axis=0)
    for s, pair in enumerate(kept):
        start = (1 + s) * rows // LANES * LANES
        stop = -(-(count - 1 - s) * rows // LANES) * LANES
        ends[start:stop, s * LANES : (s + 1) * LANES] = dot(
            jnp.concatenate(parts(pair[:, start:stop]), axis=0), place_in, 0, 0)

    piece = 24
    first, last = iota((piece, LANES), 1) == 0, iota((piece, LANES), 1) == LANES - 1
    blank = jnp.zeros((EDGE, LANES), F32)

    @pl.loop(0, count)
    def _(k):
        for ref in (xa, xb):
            ref[k, pl.ds(0, EDGE)] = blank
            ref[k, pl.ds(rows + EDGE, EDGE)] = blank

    for s, (keep, add) in enumerate(factors):
        src, into = (xm if s == 0 else (xa if s % 2 else xb)), (xb if s % 2 else xa)

        @pl.loop(1 + s, count - 1 - s)
        def _(k):
            for at in range(0, rows, piece):
                here, to = pl.ds(EDGE + at, piece), pl.ds(at, piece)
                x = src[k, here]
                end = ends[pl.ds(pl.multiple_of(k * rows + at, 8), piece), s * LANES : (s + 1) * LANES]
                e = jnp.where(last, end, turned(x, -1, 1))
                w = jnp.where(first, end, turned(x, 1, 1))
                near = wz[k, to] * src[k + 1, here] + wz[k - 1, to] * src[k - 1, here]
                near += wx[k, here] * src[k, pl.ds(EDGE + at + 1, piece)]
                near += wx[k, pl.ds(EDGE + at - 1, piece)] * src[k, pl.ds(EDGE + at - 1, piece)]
                near += wy[k, to] * e + wyw[k, to] * w
                if s == 0:
                    rhs = b0[k, to] + full[k, to] * inv[k, to]
                    b[k, to] = rhs
                else:
                    rhs = b[k, to]
                step = add * (rhs - x + inv[k, to] * near)
                if s > 0:
                    step = step + keep * d[k, to]
                if s < SWEEPS - 1:
                    d[k, to] = step
                into[k, here] = x + step

    final = xb if SWEEPS % 2 == 0 else xa
    for k in range(4):
        out[pl.ds(k * LANES, LANES), :] = final[SWEEPS + k, pl.ds(2 * EDGE, LANES)]
    scale = 1.0
    for _, add in factors:
        scale = scale * add
    tile = pl.ds(EDGE, LANES)
    for i, (start, way) in enumerate(((1, 1), (count - 2, -1))):
        gain = scale * inv[start, tile]
        for j in range(1, SWEEPS):
            at = start + way * j
            gain = gain * inv[at, tile] * wz[at - 1 if way > 0 else at, tile]
        pull[pl.ds(i * LANES, LANES), :] = gain


def reply_kernel(x, pull, low2, high2, hot, out, replies):
    n = out.shape[0]
    first, last = pl.ds(0, LANES), pl.ds(n - LANES, LANES)
    out[...] = x[...]
    out[first, :] = x[first, :] + pull[pl.ds(0, LANES), :] * low2[...]
    out[last, :] = x[last, :] + pull[pl.ds(LANES, LANES), :] * high2[...]
    replies[...] = pick_rows(hot[...], out[...])


def final_kernel(returned, hot, gain, mob, mobility, ionization):
    back = pick_rows(hot[...], returned[...])
    mobility[...] = mob[...] * jnp.exp(-0.7 * back)
    ionization[...] = jnp.exp(gain[...] * (1.0 + 0.3 * back))


def shifted(v, axis, by):
    count = lax.axis_size(axis)
    pairs = [(i, i + by) for i in range(count) if 0 <= i + by < count]
    return lax.ppermute(v, axis, pairs) if pairs else jnp.zeros_like(v)


def exchanged(v):
    lines = v.reshape(v.shape[0], 1, v.shape[1])
    return lax.all_to_all(lines, ("gx", "gy"), split_axis=0, concat_axis=0, tiled=True).reshape(v.shape)


def per_device(
    efield, density, mobility_prev, thermal_prev, owner, block, live, material,
    mat_conductivity, mat_softening, mat_capacity,
):
    layers, xcells, width = density.shape
    n = layers * xcells
    peers = lax.axis_size("gx") * lax.axis_size("gy")
    slots = max(2, 2 * n // peers)
    line = peers * (slots + 1)
    flat = lambda a: a.reshape(n, width)
    ef = efield.reshape(3, n, width)
    den, mob, x0 = flat(density), flat(mobility_prev), flat(thermal_prev)
    own, blk, liv = owner.reshape(1, n), block.reshape(1, n), live.reshape(1, n)
    mat = material.reshape(layers, xcells)
    sized = lambda *s: (s, F32)

    given = [ef, den, mob, own, blk, liv]
    [sent] = call(
        functools.partial(dispatch_kernel, peers, slots), [sized(line, width)], given, "dispatch", flops=10**8, hbm=True, limit=60,
        scratch=[pltpu.VMEM(a.shape, a.dtype) for a in given] + [pltpu.SemaphoreType.DMA((len(given),))])
    received = exchanged(sent)

    far = SWEEPS - layers
    count = layers + 2 * SWEEPS
    rows = xcells + 2 * EDGE
    total = count * rows
    aside = sized(far * xcells + EDGE, width)
    near, up, down = call(
        functools.partial(start_z_kernel, far), [sized(n + EDGE, width), aside, aside], [x0, mat], "start_z")
    low, high = shifted(near, "gz", 1), shifted(near, "gz", -1)
    low2, high2 = shifted(up, "gz", 2), shifted(down, "gz", -2)
    gain, dest = call(functools.partial(after_kernel, slots), [sized(n, width), ((n, peers * slots), BF16)], [ef, own], "gain")
    edge = sized(count * (EDGE + 1), width)
    xz, mats, start_low, start_high = call(
        functools.partial(start_x_kernel, far), [sized(count, xcells, width), sized(count, width), edge, edge],
        [low2, low, near, high, high2], "start_x")
    received, start_low, start_high, gain, dest = lax.optimization_barrier(
        (received, start_low, start_high, gain, dest))

    source, first, last = call(
        functools.partial(combine_kernel, peers, slots), [sized(n, width)] + [sized(xcells, width)] * 2,
        [received], "combine", flops=10**8)
    [ids] = call(functools.partial(ids_kernel, peers, slots), [((peers * slots, n), BF16)], [received], "ids")
    edge = sized(count * (EDGE + 1) + layers * EDGE, width)
    xlow, xhigh = call(pack_x_kernel, [edge, edge], [source, start_low, start_high], "pack_x")
    before, after = shifted(xhigh, "gx", 1), shifted(xlow, "gx", -1)
    before, after, ids = lax.optimization_barrier((before, after, ids))
    tall, tile, flat_edge = sized(count, rows + 2 * EDGE, width), sized(count, rows, width), sized(2 * EDGE, total)
    inner = layers * rows
    xm, full, sides, heat_sides, flat_mat, ylow, yhigh = call(
        pack_y_kernel,
        [tall, sized(inner, width), flat_edge, sized(2 * EDGE, inner), sized(EDGE, total), flat_edge, flat_edge],
        [xz, mats, source, after, before], "pack_y")
    before, after = shifted(yhigh, "gy", 1), shifted(ylow, "gy", -1)
    blocks = -(-inner // LANES)
    [around] = call(
        pack_z_kernel, [sized(inner + 4 * EDGE * blocks, width)], [full, heat_sides, before, after], "pack_z")
    around, first, last = lax.optimization_barrier((around, first, last))
    low, high = shifted(around, "gz", 1), shifted(around, "gz", -1)
    low2, high2 = shifted(last, "gz", 2), shifted(first, "gz", -2)
    weights = call(
        weights_kernel, [tile, tall, tile, tile, tile, tile, sized(9, 4 * EDGE, total)],
        [mat_conductivity, mat_softening, mat_capacity, xm, sides, flat_mat, before, after], "weights",
        scratch=[pltpu.VMEM((count, rows + 2 * EDGE, width), F32), pltpu.VMEM((total, 3 * width), F32),
                 pltpu.VMEM((total, width), F32)],
        limit=32, flops=10**9, smem=(0, 1, 2))
    low, high, weights = lax.optimization_barrier((low, high, weights))
    x, pull = call(
        sweep_kernel, [sized(n, width), sized(2 * xcells, width)],
        [xm] + list(weights) + [low, around, high], "sweeps",
        scratch=[pltpu.VMEM((count, rows, width), F32)] * 3 + [pltpu.VMEM((count, rows + 2 * EDGE, width), F32)] * 2
        + [pltpu.VMEM((total, SWEEPS * width), F32)],
        limit=36, flops=10**8)
    x, pull, low2, high2 = lax.optimization_barrier((x, pull, low2, high2))
    x, replies = call(
        reply_kernel, [sized(n, width), sized(peers * slots, width)], [x, pull, low2, high2, ids], "reply", flops=10**8)
    returned = exchanged(replies)
    mobility, ionization = call(final_kernel, [sized(n, width)] * 2, [returned, dest, gain, mob], "finish", flops=10**8)
    shape = density.shape
    return x.reshape(shape), mobility.reshape(shape), ionization.reshape(shape)


def solution(mesh):
    tile = P("gz", "gx", "gy")
    rows = P("gz", "gx", "gy", None)
    placed = (
        P(None, "gz", "gx", "gy"), tile, tile, tile,
        P("gz", "gx", "gy", None, None), rows, rows, rows, P(), P(), P(),
    )
    return jax.shard_map(
        per_device, mesh=mesh, in_specs=placed, out_specs=(tile, tile, tile), check_vma=False
    )
```

```python
import functools

import jax
import jax.numpy as jnp
from jax import lax
from jax.experimental import pallas as pl
from jax.experimental.pallas import tpu as pltpu
from jax.sharding import PartitionSpec as P

SWEEPS = 6
THETA = 1.01
DELTA = 0.99
LANES = 128
EDGE = 8
F32 = jnp.float32
BF16 = jnp.bfloat16
I32 = jnp.int32


def steps():
    sigma = THETA / DELTA
    rho = 1.0 / sigma
    found = [(0.0, 1.0 / THETA)]
    for _ in range(SWEEPS - 1):
        rho_new = 1.0 / (2.0 * sigma - rho)
        found.append((rho_new * rho, 2.0 * rho_new / DELTA))
        rho = rho_new
    return found


def iota(shape, dim):
    return lax.broadcasted_iota(I32, shape, dim)


def dot(a, b, ca, cb):
    return lax.dot_general(a, b, (((ca,), (cb,)), ((), ())), preferred_element_type=F32)


def parts(v):
    high = v.astype(BF16)
    return high, (v - high.astype(F32)).astype(BF16)


def pick_rows(hot, rows):
    high, low = parts(rows)
    got = dot(hot, jnp.concatenate([high, low], axis=1), 1, 0)
    width = rows.shape[1]
    return got[:, :width] + got[:, width:]


def column(row):
    same = iota((LANES, LANES), 0) == iota((LANES, LANES), 1)
    found = []
    for at in range(0, row.shape[1], LANES):
        piece = jnp.broadcast_to(row[:, at : at + LANES], (LANES, LANES))
        found.append(jnp.sum(jnp.where(same, piece, 0), axis=1, keepdims=True))
    return jnp.concatenate(found, axis=0)


def hot_of(cond):
    return jnp.where(cond, F32(1.0), F32(0.0)).astype(BF16)


def edge_lanes():
    r, y = iota((2 * EDGE, LANES), 0), iota((2 * EDGE, LANES), 1)
    return hot_of(y == jnp.where(r < EDGE, r, r + LANES - 2 * EDGE))


def call(kernel, outs, ins, name, scratch=(), limit=32, flops=0, smem=(), hbm=False):
    bytes_of = lambda a: a.size * a.dtype.itemsize
    return pl.pallas_call(
        kernel,
        out_shape=[jax.ShapeDtypeStruct(s, t) for s, t in outs],
        in_specs=[
            pl.BlockSpec(memory_space=pltpu.SMEM if i in smem else pltpu.HBM if hbm else pltpu.VMEM)
            for i in range(len(ins))
        ],
        out_specs=[pl.BlockSpec(memory_space=pltpu.VMEM) for _ in outs],
        scratch_shapes=list(scratch),
        compiler_params=pltpu.CompilerParams(vmem_limit_bytes=limit << 20),
        cost_estimate=pl.CostEstimate(
            flops=flops,
            bytes_accessed=sum(bytes_of(a) for a in ins)
            + sum(jax.ShapeDtypeStruct(s, t).size * 4 for s, t in outs),
            transcendentals=0,
        ),
        name=name,
    )(*ins)


def dispatch_kernel(peers, slots, *refs):
    far, out, near, sems = refs[:6], refs[6], refs[7:13], refs[13]
    copies = [pltpu.make_async_copy(a, b, sems.at[i]) for i, (a, b) in enumerate(zip(far, near))]
    for copy in copies[3:] + copies[:3]:
        copy.start()
    for copy in copies[3:]:
        copy.wait()
    ef, den, mob, owner, block, live = near
    n = owner.shape[1]
    own = owner[...]
    own_col = column(own)
    pos = jnp.zeros((1, n), I32)
    for at in range(0, n, LANES):
        r = iota((LANES, n), 0) + at
        earlier = (own_col[at : at + LANES] == own) & (r < iota((LANES, n), 1))
        pos = pos + jnp.sum(jnp.where(earlier, 1, 0), axis=0, keepdims=True)
    dest = own * (slots + 1) + pos
    hot = hot_of(iota((peers * (slots + 1), n), 0) == dest)
    named = hot_of(iota((peers, n), 0) == own)
    at_slot = iota((LANES, n), 0) == pos
    code = block[...] + 1
    high = jnp.where(at_slot, code // 32, 0).astype(F32).astype(BF16)
    low = jnp.where(at_slot, code % 32, 0).astype(F32).astype(BF16)
    labels = dot(named, high, 1, 1) * 32.0 + dot(named, low, 1, 1)
    live_col = column(live[...])
    for copy in copies[:3]:
        copy.wait()
    esq = ef[0] * ef[0] + ef[1] * ef[1] + ef[2] * ef[2]
    heat = 0.2 * den[...] * mob[...] * esq
    heat = jnp.where(iota(heat.shape, 1) < live_col, heat, F32(0.0))
    out[...] = pick_rows(hot, heat)
    out[pl.ds(slots, peers, stride=slots + 1), :] = labels


def after_kernel(slots, ef, owner, gain, hot):
    n = owner.shape[1]
    esq = ef[0] * ef[0] + ef[1] * ef[1] + ef[2] * ef[2]
    gain[...] = -2.0 * lax.rsqrt(esq + 1.0)
    own = owner[...]
    own_col = column(own)
    for at in range(0, n, LANES):
        r = iota((LANES, n), 0) + at
        piece = own_col[at : at + LANES]
        earlier = (piece == own) & (iota((LANES, n), 1) < r)
        pos = jnp.sum(jnp.where(earlier, 1, 0), axis=1, keepdims=True)
        size = (LANES, hot.shape[1])
        hot[pl.ds(at, LANES), :] = hot_of(jnp.broadcast_to(piece * slots + pos, size) == iota(size, 1))


def labels_of(received, peers, slots):
    got = received[pl.ds(slots, peers, stride=slots + 1), :]
    high = jnp.floor(got * (1.0 / 32.0))
    return high.astype(BF16), (got - 32.0 * high).astype(BF16)


def combine_kernel(peers, slots, received, source, first, last):
    n = source.shape[0]
    total = received.shape[0]
    high, low = labels_of(received, peers, slots)
    j = iota((LANES, total), 1)
    spread = hot_of(iota((LANES, total), 0) == j - (slots + 1) * lax.div(j, slots + 1))
    named = dot(high, spread, 1, 0) * 32.0 + dot(low, spread, 1, 0)
    mine = iota((peers, total), 0) == lax.div(iota((peers, total), 1), slots + 1)
    ids = jnp.sum(jnp.where(mine, named, 0.0), axis=0, keepdims=True).astype(I32)
    picks = hot_of(iota((n, total), 0) + 1 == ids)
    source[...] = pick_rows(picks, received[...])
    first[...] = source[pl.ds(0, LANES), :]
    last[...] = source[pl.ds(n - LANES, LANES), :]


def ids_kernel(peers, slots, received, hot):
    total = peers * slots
    high, low = labels_of(received, peers, slots)
    own = hot_of(lax.div(iota((total, peers), 0), slots) == iota((total, peers), 1))
    named = dot(own, high, 1, 0) * 32.0 + dot(own, low, 1, 0)
    i = iota((total, LANES), 0)
    mine = iota((total, LANES), 1) == i - slots * lax.div(i, slots)
    found = jnp.sum(jnp.where(mine, named, 0.0), axis=1, keepdims=True) - 1.0
    hot[...] = hot_of(jnp.broadcast_to(found.astype(I32), hot.shape) == iota(hot.shape, 1))


def start_z_kernel(far, x0, material, near, up, down):
    layers, xcells = material.shape
    n = layers * xcells
    mat = (material[...] + 1).astype(F32)
    rows = far * xcells
    zeros = lambda k: jnp.zeros((k, LANES), F32)
    near[pl.ds(0, n), :] = x0[...]
    near[pl.ds(n, EDGE), :] = jnp.concatenate([mat, zeros(EDGE - layers)], axis=0)
    up[pl.ds(0, rows), :] = x0[pl.ds(n - rows, rows), :]
    up[pl.ds(rows, EDGE), :] = jnp.concatenate([mat[layers - far :], zeros(EDGE - far)], axis=0)
    down[pl.ds(0, rows), :] = x0[pl.ds(0, rows), :]
    down[pl.ds(rows, EDGE), :] = jnp.concatenate([mat[:far], zeros(EDGE - far)], axis=0)


def start_x_kernel(far, low2, low, own, high, high2, xz, mats, xlow, xhigh):
    found = [(low2, k) for k in range(far)]
    for ref in (low, own, high):
        found += [(ref, k) for k in range(4)]
    found += [(high2, k) for k in range(far)]
    count = len(found)
    for k, (ref, at) in enumerate(found):
        piece = ref[pl.ds(at * LANES, LANES), :]
        xz[k] = piece
        xlow[pl.ds(k * EDGE, EDGE), :] = piece[:EDGE]
        xhigh[pl.ds(k * EDGE, EDGE), :] = piece[LANES - EDGE :]
        mats[pl.ds(k, 1), :] = ref[pl.ds(ref.shape[0] - EDGE + at, 1), :]
    xlow[pl.ds(count * EDGE, count), :] = mats[...]
    xhigh[pl.ds(count * EDGE, count), :] = mats[...]


def pack_x_kernel(source, start_low, start_high, xlow, xhigh):
    top = start_low.shape[0]
    xlow[pl.ds(0, top), :] = start_low[...]
    xhigh[pl.ds(0, top), :] = start_high[...]
    for k in range(source.shape[0] // LANES):
        to = pl.ds(top + k * EDGE, EDGE)
        xlow[to, :] = source[pl.ds(k * LANES, EDGE), :]
        xhigh[to, :] = source[pl.ds((k + 1) * LANES - EDGE, EDGE), :]


def flat_sides(rows):
    high, low = parts(rows)
    edges = edge_lanes()
    return dot(edges, high, 1, 1) + dot(edges, low, 1, 1)


def pack_y_kernel(xz, mats, own, after, before, xm, full, sides, heat_sides, flat_mat, ylow, yhigh):
    count = xz.shape[0]
    blank = jnp.zeros((EDGE, LANES), F32)
    for k in range(count):
        part = pl.ds(k * EDGE, EDGE)
        xm[k, pl.ds(0, EDGE)] = blank
        xm[k, pl.ds(EDGE, EDGE)] = before[part, :]
        xm[k, pl.ds(2 * EDGE, LANES)] = xz[k]
        xm[k, pl.ds(LANES + 2 * EDGE, EDGE)] = after[part, :]
        xm[k, pl.ds(LANES + 3 * EDGE, EDGE)] = blank
    top = count * (EDGE + 1)
    size = LANES + 2 * EDGE
    layers = own.shape[0] // LANES
    for k in range(layers):
        part = pl.ds(top + k * EDGE, EDGE)
        full[pl.ds(k * size, EDGE), :] = before[part, :]
        full[pl.ds(k * size + EDGE, LANES), :] = own[pl.ds(k * LANES, LANES), :]
        full[pl.ds(k * size + EDGE + LANES, EDGE), :] = after[part, :]
    rows = LANES + 2 * EDGE
    total = count * rows
    found = flat_sides(xm[:, EDGE : EDGE + rows].reshape(total, LANES))
    sides[...] = found
    beside = pl.ds(count * EDGE, count)
    around = jnp.concatenate([before[beside, :], mats[...], after[beside, :]], axis=0)
    q = iota((1, total), 1)
    layer = lax.div(q, rows)
    row = q - layer * rows
    tile = jnp.where(row < EDGE, 0, jnp.where(row < LANES + EDGE, 1, 2))
    lane = row - EDGE + LANES * (1 - tile)
    spread = hot_of(iota((LANES, total), 0) == lane)
    named = dot(around.astype(BF16), spread, 1, 0)
    mine = iota((3 * count, total), 0) == tile * count + layer
    mat = jnp.sum(jnp.where(mine, named, 0.0), axis=0, keepdims=True)
    flat_mat[...] = jnp.broadcast_to(mat, (EDGE, total))
    heat_found = flat_sides(full[...])
    inner = pl.ds(0, layers * rows)
    beyond = jnp.zeros((EDGE, total), F32)
    heat_sides[...] = heat_found
    ylow[pl.ds(0, EDGE), :] = found[:EDGE]
    yhigh[pl.ds(0, EDGE), :] = found[EDGE:]
    ylow[pl.ds(EDGE, EDGE), :] = beyond
    yhigh[pl.ds(EDGE, EDGE), :] = beyond
    ylow[pl.ds(EDGE, EDGE), inner] = heat_found[:EDGE]
    yhigh[pl.ds(EDGE, EDGE), inner] = heat_found[EDGE:]
    ylow[pl.ds(2 * EDGE - 1, 1), :] = mat
    yhigh[pl.ds(EDGE, 1), :] = mat


def three_parts(v):
    high = v.astype(BF16)
    rest = v - high.astype(F32)
    mid = rest.astype(BF16)
    return high, mid, (rest - mid.astype(F32)).astype(BF16)


def ends_of(strip):
    return jnp.concatenate([strip[EDGE - 1 : EDGE], strip[3 * EDGE : 3 * EDGE + 1]], axis=0)


def end_lanes(depth, times):
    r, y = iota((depth, times * LANES), 0), iota((depth, times * LANES), 1)
    first = (r % 2 == 0) & (y == (r // 2) * LANES)
    last = (r % 2 == 1) & (y == (r // 2) * LANES + LANES - 1)
    return hot_of(first | last)


def turned(v, by, axis):
    return pltpu.roll(v, by % v.shape[axis], axis)


def strip_of(sides, before, after):
    return jnp.concatenate([before, sides, after], axis=0)


def pack_z_kernel(full, sides, before, after, out):
    n = full.shape[0]
    out[pl.ds(0, n), :] = full[...]
    strip = strip_of(sides[...], before[pl.ds(EDGE, EDGE), 0:n], after[pl.ds(EDGE, EDGE), 0:n])
    blocks = -(-n // LANES)
    strip = jnp.concatenate([strip, jnp.zeros((4 * EDGE, blocks * LANES - n), F32)], axis=1)
    for i in range(blocks):
        out[pl.ds(n + 4 * EDGE * i, 4 * EDGE), :] = strip[:, i * LANES : (i + 1) * LANES]


def weights_kernel(base, soft, heat, xm, sides, flat_mat, before, after, wz, wx, wy, wyw, inv, b0, strips, cond, cols, ends):
    count, rows = inv.shape[0], inv.shape[1]
    total = count * rows
    mat = jnp.concatenate(
        [flat_mat[0:1], before[pl.ds(EDGE, 1), :], after[pl.ds(2 * EDGE - 1, 1), :]], axis=0
    )
    tables = []
    for values in (base, soft, heat):
        found = jnp.zeros(mat.shape, F32)
        for m in range(values.shape[0]):
            found = jnp.where(mat == F32(m + 1), values[m], found)
        tables.append(found)
    own = [p for t in tables for p in three_parts(t[0:1])]
    r, y = iota((9, 3 * LANES), 0), iota((9, 3 * LANES), 1)
    cols[...] = dot(jnp.concatenate(own, axis=0), hot_of(lax.div(r, 3) == lax.div(y, LANES)), 0, 0)
    wide = lambda t, i: jnp.broadcast_to(t[i : i + 1], (EDGE, total))
    kb, ks, cf = (jnp.concatenate([wide(t, 1), wide(t, 0), wide(t, 0), wide(t, 2)], axis=0) for t in tables)
    sx = strip_of(sides[...], before[:EDGE], after[:EDGE])
    sc = kb / (1.0 + ks * sx)
    down = lambda by, axis: 0.5 * (sc + turned(sc, by, axis))
    around = [down(rows, 1), down(-rows, 1), down(1, 1), down(-1, 1), down(1, 0), down(-1, 0)]
    diag = cf
    for w in around:
        diag = diag + w
    si = jnp.where(cf > 0.0, 1.0 / diag, 0.0)
    for i, w in enumerate(around):
        strips[i] = w * si
    strips[6] = si
    strips[7] = cf * sx * si
    strips[8] = sx
    got = [dot(p, end_lanes(2, 1), 0, 0) for p in three_parts(ends_of(sc))]
    ends[...] = got[0] + got[1] + got[2]

    piece = 16
    blank = jnp.zeros((EDGE, LANES), F32)

    @pl.loop(0, count)
    def _(k):
        cond[k, pl.ds(0, EDGE)] = blank
        cond[k, pl.ds(rows + EDGE, EDGE)] = blank
        wx[k, pl.ds(0, EDGE)] = blank
        wx[k, pl.ds(rows + EDGE, EDGE)] = blank
        for at in range(0, rows, piece):
            part = pl.ds(pl.multiple_of(k * rows + at, 8), piece)
            x = xm[k, pl.ds(EDGE + at, piece)]
            cond[k, pl.ds(EDGE + at, piece)] = cols[part, 0:LANES] / (1.0 + cols[part, LANES : 2 * LANES] * x)

    first, last = iota((piece, LANES), 1) == 0, iota((piece, LANES), 1) == LANES - 1
    wz[0] = 0.5 * (cond[0, pl.ds(EDGE, rows)] + cond[1, pl.ds(EDGE, rows)])

    @pl.loop(1, count - 1)
    def _(k):
        for at in range(0, rows, piece):
            here = pl.ds(EDGE + at, piece)
            part = pl.ds(pl.multiple_of(k * rows + at, 8), piece)
            to = pl.ds(at, piece)
            c, end = cond[k, here], ends[part, :]
            up = 0.5 * (c + cond[k + 1, here])
            low = 0.5 * (c + cond[k - 1, here])
            right = 0.5 * (c + cond[k, pl.ds(EDGE + at + 1, piece)])
            left = 0.5 * (c + cond[k, pl.ds(EDGE + at - 1, piece)])
            e = 0.5 * (c + jnp.where(last, end, turned(c, -1, 1)))
            w = 0.5 * (c + jnp.where(first, end, turned(c, 1, 1)))
            cf = cols[part, 2 * LANES : 3 * LANES]
            diag = cf + up + low + right + left + e + w
            i = jnp.where(cf > 0.0, 1.0 / diag, 0.0)
            wz[k, to] = up
            wx[k, here] = right
            wy[k, to] = e
            wyw[k, to] = w
            inv[k, to] = i
            b0[k, to] = cf * xm[k, here] * i


def sweep_kernel(xm, wz, wx, wy, wyw, inv, b0, strips, low, own, high,
                 out, pull, full, b, d, xa, xb, ends):
    count, rows, _ = inv.shape
    total = count * rows
    factors = steps()

    layers = out.shape[0] // LANES
    n = layers * rows
    skip = (count - 3 * layers) // 2
    sb = jnp.zeros((4 * EDGE, total), F32)
    blocks = -(-n // LANES)
    blank = jnp.zeros((4 * EDGE, total - blocks * LANES), F32)
    for i, ref in enumerate((low, own, high)):
        start = skip + i * layers
        for k in range(layers):
            full[start + k] = ref[pl.ds(k * rows, rows), :]
        cells = [ref[pl.ds(n + 4 * EDGE * j, 4 * EDGE), :] for j in range(blocks)]
        sb = sb + turned(jnp.concatenate(cells + [blank], axis=1), start * rows, 1)
    for k in range(skip):
        full[k] = jnp.zeros((rows, LANES), F32)
        full[count - 1 - k] = jnp.zeros((rows, LANES), F32)
    sb = strips[7] + sb * strips[6]
    sx, sd = strips[8], None
    kept = [ends_of(sx)]
    for keep, add in factors[:-1]:
        near = strips[0] * turned(sx, rows, 1) + strips[1] * turned(sx, -rows, 1)
        near += strips[2] * turned(sx, 1, 1) + strips[3] * turned(sx, -1, 1)
        near += strips[4] * turned(sx, 1, 0) + strips[5] * turned(sx, -1, 0)
        step = add * (sb - sx + near)
        sd = step if sd is None else step + keep * sd
        sx = sx + sd
        kept.append(ends_of(sx))
    place_in = end_lanes(2, 1)
    place_in = jnp.concatenate([place_in, place_in], axis=0)
    for s, pair in enumerate(kept):
        start = (1 + s) * rows // LANES * LANES
        stop = -(-(count - 1 - s) * rows // LANES) * LANES
        ends[start:stop, s * LANES : (s + 1) * LANES] = dot(
            jnp.concatenate(parts(pair[:, start:stop]), axis=0), place_in, 0, 0)

    piece = 24
    first, last = iota((piece, LANES), 1) == 0, iota((piece, LANES), 1) == LANES - 1
    blank = jnp.zeros((EDGE, LANES), F32)

    @pl.loop(0, count)
    def _(k):
        for ref in (xa, xb):
            ref[k, pl.ds(0, EDGE)] = blank
            ref[k, pl.ds(rows + EDGE, EDGE)] = blank

    for s, (keep, add) in enumerate(factors):
        src, into = (xm if s == 0 else (xa if s % 2 else xb)), (xb if s % 2 else xa)

        @pl.loop(1 + s, count - 1 - s)
        def _(k):
            for at in range(0, rows, piece):
                here, to = pl.ds(EDGE + at, piece), pl.ds(at, piece)
                x = src[k, here]
                end = ends[pl.ds(pl.multiple_of(k * rows + at, 8), piece), s * LANES : (s + 1) * LANES]
                e = jnp.where(last, end, turned(x, -1, 1))
                w = jnp.where(first, end, turned(x, 1, 1))
                near = wz[k, to] * src[k + 1, here] + wz[k - 1, to] * src[k - 1, here]
                near += wx[k, here] * src[k, pl.ds(EDGE + at + 1, piece)]
                near += wx[k, pl.ds(EDGE + at - 1, piece)] * src[k, pl.ds(EDGE + at - 1, piece)]
                near += wy[k, to] * e + wyw[k, to] * w
                if s == 0:
                    rhs = b0[k, to] + full[k, to] * inv[k, to]
                    b[k, to] = rhs
                else:
                    rhs = b[k, to]
                step = add * (rhs - x + inv[k, to] * near)
                if s > 0:
                    step = step + keep * d[k, to]
                if s < SWEEPS - 1:
                    d[k, to] = step
                into[k, here] = x + step

    final = xb if SWEEPS % 2 == 0 else xa
    for k in range(4):
        out[pl.ds(k * LANES, LANES), :] = final[SWEEPS + k, pl.ds(2 * EDGE, LANES)]
    scale = 1.0
    for _, add in factors:
        scale = scale * add
    tile = pl.ds(EDGE, LANES)
    for i, (start, way) in enumerate(((1, 1), (count - 2, -1))):
        gain = scale * inv[start, tile]
        for j in range(1, SWEEPS):
            at = start + way * j
            gain = gain * inv[at, tile] * wz[at - 1 if way > 0 else at, tile]
        pull[pl.ds(i * LANES, LANES), :] = gain


def reply_kernel(x, pull, low2, high2, hot, out, replies):
    n = out.shape[0]
    first, last = pl.ds(0, LANES), pl.ds(n - LANES, LANES)
    out[...] = x[...]
    out[first, :] = x[first, :] + pull[pl.ds(0, LANES), :] * low2[...]
    out[last, :] = x[last, :] + pull[pl.ds(LANES, LANES), :] * high2[...]
    replies[...] = pick_rows(hot[...], out[...])


def final_kernel(returned, hot, gain, mob, mobility, ionization):
    back = pick_rows(hot[...], returned[...])
    mobility[...] = mob[...] * jnp.exp(-0.7 * back)
    ionization[...] = jnp.exp(gain[...] * (1.0 + 0.3 * back))


def shifted(v, axis, by):
    count = lax.axis_size(axis)
    pairs = [(i, i + by) for i in range(count) if 0 <= i + by < count]
    return lax.ppermute(v, axis, pairs) if pairs else jnp.zeros_like(v)


def exchanged(v):
    lines = v.reshape(v.shape[0], 1, v.shape[1])
    return lax.all_to_all(lines, ("gx", "gy"), split_axis=0, concat_axis=0, tiled=True).reshape(v.shape)


def per_device(
    efield, density, mobility_prev, thermal_prev, owner, block, live, material,
    mat_conductivity, mat_softening, mat_capacity,
):
    layers, xcells, width = density.shape
    n = layers * xcells
    peers = lax.axis_size("gx") * lax.axis_size("gy")
    slots = max(2, 2 * n // peers)
    line = peers * (slots + 1)
    flat = lambda a: a.reshape(n, width)
    ef = efield.reshape(3, n, width)
    den, mob, x0 = flat(density), flat(mobility_prev), flat(thermal_prev)
    own, blk, liv = owner.reshape(1, n), block.reshape(1, n), live.reshape(1, n)
    mat = material.reshape(layers, xcells)
    sized = lambda *s: (s, F32)

    given = [ef, den, mob, own, blk, liv]
    [sent] = call(
        functools.partial(dispatch_kernel, peers, slots), [sized(line, width)], given, "dispatch", flops=10**8, hbm=True, limit=60,
        scratch=[pltpu.VMEM(a.shape, a.dtype) for a in given] + [pltpu.SemaphoreType.DMA((len(given),))])
    received = exchanged(sent)

    far = SWEEPS - layers
    count = layers + 2 * SWEEPS
    rows = xcells + 2 * EDGE
    total = count * rows
    aside = sized(far * xcells + EDGE, width)
    near, up, down = call(
        functools.partial(start_z_kernel, far), [sized(n + EDGE, width), aside, aside], [x0, mat], "start_z")
    low, high = shifted(near, "gz", 1), shifted(near, "gz", -1)
    low2, high2 = shifted(up, "gz", 2), shifted(down, "gz", -2)
    gain, dest = call(functools.partial(after_kernel, slots), [sized(n, width), ((n, peers * slots), BF16)], [ef, own], "gain")
    edge = sized(count * (EDGE + 1), width)
    xz, mats, start_low, start_high = call(
        functools.partial(start_x_kernel, far), [sized(count, xcells, width), sized(count, width), edge, edge],
        [low2, low, near, high, high2], "start_x")
    received, start_low, start_high, gain, dest = lax.optimization_barrier(
        (received, start_low, start_high, gain, dest))

    source, first, last = call(
        functools.partial(combine_kernel, peers, slots), [sized(n, width)] + [sized(xcells, width)] * 2,
        [received], "combine", flops=10**8)
    [ids] = call(functools.partial(ids_kernel, peers, slots), [((peers * slots, n), BF16)], [received], "ids")
    edge = sized(count * (EDGE + 1) + layers * EDGE, width)
    xlow, xhigh = call(pack_x_kernel, [edge, edge], [source, start_low, start_high], "pack_x")
    before, after = shifted(xhigh, "gx", 1), shifted(xlow, "gx", -1)
    before, after, ids = lax.optimization_barrier((before, after, ids))
    tall, tile, flat_edge = sized(count, rows + 2 * EDGE, width), sized(count, rows, width), sized(2 * EDGE, total)
    inner = layers * rows
    xm, full, sides, heat_sides, flat_mat, ylow, yhigh = call(
        pack_y_kernel,
        [tall, sized(inner, width), flat_edge, sized(2 * EDGE, inner), sized(EDGE, total), flat_edge, flat_edge],
        [xz, mats, source, after, before], "pack_y")
    ylow, yhigh, first, last = lax.optimization_barrier((ylow, yhigh, first, last))
    before, after = shifted(yhigh, "gy", 1), shifted(ylow, "gy", -1)
    low2, high2 = shifted(last, "gz", 2), shifted(first, "gz", -2)
    blocks = -(-inner // LANES)
    [around] = call(
        pack_z_kernel, [sized(inner + 4 * EDGE * blocks, width)], [full, heat_sides, before, after], "pack_z")
    around, low2, high2 = lax.optimization_barrier((around, low2, high2))
    low, high = shifted(around, "gz", 1), shifted(around, "gz", -1)
    weights = call(
        weights_kernel, [tile, tall, tile, tile, tile, tile, sized(9, 4 * EDGE, total)],
        [mat_conductivity, mat_softening, mat_capacity, xm, sides, flat_mat, before, after], "weights",
        scratch=[pltpu.VMEM((count, rows + 2 * EDGE, width), F32), pltpu.VMEM((total, 3 * width), F32),
                 pltpu.VMEM((total, width), F32)],
        limit=32, flops=10**9, smem=(0, 1, 2))
    low, high, weights = lax.optimization_barrier((low, high, weights))
    x, pull = call(
        sweep_kernel, [sized(n, width), sized(2 * xcells, width)],
        [xm] + list(weights) + [low, around, high], "sweeps",
        scratch=[pltpu.VMEM((count, rows, width), F32)] * 3 + [pltpu.VMEM((count, rows + 2 * EDGE, width), F32)] * 2
        + [pltpu.VMEM((total, SWEEPS * width), F32)],
        limit=36, flops=10**8)
    x, pull, low2, high2 = lax.optimization_barrier((x, pull, low2, high2))
    x, replies = call(
        reply_kernel, [sized(n, width), sized(peers * slots, width)], [x, pull, low2, high2, ids], "reply", flops=10**8)
    returned = exchanged(replies)
    mobility, ionization = call(final_kernel, [sized(n, width)] * 2, [returned, dest, gain, mob], "finish", flops=10**8)
    shape = density.shape
    return x.reshape(shape), mobility.reshape(shape), ionization.reshape(shape)


def solution(mesh):
    tile = P("gz", "gx", "gy")
    rows = P("gz", "gx", "gy", None)
    placed = (
        P(None, "gz", "gx", "gy"), tile, tile, tile,
        P("gz", "gx", "gy", None, None), rows, rows, rows, P(), P(), P(),
    )
    return jax.shard_map(
        per_device, mesh=mesh, in_specs=placed, out_specs=(tile, tile, tile), check_vma=False
    )
```

```python
import functools

import jax
import jax.numpy as jnp
from jax import lax
from jax.experimental import pallas as pl
from jax.experimental.pallas import tpu as pltpu
from jax.sharding import PartitionSpec as P

SWEEPS = 6
THETA = 1.01
DELTA = 0.99
LANES = 128
EDGE = 8
F32 = jnp.float32
BF16 = jnp.bfloat16
I32 = jnp.int32


def steps():
    sigma = THETA / DELTA
    rho = 1.0 / sigma
    found = [(0.0, 1.0 / THETA)]
    for _ in range(SWEEPS - 1):
        rho_new = 1.0 / (2.0 * sigma - rho)
        found.append((rho_new * rho, 2.0 * rho_new / DELTA))
        rho = rho_new
    return found


def iota(shape, dim):
    return lax.broadcasted_iota(I32, shape, dim)


def dot(a, b, ca, cb):
    return lax.dot_general(a, b, (((ca,), (cb,)), ((), ())), preferred_element_type=F32)


def parts(v):
    high = v.astype(BF16)
    return high, (v - high.astype(F32)).astype(BF16)


def pick_rows(hot, rows):
    high, low = parts(rows)
    got = dot(hot, jnp.concatenate([high, low], axis=1), 1, 0)
    width = rows.shape[1]
    return got[:, :width] + got[:, width:]


def column(row):
    same = iota((LANES, LANES), 0) == iota((LANES, LANES), 1)
    found = []
    for at in range(0, row.shape[1], LANES):
        piece = jnp.broadcast_to(row[:, at : at + LANES], (LANES, LANES))
        found.append(jnp.sum(jnp.where(same, piece, 0), axis=1, keepdims=True))
    return jnp.concatenate(found, axis=0)


def hot_of(cond):
    return jnp.where(cond, F32(1.0), F32(0.0)).astype(BF16)


def edge_lanes():
    r, y = iota((2 * EDGE, LANES), 0), iota((2 * EDGE, LANES), 1)
    return hot_of(y == jnp.where(r < EDGE, r, r + LANES - 2 * EDGE))


def call(kernel, outs, ins, name, scratch=(), limit=32, flops=0, smem=(), hbm=False):
    bytes_of = lambda a: a.size * a.dtype.itemsize
    return pl.pallas_call(
        kernel,
        out_shape=[jax.ShapeDtypeStruct(s, t) for s, t in outs],
        in_specs=[
            pl.BlockSpec(memory_space=pltpu.SMEM if i in smem else pltpu.HBM if hbm else pltpu.VMEM)
            for i in range(len(ins))
        ],
        out_specs=[pl.BlockSpec(memory_space=pltpu.VMEM) for _ in outs],
        scratch_shapes=list(scratch),
        compiler_params=pltpu.CompilerParams(vmem_limit_bytes=limit << 20),
        cost_estimate=pl.CostEstimate(
            flops=flops,
            bytes_accessed=sum(bytes_of(a) for a in ins)
            + sum(jax.ShapeDtypeStruct(s, t).size * 4 for s, t in outs),
            transcendentals=0,
        ),
        name=name,
    )(*ins)


def dispatch_kernel(peers, slots, *refs):
    far, out, near, sems = refs[:6], refs[6], refs[7:13], refs[13]
    copies = [pltpu.make_async_copy(a, b, sems.at[i]) for i, (a, b) in enumerate(zip(far, near))]
    for copy in copies[3:] + copies[:3]:
        copy.start()
    for copy in copies[3:]:
        copy.wait()
    ef, den, mob, owner, block, live = near
    n = owner.shape[1]
    own = owner[...]
    own_col = column(own)
    pos = jnp.zeros((1, n), I32)
    for at in range(0, n, LANES):
        r = iota((LANES, n), 0) + at
        earlier = (own_col[at : at + LANES] == own) & (r < iota((LANES, n), 1))
        pos = pos + jnp.sum(jnp.where(earlier, 1, 0), axis=0, keepdims=True)
    dest = own * (slots + 1) + pos
    hot = hot_of(iota((peers * (slots + 1), n), 0) == dest)
    named = hot_of(iota((peers, n), 0) == own)
    at_slot = iota((LANES, n), 0) == pos
    code = block[...] + 1
    high = jnp.where(at_slot, code // 32, 0).astype(F32).astype(BF16)
    low = jnp.where(at_slot, code % 32, 0).astype(F32).astype(BF16)
    labels = dot(named, high, 1, 1) * 32.0 + dot(named, low, 1, 1)
    live_col = column(live[...])
    for copy in copies[:3]:
        copy.wait()
    esq = ef[0] * ef[0] + ef[1] * ef[1] + ef[2] * ef[2]
    heat = 0.2 * den[...] * mob[...] * esq
    heat = jnp.where(iota(heat.shape, 1) < live_col, heat, F32(0.0))
    out[...] = pick_rows(hot, heat)
    out[pl.ds(slots, peers, stride=slots + 1), :] = labels


def after_kernel(slots, ef, owner, gain, hot):
    n = owner.shape[1]
    esq = ef[0] * ef[0] + ef[1] * ef[1] + ef[2] * ef[2]
    gain[...] = -2.0 * lax.rsqrt(esq + 1.0)
    own = owner[...]
    own_col = column(own)
    for at in range(0, n, LANES):
        r = iota((LANES, n), 0) + at
        piece = own_col[at : at + LANES]
        earlier = (piece == own) & (iota((LANES, n), 1) < r)
        pos = jnp.sum(jnp.where(earlier, 1, 0), axis=1, keepdims=True)
        size = (LANES, hot.shape[1])
        hot[pl.ds(at, LANES), :] = hot_of(jnp.broadcast_to(piece * slots + pos, size) == iota(size, 1))


def labels_of(received, peers, slots):
    got = received[pl.ds(slots, peers, stride=slots + 1), :]
    high = jnp.floor(got * (1.0 / 32.0))
    return high.astype(BF16), (got - 32.0 * high).astype(BF16)


def combine_kernel(peers, slots, received, source, first, last):
    n = source.shape[0]
    total = received.shape[0]
    high, low = labels_of(received, peers, slots)
    j = iota((LANES, total), 1)
    spread = hot_of(iota((LANES, total), 0) == j - (slots + 1) * lax.div(j, slots + 1))
    named = dot(high, spread, 1, 0) * 32.0 + dot(low, spread, 1, 0)
    mine = iota((peers, total), 0) == lax.div(iota((peers, total), 1), slots + 1)
    ids = jnp.sum(jnp.where(mine, named, 0.0), axis=0, keepdims=True).astype(I32)
    picks = hot_of(iota((n, total), 0) + 1 == ids)
    source[...] = pick_rows(picks, received[...])
    first[...] = source[pl.ds(0, LANES), :]
    last[...] = source[pl.ds(n - LANES, LANES), :]


def ids_kernel(peers, slots, received, hot):
    total = peers * slots
    high, low = labels_of(received, peers, slots)
    own = hot_of(lax.div(iota((total, peers), 0), slots) == iota((total, peers), 1))
    named = dot(own, high, 1, 0) * 32.0 + dot(own, low, 1, 0)
    i = iota((total, LANES), 0)
    mine = iota((total, LANES), 1) == i - slots * lax.div(i, slots)
    found = jnp.sum(jnp.where(mine, named, 0.0), axis=1, keepdims=True) - 1.0
    hot[...] = hot_of(jnp.broadcast_to(found.astype(I32), hot.shape) == iota(hot.shape, 1))


def start_z_kernel(far, x0, material, near, up, down):
    layers, xcells = material.shape
    n = layers * xcells
    mat = (material[...] + 1).astype(F32)
    rows = far * xcells
    zeros = lambda k: jnp.zeros((k, LANES), F32)
    near[pl.ds(0, n), :] = x0[...]
    near[pl.ds(n, EDGE), :] = jnp.concatenate([mat, zeros(EDGE - layers)], axis=0)
    up[pl.ds(0, rows), :] = x0[pl.ds(n - rows, rows), :]
    up[pl.ds(rows, EDGE), :] = jnp.concatenate([mat[layers - far :], zeros(EDGE - far)], axis=0)
    down[pl.ds(0, rows), :] = x0[pl.ds(0, rows), :]
    down[pl.ds(rows, EDGE), :] = jnp.concatenate([mat[:far], zeros(EDGE - far)], axis=0)


def start_x_kernel(far, low2, low, own, high, high2, xz, mats, xlow, xhigh):
    found = [(low2, k) for k in range(far)]
    for ref in (low, own, high):
        found += [(ref, k) for k in range(4)]
    found += [(high2, k) for k in range(far)]
    count = len(found)
    for k, (ref, at) in enumerate(found):
        piece = ref[pl.ds(at * LANES, LANES), :]
        xz[k] = piece
        xlow[pl.ds(k * EDGE, EDGE), :] = piece[:EDGE]
        xhigh[pl.ds(k * EDGE, EDGE), :] = piece[LANES - EDGE :]
        mats[pl.ds(k, 1), :] = ref[pl.ds(ref.shape[0] - EDGE + at, 1), :]
    xlow[pl.ds(count * EDGE, count), :] = mats[...]
    xhigh[pl.ds(count * EDGE, count), :] = mats[...]


def pack_x_kernel(source, start_low, start_high, xlow, xhigh):
    top = start_low.shape[0]
    xlow[pl.ds(0, top), :] = start_low[...]
    xhigh[pl.ds(0, top), :] = start_high[...]
    for k in range(source.shape[0] // LANES):
        to = pl.ds(top + k * EDGE, EDGE)
        xlow[to, :] = source[pl.ds(k * LANES, EDGE), :]
        xhigh[to, :] = source[pl.ds((k + 1) * LANES - EDGE, EDGE), :]


def flat_sides(rows):
    high, low = parts(rows)
    edges = edge_lanes()
    return dot(edges, high, 1, 1) + dot(edges, low, 1, 1)


def pack_y_kernel(xz, mats, own, after, before, xm, full, sides, heat_sides, flat_mat, ylow, yhigh):
    count = xz.shape[0]
    blank = jnp.zeros((EDGE, LANES), F32)
    for k in range(count):
        part = pl.ds(k * EDGE, EDGE)
        xm[k, pl.ds(0, EDGE)] = blank
        xm[k, pl.ds(EDGE, EDGE)] = before[part, :]
        xm[k, pl.ds(2 * EDGE, LANES)] = xz[k]
        xm[k, pl.ds(LANES + 2 * EDGE, EDGE)] = after[part, :]
        xm[k, pl.ds(LANES + 3 * EDGE, EDGE)] = blank
    top = count * (EDGE + 1)
    size = LANES + 2 * EDGE
    layers = own.shape[0] // LANES
    for k in range(layers):
        part = pl.ds(top + k * EDGE, EDGE)
        full[pl.ds(k * size, EDGE), :] = before[part, :]
        full[pl.ds(k * size + EDGE, LANES), :] = own[pl.ds(k * LANES, LANES), :]
        full[pl.ds(k * size + EDGE + LANES, EDGE), :] = after[part, :]
    rows = LANES + 2 * EDGE
    total = count * rows
    found = flat_sides(xm[:, EDGE : EDGE + rows].reshape(total, LANES))
    sides[...] = found
    beside = pl.ds(count * EDGE, count)
    around = jnp.concatenate([before[beside, :], mats[...], after[beside, :]], axis=0)
    q = iota((1, total), 1)
    layer = lax.div(q, rows)
    row = q - layer * rows
    tile = jnp.where(row < EDGE, 0, jnp.where(row < LANES + EDGE, 1, 2))
    lane = row - EDGE + LANES * (1 - tile)
    spread = hot_of(iota((LANES, total), 0) == lane)
    named = dot(around.astype(BF16), spread, 1, 0)
    mine = iota((3 * count, total), 0) == tile * count + layer
    mat = jnp.sum(jnp.where(mine, named, 0.0), axis=0, keepdims=True)
    flat_mat[...] = jnp.broadcast_to(mat, (EDGE, total))
    heat_found = flat_sides(full[...])
    inner = pl.ds(0, layers * rows)
    beyond = jnp.zeros((EDGE, total), F32)
    heat_sides[...] = heat_found
    ylow[pl.ds(0, EDGE), :] = found[:EDGE]
    yhigh[pl.ds(0, EDGE), :] = found[EDGE:]
    ylow[pl.ds(EDGE, EDGE), :] = beyond
    yhigh[pl.ds(EDGE, EDGE), :] = beyond
    ylow[pl.ds(EDGE, EDGE), inner] = heat_found[:EDGE]
    yhigh[pl.ds(EDGE, EDGE), inner] = heat_found[EDGE:]
    ylow[pl.ds(2 * EDGE - 1, 1), :] = mat
    yhigh[pl.ds(EDGE, 1), :] = mat


def three_parts(v):
    high = v.astype(BF16)
    rest = v - high.astype(F32)
    mid = rest.astype(BF16)
    return high, mid, (rest - mid.astype(F32)).astype(BF16)


def ends_of(strip):
    return jnp.concatenate([strip[EDGE - 1 : EDGE], strip[3 * EDGE : 3 * EDGE + 1]], axis=0)


def end_lanes(depth, times):
    r, y = iota((depth, times * LANES), 0), iota((depth, times * LANES), 1)
    first = (r % 2 == 0) & (y == (r // 2) * LANES)
    last = (r % 2 == 1) & (y == (r // 2) * LANES + LANES - 1)
    return hot_of(first | last)


def turned(v, by, axis):
    return pltpu.roll(v, by % v.shape[axis], axis)


def strip_of(sides, before, after):
    return jnp.concatenate([before, sides, after], axis=0)


def pack_z_kernel(full, sides, before, after, out):
    n = full.shape[0]
    out[pl.ds(0, n), :] = full[...]
    strip = strip_of(sides[...], before[pl.ds(EDGE, EDGE), 0:n], after[pl.ds(EDGE, EDGE), 0:n])
    blocks = -(-n // LANES)
    strip = jnp.concatenate([strip, jnp.zeros((4 * EDGE, blocks * LANES - n), F32)], axis=1)
    for i in range(blocks):
        out[pl.ds(n + 4 * EDGE * i, 4 * EDGE), :] = strip[:, i * LANES : (i + 1) * LANES]


def weights_kernel(base, soft, heat, xm, sides, flat_mat, before, after, wz, wx, wy, wyw, inv, b0, strips, cond, cols, ends):
    count, rows = inv.shape[0], inv.shape[1]
    total = count * rows
    mat = jnp.concatenate(
        [flat_mat[0:1], before[pl.ds(EDGE, 1), :], after[pl.ds(2 * EDGE - 1, 1), :]], axis=0
    )
    tables = []
    for values in (base, soft, heat):
        found = jnp.zeros(mat.shape, F32)
        for m in range(values.shape[0]):
            found = jnp.where(mat == F32(m + 1), values[m], found)
        tables.append(found)
    own = [p for t in tables for p in three_parts(t[0:1])]
    r, y = iota((9, 3 * LANES), 0), iota((9, 3 * LANES), 1)
    cols[...] = dot(jnp.concatenate(own, axis=0), hot_of(lax.div(r, 3) == lax.div(y, LANES)), 0, 0)
    wide = lambda t, i: jnp.broadcast_to(t[i : i + 1], (EDGE, total))
    kb, ks, cf = (jnp.concatenate([wide(t, 1), wide(t, 0), wide(t, 0), wide(t, 2)], axis=0) for t in tables)
    sx = strip_of(sides[...], before[:EDGE], after[:EDGE])
    sc = kb / (1.0 + ks * sx)
    down = lambda by, axis: 0.5 * (sc + turned(sc, by, axis))
    around = [down(rows, 1), down(-rows, 1), down(1, 1), down(-1, 1), down(1, 0), down(-1, 0)]
    diag = cf
    for w in around:
        diag = diag + w
    si = jnp.where(cf > 0.0, 1.0 / diag, 0.0)
    for i, w in enumerate(around):
        strips[i] = w * si
    strips[6] = si
    strips[7] = cf * sx * si
    strips[8] = sx
    got = [dot(p, end_lanes(2, 1), 0, 0) for p in three_parts(ends_of(sc))]
    ends[...] = got[0] + got[1] + got[2]

    piece = 16
    blank = jnp.zeros((EDGE, LANES), F32)

    @pl.loop(0, count)
    def _(k):
        cond[k, pl.ds(0, EDGE)] = blank
        cond[k, pl.ds(rows + EDGE, EDGE)] = blank
        wx[k, pl.ds(0, EDGE)] = blank
        wx[k, pl.ds(rows + EDGE, EDGE)] = blank
        for at in range(0, rows, piece):
            part = pl.ds(pl.multiple_of(k * rows + at, 8), piece)
            x = xm[k, pl.ds(EDGE + at, piece)]
            cond[k, pl.ds(EDGE + at, piece)] = cols[part, 0:LANES] / (1.0 + cols[part, LANES : 2 * LANES] * x)

    first, last = iota((piece, LANES), 1) == 0, iota((piece, LANES), 1) == LANES - 1
    wz[0] = 0.5 * (cond[0, pl.ds(EDGE, rows)] + cond[1, pl.ds(EDGE, rows)])

    @pl.loop(1, count - 1)
    def _(k):
        for at in range(0, rows, piece):
            here = pl.ds(EDGE + at, piece)
            part = pl.ds(pl.multiple_of(k * rows + at, 8), piece)
            to = pl.ds(at, piece)
            c, end = cond[k, here], ends[part, :]
            up = 0.5 * (c + cond[k + 1, here])
            low = 0.5 * (c + cond[k - 1, here])
            right = 0.5 * (c + cond[k, pl.ds(EDGE + at + 1, piece)])
            left = 0.5 * (c + cond[k, pl.ds(EDGE + at - 1, piece)])
            e = 0.5 * (c + jnp.where(last, end, turned(c, -1, 1)))
            w = 0.5 * (c + jnp.where(first, end, turned(c, 1, 1)))
            cf = cols[part, 2 * LANES : 3 * LANES]
            diag = cf + up + low + right + left + e + w
            i = jnp.where(cf > 0.0, 1.0 / diag, 0.0)
            wz[k, to] = up
            wx[k, here] = right
            wy[k, to] = e
            wyw[k, to] = w
            inv[k, to] = i
            b0[k, to] = cf * xm[k, here] * i


def sweep_kernel(xm, wz, wx, wy, wyw, inv, b0, strips, low, own, high,
                 out, pull, full, b, d, xa, xb, ends):
    count, rows, _ = inv.shape
    total = count * rows
    factors = steps()

    layers = out.shape[0] // LANES
    n = layers * rows
    skip = (count - 3 * layers) // 2
    sb = jnp.zeros((4 * EDGE, total), F32)
    blocks = -(-n // LANES)
    blank = jnp.zeros((4 * EDGE, total - blocks * LANES), F32)
    for i, ref in enumerate((low, own, high)):
        start = skip + i * layers
        for k in range(layers):
            full[start + k] = ref[pl.ds(k * rows, rows), :]
        cells = [ref[pl.ds(n + 4 * EDGE * j, 4 * EDGE), :] for j in range(blocks)]
        sb = sb + turned(jnp.concatenate(cells + [blank], axis=1), start * rows, 1)
    for k in range(skip):
        full[k] = jnp.zeros((rows, LANES), F32)
        full[count - 1 - k] = jnp.zeros((rows, LANES), F32)
    sb = strips[7] + sb * strips[6]
    sx, sd = strips[8], None
    kept = [ends_of(sx)]
    for keep, add in factors[:-1]:
        near = strips[0] * turned(sx, rows, 1) + strips[1] * turned(sx, -rows, 1)
        near += strips[2] * turned(sx, 1, 1) + strips[3] * turned(sx, -1, 1)
        near += strips[4] * turned(sx, 1, 0) + strips[5] * turned(sx, -1, 0)
        step = add * (sb - sx + near)
        sd = step if sd is None else step + keep * sd
        sx = sx + sd
        kept.append(ends_of(sx))
    place_in = end_lanes(2, 1)
    place_in = jnp.concatenate([place_in, place_in], axis=0)
    for s, pair in enumerate(kept):
        start = (1 + s) * rows // LANES * LANES
        stop = -(-(count - 1 - s) * rows // LANES) * LANES
        ends[start:stop, s * LANES : (s + 1) * LANES] = dot(
            jnp.concatenate(parts(pair[:, start:stop]), axis=0), place_in, 0, 0)

    piece = 24
    first, last = iota((piece, LANES), 1) == 0, iota((piece, LANES), 1) == LANES - 1
    blank = jnp.zeros((EDGE, LANES), F32)

    @pl.loop(0, count)
    def _(k):
        for ref in (xa, xb):
            ref[k, pl.ds(0, EDGE)] = blank
            ref[k, pl.ds(rows + EDGE, EDGE)] = blank

    for s, (keep, add) in enumerate(factors):
        src, into = (xm if s == 0 else (xa if s % 2 else xb)), (xb if s % 2 else xa)

        @pl.loop(1 + s, count - 1 - s)
        def _(k):
            for at in range(0, rows, piece):
                here, to = pl.ds(EDGE + at, piece), pl.ds(at, piece)
                x = src[k, here]
                end = ends[pl.ds(pl.multiple_of(k * rows + at, 8), piece), s * LANES : (s + 1) * LANES]
                e = jnp.where(last, end, turned(x, -1, 1))
                w = jnp.where(first, end, turned(x, 1, 1))
                near = wz[k, to] * src[k + 1, here] + wz[k - 1, to] * src[k - 1, here]
                near += wx[k, here] * src[k, pl.ds(EDGE + at + 1, piece)]
                near += wx[k, pl.ds(EDGE + at - 1, piece)] * src[k, pl.ds(EDGE + at - 1, piece)]
                near += wy[k, to] * e + wyw[k, to] * w
                if s == 0:
                    rhs = b0[k, to] + full[k, to] * inv[k, to]
                    b[k, to] = rhs
                else:
                    rhs = b[k, to]
                step = add * (rhs - x + inv[k, to] * near)
                if s > 0:
                    step = step + keep * d[k, to]
                if s < SWEEPS - 1:
                    d[k, to] = step
                into[k, here] = x + step

    final = xb if SWEEPS % 2 == 0 else xa
    for k in range(4):
        out[pl.ds(k * LANES, LANES), :] = final[SWEEPS + k, pl.ds(2 * EDGE, LANES)]
    scale = 1.0
    for _, add in factors:
        scale = scale * add
    tile = pl.ds(EDGE, LANES)
    for i, (start, way) in enumerate(((1, 1), (count - 2, -1))):
        gain = scale * inv[start, tile]
        for j in range(1, SWEEPS):
            at = start + way * j
            gain = gain * inv[at, tile] * wz[at - 1 if way > 0 else at, tile]
        pull[pl.ds(i * LANES, LANES), :] = gain


def reply_kernel(x, pull, low2, high2, hot, out, replies):
    n = out.shape[0]
    first, last = pl.ds(0, LANES), pl.ds(n - LANES, LANES)
    out[...] = x[...]
    out[first, :] = x[first, :] + pull[pl.ds(0, LANES), :] * low2[...]
    out[last, :] = x[last, :] + pull[pl.ds(LANES, LANES), :] * high2[...]
    replies[...] = pick_rows(hot[...], out[...])


def final_kernel(returned, hot, gain, mob, mobility, ionization):
    back = pick_rows(hot[...], returned[...])
    mobility[...] = mob[...] * jnp.exp(-0.7 * back)
    ionization[...] = jnp.exp(gain[...] * (1.0 + 0.3 * back))


def shifted(v, axis, by):
    count = lax.axis_size(axis)
    pairs = [(i, i + by) for i in range(count) if 0 <= i + by < count]
    return lax.ppermute(v, axis, pairs) if pairs else jnp.zeros_like(v)


def exchanged(v):
    lines = v.reshape(v.shape[0], 1, v.shape[1])
    return lax.all_to_all(lines, ("gx", "gy"), split_axis=0, concat_axis=0, tiled=True).reshape(v.shape)


def per_device(
    efield, density, mobility_prev, thermal_prev, owner, block, live, material,
    mat_conductivity, mat_softening, mat_capacity,
):
    layers, xcells, width = density.shape
    n = layers * xcells
    peers = lax.axis_size("gx") * lax.axis_size("gy")
    slots = max(2, 2 * n // peers)
    line = peers * (slots + 1)
    flat = lambda a: a.reshape(n, width)
    ef = efield.reshape(3, n, width)
    den, mob, x0 = flat(density), flat(mobility_prev), flat(thermal_prev)
    own, blk, liv = owner.reshape(1, n), block.reshape(1, n), live.reshape(1, n)
    mat = material.reshape(layers, xcells)
    sized = lambda *s: (s, F32)

    given = [ef, den, mob, own, blk, liv]
    [sent] = call(
        functools.partial(dispatch_kernel, peers, slots), [sized(line, width)], given, "dispatch", flops=10**8, hbm=True, limit=60,
        scratch=[pltpu.VMEM(a.shape, a.dtype) for a in given] + [pltpu.SemaphoreType.DMA((len(given),))])
    received = exchanged(sent)

    far = SWEEPS - layers
    count = layers + 2 * SWEEPS
    rows = xcells + 2 * EDGE
    total = count * rows
    aside = sized(far * xcells + EDGE, width)
    near, up, down = call(
        functools.partial(start_z_kernel, far), [sized(n + EDGE, width), aside, aside], [x0, mat], "start_z")
    low, high = shifted(near, "gz", 1), shifted(near, "gz", -1)
    low2, high2 = shifted(up, "gz", 2), shifted(down, "gz", -2)
    gain, dest = call(functools.partial(after_kernel, slots), [sized(n, width), ((n, peers * slots), BF16)], [ef, own], "gain")
    edge = sized(count * (EDGE + 1), width)
    xz, mats, start_low, start_high = call(
        functools.partial(start_x_kernel, far), [sized(count, xcells, width), sized(count, width), edge, edge],
        [low2, low, near, high, high2], "start_x")
    received, start_low, start_high, gain, dest = lax.optimization_barrier(
        (received, start_low, start_high, gain, dest))

    source, first, last = call(
        functools.partial(combine_kernel, peers, slots), [sized(n, width)] + [sized(xcells, width)] * 2,
        [received], "combine", flops=10**8)
    [ids] = call(functools.partial(ids_kernel, peers, slots), [((peers * slots, n), BF16)], [received], "ids")
    edge = sized(count * (EDGE + 1) + layers * EDGE, width)
    xlow, xhigh = call(pack_x_kernel, [edge, edge], [source, start_low, start_high], "pack_x")
    before, after = shifted(xhigh, "gx", 1), shifted(xlow, "gx", -1)
    before, after, ids = lax.optimization_barrier((before, after, ids))
    tall, tile, flat_edge = sized(count, rows + 2 * EDGE, width), sized(count, rows, width), sized(2 * EDGE, total)
    inner = layers * rows
    xm, full, sides, heat_sides, flat_mat, ylow, yhigh = call(
        pack_y_kernel,
        [tall, sized(inner, width), flat_edge, sized(2 * EDGE, inner), sized(EDGE, total), flat_edge, flat_edge],
        [xz, mats, source, after, before], "pack_y")
    before, after = shifted(yhigh, "gy", 1), shifted(ylow, "gy", -1)
    blocks = -(-inner // LANES)
    [around] = call(
        pack_z_kernel, [sized(inner + 4 * EDGE * blocks, width)], [full, heat_sides, before, after], "pack_z")
    low, high = shifted(around, "gz", 1), shifted(around, "gz", -1)
    weights = call(
        weights_kernel, [tile, tall, tile, tile, tile, tile, sized(9, 4 * EDGE, total)],
        [mat_conductivity, mat_softening, mat_capacity, xm, sides, flat_mat, before, after], "weights",
        scratch=[pltpu.VMEM((count, rows + 2 * EDGE, width), F32), pltpu.VMEM((total, 3 * width), F32),
                 pltpu.VMEM((total, width), F32)],
        limit=32, flops=10**9, smem=(0, 1, 2))
    first, last, weights = lax.optimization_barrier((first, last, weights))
    low2, high2 = shifted(last, "gz", 2), shifted(first, "gz", -2)
    x, pull = call(
        sweep_kernel, [sized(n, width), sized(2 * xcells, width)],
        [xm] + list(weights) + [low, around, high], "sweeps",
        scratch=[pltpu.VMEM((count, rows, width), F32)] * 3 + [pltpu.VMEM((count, rows + 2 * EDGE, width), F32)] * 2
        + [pltpu.VMEM((total, SWEEPS * width), F32)],
        limit=36, flops=10**8)
    x, pull, low2, high2 = lax.optimization_barrier((x, pull, low2, high2))
    x, replies = call(
        reply_kernel, [sized(n, width), sized(peers * slots, width)], [x, pull, low2, high2, ids], "reply", flops=10**8)
    returned = exchanged(replies)
    mobility, ionization = call(final_kernel, [sized(n, width)] * 2, [returned, dest, gain, mob], "finish", flops=10**8)
    shape = density.shape
    return x.reshape(shape), mobility.reshape(shape), ionization.reshape(shape)


def solution(mesh):
    tile = P("gz", "gx", "gy")
    rows = P("gz", "gx", "gy", None)
    placed = (
        P(None, "gz", "gx", "gy"), tile, tile, tile,
        P("gz", "gx", "gy", None, None), rows, rows, rows, P(), P(), P(),
    )
    return jax.shard_map(
        per_device, mesh=mesh, in_specs=placed, out_specs=(tile, tile, tile), check_vma=False
    )
```

```python
import functools

import jax
import jax.numpy as jnp
from jax import lax
from jax.experimental import pallas as pl
from jax.experimental.pallas import tpu as pltpu
from jax.sharding import PartitionSpec as P

SWEEPS = 6
THETA = 1.01
DELTA = 0.99
LANES = 128
EDGE = 8
F32 = jnp.float32
BF16 = jnp.bfloat16
I32 = jnp.int32


def steps():
    sigma = THETA / DELTA
    rho = 1.0 / sigma
    found = [(0.0, 1.0 / THETA)]
    for _ in range(SWEEPS - 1):
        rho_new = 1.0 / (2.0 * sigma - rho)
        found.append((rho_new * rho, 2.0 * rho_new / DELTA))
        rho = rho_new
    return found


def iota(shape, dim):
    return lax.broadcasted_iota(I32, shape, dim)


def dot(a, b, ca, cb):
    return lax.dot_general(a, b, (((ca,), (cb,)), ((), ())), preferred_element_type=F32)


def parts(v):
    high = v.astype(BF16)
    return high, (v - high.astype(F32)).astype(BF16)


def pick_rows(hot, rows):
    high, low = parts(rows)
    got = dot(hot, jnp.concatenate([high, low], axis=1), 1, 0)
    width = rows.shape[1]
    return got[:, :width] + got[:, width:]


def column(row):
    same = iota((LANES, LANES), 0) == iota((LANES, LANES), 1)
    found = []
    for at in range(0, row.shape[1], LANES):
        piece = jnp.broadcast_to(row[:, at : at + LANES], (LANES, LANES))
        found.append(jnp.sum(jnp.where(same, piece, 0), axis=1, keepdims=True))
    return jnp.concatenate(found, axis=0)


def hot_of(cond):
    return jnp.where(cond, F32(1.0), F32(0.0)).astype(BF16)


def edge_lanes():
    r, y = iota((2 * EDGE, LANES), 0), iota((2 * EDGE, LANES), 1)
    return hot_of(y == jnp.where(r < EDGE, r, r + LANES - 2 * EDGE))


def call(kernel, outs, ins, name, scratch=(), limit=32, flops=0, smem=(), hbm=False):
    bytes_of = lambda a: a.size * a.dtype.itemsize
    return pl.pallas_call(
        kernel,
        out_shape=[jax.ShapeDtypeStruct(s, t) for s, t in outs],
        in_specs=[
            pl.BlockSpec(memory_space=pltpu.SMEM if i in smem else pltpu.HBM if hbm else pltpu.VMEM)
            for i in range(len(ins))
        ],
        out_specs=[pl.BlockSpec(memory_space=pltpu.VMEM) for _ in outs],
        scratch_shapes=list(scratch),
        compiler_params=pltpu.CompilerParams(vmem_limit_bytes=limit << 20),
        cost_estimate=pl.CostEstimate(
            flops=flops,
            bytes_accessed=sum(bytes_of(a) for a in ins)
            + sum(jax.ShapeDtypeStruct(s, t).size * 4 for s, t in outs),
            transcendentals=0,
        ),
        name=name,
    )(*ins)


def dispatch_kernel(peers, slots, *refs):
    far, out, near, sems = refs[:6], refs[6], refs[7:13], refs[13]
    copies = [pltpu.make_async_copy(a, b, sems.at[i]) for i, (a, b) in enumerate(zip(far, near))]
    for copy in copies[3:] + copies[:3]:
        copy.start()
    for copy in copies[3:]:
        copy.wait()
    ef, den, mob, owner, block, live = near
    n = owner.shape[1]
    own = owner[...]
    own_col = column(own)
    pos = jnp.zeros((1, n), I32)
    for at in range(0, n, LANES):
        r = iota((LANES, n), 0) + at
        earlier = (own_col[at : at + LANES] == own) & (r < iota((LANES, n), 1))
        pos = pos + jnp.sum(jnp.where(earlier, 1, 0), axis=0, keepdims=True)
    dest = own * (slots + 1) + pos
    hot = hot_of(iota((peers * (slots + 1), n), 0) == dest)
    named = hot_of(iota((peers, n), 0) == own)
    at_slot = iota((LANES, n), 0) == pos
    code = block[...] + 1
    high = jnp.where(at_slot, code // 32, 0).astype(F32).astype(BF16)
    low = jnp.where(at_slot, code % 32, 0).astype(F32).astype(BF16)
    labels = dot(named, high, 1, 1) * 32.0 + dot(named, low, 1, 1)
    live_col = column(live[...])
    for copy in copies[:3]:
        copy.wait()
    esq = ef[0] * ef[0] + ef[1] * ef[1] + ef[2] * ef[2]
    heat = 0.2 * den[...] * mob[...] * esq
    heat = jnp.where(iota(heat.shape, 1) < live_col, heat, F32(0.0))
    out[...] = pick_rows(hot, heat)
    out[pl.ds(slots, peers, stride=slots + 1), :] = labels


def after_kernel(slots, ef, owner, gain, hot):
    n = owner.shape[1]
    esq = ef[0] * ef[0] + ef[1] * ef[1] + ef[2] * ef[2]
    gain[...] = -2.0 * lax.rsqrt(esq + 1.0)
    own = owner[...]
    own_col = column(own)
    for at in range(0, n, LANES):
        r = iota((LANES, n), 0) + at
        piece = own_col[at : at + LANES]
        earlier = (piece == own) & (iota((LANES, n), 1) < r)
        pos = jnp.sum(jnp.where(earlier, 1, 0), axis=1, keepdims=True)
        size = (LANES, hot.shape[1])
        hot[pl.ds(at, LANES), :] = hot_of(jnp.broadcast_to(piece * slots + pos, size) == iota(size, 1))


def labels_of(received, peers, slots):
    got = received[pl.ds(slots, peers, stride=slots + 1), :]
    high = jnp.floor(got * (1.0 / 32.0))
    return high.astype(BF16), (got - 32.0 * high).astype(BF16)


def combine_kernel(peers, slots, received, source, first, last):
    n = source.shape[0]
    total = received.shape[0]
    high, low = labels_of(received, peers, slots)
    j = iota((LANES, total), 1)
    spread = hot_of(iota((LANES, total), 0) == j - (slots + 1) * lax.div(j, slots + 1))
    named = dot(high, spread, 1, 0) * 32.0 + dot(low, spread, 1, 0)
    mine = iota((peers, total), 0) == lax.div(iota((peers, total), 1), slots + 1)
    ids = jnp.sum(jnp.where(mine, named, 0.0), axis=0, keepdims=True).astype(I32)
    picks = hot_of(iota((n, total), 0) + 1 == ids)
    source[...] = pick_rows(picks, received[...])
    first[...] = source[pl.ds(0, LANES), :]
    last[...] = source[pl.ds(n - LANES, LANES), :]


def ids_kernel(peers, slots, received, hot):
    total = peers * slots
    high, low = labels_of(received, peers, slots)
    own = hot_of(lax.div(iota((total, peers), 0), slots) == iota((total, peers), 1))
    named = dot(own, high, 1, 0) * 32.0 + dot(own, low, 1, 0)
    i = iota((total, LANES), 0)
    mine = iota((total, LANES), 1) == i - slots * lax.div(i, slots)
    found = jnp.sum(jnp.where(mine, named, 0.0), axis=1, keepdims=True) - 1.0
    hot[...] = hot_of(jnp.broadcast_to(found.astype(I32), hot.shape) == iota(hot.shape, 1))


def start_z_kernel(far, x0, material, near, up, down):
    layers, xcells = material.shape
    n = layers * xcells
    mat = (material[...] + 1).astype(F32)
    rows = far * xcells
    zeros = lambda k: jnp.zeros((k, LANES), F32)
    near[pl.ds(0, n), :] = x0[...]
    near[pl.ds(n, EDGE), :] = jnp.concatenate([mat, zeros(EDGE - layers)], axis=0)
    up[pl.ds(0, rows), :] = x0[pl.ds(n - rows, rows), :]
    up[pl.ds(rows, EDGE), :] = jnp.concatenate([mat[layers - far :], zeros(EDGE - far)], axis=0)
    down[pl.ds(0, rows), :] = x0[pl.ds(0, rows), :]
    down[pl.ds(rows, EDGE), :] = jnp.concatenate([mat[:far], zeros(EDGE - far)], axis=0)


def start_x_kernel(far, low2, low, own, high, high2, xz, mats, xlow, xhigh):
    found = [(low2, k) for k in range(far)]
    for ref in (low, own, high):
        found += [(ref, k) for k in range(4)]
    found += [(high2, k) for k in range(far)]
    count = len(found)
    for k, (ref, at) in enumerate(found):
        piece = ref[pl.ds(at * LANES, LANES), :]
        xz[k] = piece
        xlow[pl.ds(k * EDGE, EDGE), :] = piece[:EDGE]
        xhigh[pl.ds(k * EDGE, EDGE), :] = piece[LANES - EDGE :]
        mats[pl.ds(k, 1), :] = ref[pl.ds(ref.shape[0] - EDGE + at, 1), :]
    xlow[pl.ds(count * EDGE, count), :] = mats[...]
    xhigh[pl.ds(count * EDGE, count), :] = mats[...]


def pack_x_kernel(source, start_low, start_high, xlow, xhigh):
    top = start_low.shape[0]
    xlow[pl.ds(0, top), :] = start_low[...]
    xhigh[pl.ds(0, top), :] = start_high[...]
    for k in range(source.shape[0] // LANES):
        to = pl.ds(top + k * EDGE, EDGE)
        xlow[to, :] = source[pl.ds(k * LANES, EDGE), :]
        xhigh[to, :] = source[pl.ds((k + 1) * LANES - EDGE, EDGE), :]


def flat_sides(rows):
    high, low = parts(rows)
    edges = edge_lanes()
    return dot(edges, high, 1, 1) + dot(edges, low, 1, 1)


def pack_y_kernel(xz, mats, own, after, before, xm, full, sides, heat_sides, flat_mat, ylow, yhigh):
    count = xz.shape[0]
    blank = jnp.zeros((EDGE, LANES), F32)
    for k in range(count):
        part = pl.ds(k * EDGE, EDGE)
        xm[k, pl.ds(0, EDGE)] = blank
        xm[k, pl.ds(EDGE, EDGE)] = before[part, :]
        xm[k, pl.ds(2 * EDGE, LANES)] = xz[k]
        xm[k, pl.ds(LANES + 2 * EDGE, EDGE)] = after[part, :]
        xm[k, pl.ds(LANES + 3 * EDGE, EDGE)] = blank
    top = count * (EDGE + 1)
    size = LANES + 2 * EDGE
    layers = own.shape[0] // LANES
    for k in range(layers):
        part = pl.ds(top + k * EDGE, EDGE)
        full[pl.ds(k * size, EDGE), :] = before[part, :]
        full[pl.ds(k * size + EDGE, LANES), :] = own[pl.ds(k * LANES, LANES), :]
        full[pl.ds(k * size + EDGE + LANES, EDGE), :] = after[part, :]
    rows = LANES + 2 * EDGE
    total = count * rows
    found = flat_sides(xm[:, EDGE : EDGE + rows].reshape(total, LANES))
    sides[...] = found
    beside = pl.ds(count * EDGE, count)
    around = jnp.concatenate([before[beside, :], mats[...], after[beside, :]], axis=0)
    q = iota((1, total), 1)
    layer = lax.div(q, rows)
    row = q - layer * rows
    tile = jnp.where(row < EDGE, 0, jnp.where(row < LANES + EDGE, 1, 2))
    lane = row - EDGE + LANES * (1 - tile)
    spread = hot_of(iota((LANES, total), 0) == lane)
    named = dot(around.astype(BF16), spread, 1, 0)
    mine = iota((3 * count, total), 0) == tile * count + layer
    mat = jnp.sum(jnp.where(mine, named, 0.0), axis=0, keepdims=True)
    flat_mat[...] = jnp.broadcast_to(mat, (EDGE, total))
    heat_found = flat_sides(full[...])
    heat_sides[...] = heat_found
    third = total // 3
    ylow[:, pl.ds(0, total)] = found[:EDGE]
    yhigh[:, pl.ds(0, total)] = found[EDGE:]
    rest = jnp.zeros((2 * EDGE, third - layers * rows), F32)
    block = jnp.concatenate([heat_found, rest], axis=1)
    ylow[:, pl.ds(total, third)] = block[:EDGE]
    yhigh[:, pl.ds(total, third)] = block[EDGE:]
    for i in range(3):
        ylow[pl.ds(EDGE - 3 + i, 1), pl.ds(total, third)] = mat[:, i * third : (i + 1) * third]
        yhigh[pl.ds(i, 1), pl.ds(total, third)] = mat[:, i * third : (i + 1) * third]


def three_parts(v):
    high = v.astype(BF16)
    rest = v - high.astype(F32)
    mid = rest.astype(BF16)
    return high, mid, (rest - mid.astype(F32)).astype(BF16)


def ends_of(strip):
    return jnp.concatenate([strip[EDGE - 1 : EDGE], strip[3 * EDGE : 3 * EDGE + 1]], axis=0)


def end_lanes(depth, times):
    r, y = iota((depth, times * LANES), 0), iota((depth, times * LANES), 1)
    first = (r % 2 == 0) & (y == (r // 2) * LANES)
    last = (r % 2 == 1) & (y == (r // 2) * LANES + LANES - 1)
    return hot_of(first | last)


def turned(v, by, axis):
    return pltpu.roll(v, by % v.shape[axis], axis)


def strip_of(sides, before, after):
    return jnp.concatenate([before, sides, after], axis=0)


def pack_z_kernel(full, sides, before, after, out):
    n = full.shape[0]
    out[pl.ds(0, n), :] = full[...]
    at = before.shape[1] * 3 // 4
    strip = strip_of(sides[...], before[:, at : at + n], after[:, at : at + n])
    blocks = -(-n // LANES)
    strip = jnp.concatenate([strip, jnp.zeros((4 * EDGE, blocks * LANES - n), F32)], axis=1)
    for i in range(blocks):
        out[pl.ds(n + 4 * EDGE * i, 4 * EDGE), :] = strip[:, i * LANES : (i + 1) * LANES]


def weights_kernel(base, soft, heat, xm, sides, flat_mat, before, after, wz, wx, wy, wyw, inv, b0, strips, cond, cols, ends):
    count, rows = inv.shape[0], inv.shape[1]
    total = count * rows
    third = pl.ds(total, total // 3)
    mat = jnp.concatenate(
        [
            flat_mat[0:1],
            jnp.concatenate([before[pl.ds(i, 1), third] for i in range(3)], axis=1),
            jnp.concatenate([after[pl.ds(EDGE - 3 + i, 1), third] for i in range(3)], axis=1),
        ],
        axis=0,
    )
    tables = []
    for values in (base, soft, heat):
        found = jnp.zeros(mat.shape, F32)
        for m in range(values.shape[0]):
            found = jnp.where(mat == F32(m + 1), values[m], found)
        tables.append(found)
    own = [p for t in tables for p in three_parts(t[0:1])]
    r, y = iota((9, 3 * LANES), 0), iota((9, 3 * LANES), 1)
    cols[...] = dot(jnp.concatenate(own, axis=0), hot_of(lax.div(r, 3) == lax.div(y, LANES)), 0, 0)
    wide = lambda t, i: jnp.broadcast_to(t[i : i + 1], (EDGE, total))
    kb, ks, cf = (jnp.concatenate([wide(t, 1), wide(t, 0), wide(t, 0), wide(t, 2)], axis=0) for t in tables)
    sx = strip_of(sides[...], before[:, :total], after[:, :total])
    sc = kb / (1.0 + ks * sx)
    down = lambda by, axis: 0.5 * (sc + turned(sc, by, axis))
    around = [down(rows, 1), down(-rows, 1), down(1, 1), down(-1, 1), down(1, 0), down(-1, 0)]
    diag = cf
    for w in around:
        diag = diag + w
    si = jnp.where(cf > 0.0, 1.0 / diag, 0.0)
    for i, w in enumerate(around):
        strips[i] = w * si
    strips[6] = si
    strips[7] = cf * sx * si
    strips[8] = sx
    got = [dot(p, end_lanes(2, 1), 0, 0) for p in three_parts(ends_of(sc))]
    ends[...] = got[0] + got[1] + got[2]

    piece = 16
    blank = jnp.zeros((EDGE, LANES), F32)

    @pl.loop(0, count)
    def _(k):
        cond[k, pl.ds(0, EDGE)] = blank
        cond[k, pl.ds(rows + EDGE, EDGE)] = blank
        wx[k, pl.ds(0, EDGE)] = blank
        wx[k, pl.ds(rows + EDGE, EDGE)] = blank
        for at in range(0, rows, piece):
            part = pl.ds(pl.multiple_of(k * rows + at, 8), piece)
            x = xm[k, pl.ds(EDGE + at, piece)]
            cond[k, pl.ds(EDGE + at, piece)] = cols[part, 0:LANES] / (1.0 + cols[part, LANES : 2 * LANES] * x)

    first, last = iota((piece, LANES), 1) == 0, iota((piece, LANES), 1) == LANES - 1
    wz[0] = 0.5 * (cond[0, pl.ds(EDGE, rows)] + cond[1, pl.ds(EDGE, rows)])

    @pl.loop(1, count - 1)
    def _(k):
        for at in range(0, rows, piece):
            here = pl.ds(EDGE + at, piece)
            part = pl.ds(pl.multiple_of(k * rows + at, 8), piece)
            to = pl.ds(at, piece)
            c, end = cond[k, here], ends[part, :]
            up = 0.5 * (c + cond[k + 1, here])
            low = 0.5 * (c + cond[k - 1, here])
            right = 0.5 * (c + cond[k, pl.ds(EDGE + at + 1, piece)])
            left = 0.5 * (c + cond[k, pl.ds(EDGE + at - 1, piece)])
            e = 0.5 * (c + jnp.where(last, end, turned(c, -1, 1)))
            w = 0.5 * (c + jnp.where(first, end, turned(c, 1, 1)))
            cf = cols[part, 2 * LANES : 3 * LANES]
            diag = cf + up + low + right + left + e + w
            i = jnp.where(cf > 0.0, 1.0 / diag, 0.0)
            wz[k, to] = up
            wx[k, here] = right
            wy[k, to] = e
            wyw[k, to] = w
            inv[k, to] = i
            b0[k, to] = cf * xm[k, here] * i


def sweep_kernel(xm, wz, wx, wy, wyw, inv, b0, strips, low, own, high,
                 out, pull, full, b, d, xa, xb, ends):
    count, rows, _ = inv.shape
    total = count * rows
    factors = steps()

    layers = out.shape[0] // LANES
    n = layers * rows
    skip = (count - 3 * layers) // 2
    sb = jnp.zeros((4 * EDGE, total), F32)
    blocks = -(-n // LANES)
    blank = jnp.zeros((4 * EDGE, total - blocks * LANES), F32)
    for i, ref in enumerate((low, own, high)):
        start = skip + i * layers
        for k in range(layers):
            full[start + k] = ref[pl.ds(k * rows, rows), :]
        cells = [ref[pl.ds(n + 4 * EDGE * j, 4 * EDGE), :] for j in range(blocks)]
        sb = sb + turned(jnp.concatenate(cells + [blank], axis=1), start * rows, 1)
    for k in range(skip):
        full[k] = jnp.zeros((rows, LANES), F32)
        full[count - 1 - k] = jnp.zeros((rows, LANES), F32)
    sb = strips[7] + sb * strips[6]
    sx, sd = strips[8], None
    kept = [ends_of(sx)]
    for s, (keep, add) in enumerate(factors[:-1]):
        lanes = slice(s * LANES, total - s * LANES)
        part = lambda i: strips[i, :, lanes]
        near = part(0) * turned(sx, rows, 1) + part(1) * turned(sx, -rows, 1)
        near += part(2) * turned(sx, 1, 1) + part(3) * turned(sx, -1, 1)
        near += part(4) * turned(sx, 1, 0) + part(5) * turned(sx, -1, 0)
        step = add * (sb[:, lanes] - sx + near)
        sd = step if sd is None else step + keep * sd
        sx, sd = (sx + sd)[:, LANES:-LANES], sd[:, LANES:-LANES]
        kept.append(ends_of(sx))
    place_in = end_lanes(2, 1)
    place_in = jnp.concatenate([place_in, place_in], axis=0)
    for s, pair in enumerate(kept):
        start = (1 + s) * rows // LANES * LANES
        stop = -(-(count - 1 - s) * rows // LANES) * LANES
        ends[start:stop, s * LANES : (s + 1) * LANES] = dot(
            jnp.concatenate(parts(pair[:, start - s * LANES : stop - s * LANES]), axis=0), place_in, 0, 0)

    piece = 24
    first, last = iota((piece, LANES), 1) == 0, iota((piece, LANES), 1) == LANES - 1
    blank = jnp.zeros((EDGE, LANES), F32)

    @pl.loop(0, count)
    def _(k):
        for ref in (xa, xb):
            ref[k, pl.ds(0, EDGE)] = blank
            ref[k, pl.ds(rows + EDGE, EDGE)] = blank

    for s, (keep, add) in enumerate(factors):
        src, into = (xm if s == 0 else (xa if s % 2 else xb)), (xb if s % 2 else xa)

        @pl.loop(1 + s, count - 1 - s)
        def _(k):
            for at in range(0, rows, piece):
                here, to = pl.ds(EDGE + at, piece), pl.ds(at, piece)
                x = src[k, here]
                end = ends[pl.ds(pl.multiple_of(k * rows + at, 8), piece), s * LANES : (s + 1) * LANES]
                e = jnp.where(last, end, turned(x, -1, 1))
                w = jnp.where(first, end, turned(x, 1, 1))
                near = wz[k, to] * src[k + 1, here] + wz[k - 1, to] * src[k - 1, here]
                near += wx[k, here] * src[k, pl.ds(EDGE + at + 1, piece)]
                near += wx[k, pl.ds(EDGE + at - 1, piece)] * src[k, pl.ds(EDGE + at - 1, piece)]
                near += wy[k, to] * e + wyw[k, to] * w
                if s == 0:
                    rhs = b0[k, to] + full[k, to] * inv[k, to]
                    b[k, to] = rhs
                else:
                    rhs = b[k, to]
                step = add * (rhs - x + inv[k, to] * near)
                if s > 0:
                    step = step + keep * d[k, to]
                if s < SWEEPS - 1:
                    d[k, to] = step
                into[k, here] = x + step

    final = xb if SWEEPS % 2 == 0 else xa
    for k in range(4):
        out[pl.ds(k * LANES, LANES), :] = final[SWEEPS + k, pl.ds(2 * EDGE, LANES)]
    scale = 1.0
    for _, add in factors:
        scale = scale * add
    tile = pl.ds(EDGE, LANES)
    for i, (start, way) in enumerate(((1, 1), (count - 2, -1))):
        gain = scale * inv[start, tile]
        for j in range(1, SWEEPS):
            at = start + way * j
            gain = gain * inv[at, tile] * wz[at - 1 if way > 0 else at, tile]
        pull[pl.ds(i * LANES, LANES), :] = gain


def reply_kernel(x, pull, low2, high2, hot, out, replies):
    n = out.shape[0]
    first, last = pl.ds(0, LANES), pl.ds(n - LANES, LANES)
    out[...] = x[...]
    out[first, :] = x[first, :] + pull[pl.ds(0, LANES), :] * low2[...]
    out[last, :] = x[last, :] + pull[pl.ds(LANES, LANES), :] * high2[...]
    replies[...] = pick_rows(hot[...], out[...])


def final_kernel(returned, hot, gain, mob, mobility, ionization):
    back = pick_rows(hot[...], returned[...])
    mobility[...] = mob[...] * jnp.exp(-0.7 * back)
    ionization[...] = jnp.exp(gain[...] * (1.0 + 0.3 * back))


def shifted(v, axis, by):
    count = lax.axis_size(axis)
    pairs = [(i, i + by) for i in range(count) if 0 <= i + by < count]
    return lax.ppermute(v, axis, pairs) if pairs else jnp.zeros_like(v)


def exchanged(v):
    lines = v.reshape(v.shape[0], 1, v.shape[1])
    return lax.all_to_all(lines, ("gx", "gy"), split_axis=0, concat_axis=0, tiled=True).reshape(v.shape)


def per_device(
    efield, density, mobility_prev, thermal_prev, owner, block, live, material,
    mat_conductivity, mat_softening, mat_capacity,
):
    layers, xcells, width = density.shape
    n = layers * xcells
    peers = lax.axis_size("gx") * lax.axis_size("gy")
    slots = max(2, 2 * n // peers)
    line = peers * (slots + 1)
    flat = lambda a: a.reshape(n, width)
    ef = efield.reshape(3, n, width)
    den, mob, x0 = flat(density), flat(mobility_prev), flat(thermal_prev)
    own, blk, liv = owner.reshape(1, n), block.reshape(1, n), live.reshape(1, n)
    mat = material.reshape(layers, xcells)
    sized = lambda *s: (s, F32)

    given = [ef, den, mob, own, blk, liv]
    [sent] = call(
        functools.partial(dispatch_kernel, peers, slots), [sized(line, width)], given, "dispatch", flops=10**8, hbm=True, limit=60,
        scratch=[pltpu.VMEM(a.shape, a.dtype) for a in given] + [pltpu.SemaphoreType.DMA((len(given),))])
    received = exchanged(sent)

    far = SWEEPS - layers
    count = layers + 2 * SWEEPS
    rows = xcells + 2 * EDGE
    total = count * rows
    aside = sized(far * xcells + EDGE, width)
    near, up, down = call(
        functools.partial(start_z_kernel, far), [sized(n + EDGE, width), aside, aside], [x0, mat], "start_z")
    low, high = shifted(near, "gz", 1), shifted(near, "gz", -1)
    low2, high2 = shifted(up, "gz", 2), shifted(down, "gz", -2)
    gain, dest = call(functools.partial(after_kernel, slots), [sized(n, width), ((n, peers * slots), BF16)], [ef, own], "gain")
    edge = sized(count * (EDGE + 1), width)
    xz, mats, start_low, start_high = call(
        functools.partial(start_x_kernel, far), [sized(count, xcells, width), sized(count, width), edge, edge],
        [low2, low, near, high, high2], "start_x")
    received, start_low, start_high, gain, dest = lax.optimization_barrier(
        (received, start_low, start_high, gain, dest))

    source, first, last = call(
        functools.partial(combine_kernel, peers, slots), [sized(n, width)] + [sized(xcells, width)] * 2,
        [received], "combine", flops=10**8)
    [ids] = call(functools.partial(ids_kernel, peers, slots), [((peers * slots, n), BF16)], [received], "ids")
    edge = sized(count * (EDGE + 1) + layers * EDGE, width)
    xlow, xhigh = call(pack_x_kernel, [edge, edge], [source, start_low, start_high], "pack_x")
    before, after = shifted(xhigh, "gx", 1), shifted(xlow, "gx", -1)
    before, after, ids = lax.optimization_barrier((before, after, ids))
    tall, tile, flat_edge = sized(count, rows + 2 * EDGE, width), sized(count, rows, width), sized(2 * EDGE, total)
    inner = layers * rows
    y_edge = sized(EDGE, total + total // 3)
    xm, full, sides, heat_sides, flat_mat, ylow, yhigh = call(
        pack_y_kernel,
        [tall, sized(inner, width), flat_edge, sized(2 * EDGE, inner), sized(EDGE, total), y_edge, y_edge],
        [xz, mats, source, after, before], "pack_y")
    before, after = shifted(yhigh, "gy", 1), shifted(ylow, "gy", -1)
    blocks = -(-inner // LANES)
    [around] = call(
        pack_z_kernel, [sized(inner + 4 * EDGE * blocks, width)], [full, heat_sides, before, after], "pack_z")
    low, high = shifted(around, "gz", 1), shifted(around, "gz", -1)
    weights = call(
        weights_kernel, [tile, tall, tile, tile, tile, tile, sized(9, 4 * EDGE, total)],
        [mat_conductivity, mat_softening, mat_capacity, xm, sides, flat_mat, before, after], "weights",
        scratch=[pltpu.VMEM((count, rows + 2 * EDGE, width), F32), pltpu.VMEM((total, 3 * width), F32),
                 pltpu.VMEM((total, width), F32)],
        limit=32, flops=10**9, smem=(0, 1, 2))
    first, last, weights = lax.optimization_barrier((first, last, weights))
    low2, high2 = shifted(last, "gz", 2), shifted(first, "gz", -2)
    x, pull = call(
        sweep_kernel, [sized(n, width), sized(2 * xcells, width)],
        [xm] + list(weights) + [low, around, high], "sweeps",
        scratch=[pltpu.VMEM((count, rows, width), F32)] * 3 + [pltpu.VMEM((count, rows + 2 * EDGE, width), F32)] * 2
        + [pltpu.VMEM((total, SWEEPS * width), F32)],
        limit=36, flops=10**8)
    x, pull, low2, high2 = lax.optimization_barrier((x, pull, low2, high2))
    x, replies = call(
        reply_kernel, [sized(n, width), sized(peers * slots, width)], [x, pull, low2, high2, ids], "reply", flops=10**8)
    returned = exchanged(replies)
    mobility, ionization = call(final_kernel, [sized(n, width)] * 2, [returned, dest, gain, mob], "finish", flops=10**8)
    shape = density.shape
    return x.reshape(shape), mobility.reshape(shape), ionization.reshape(shape)


def solution(mesh):
    tile = P("gz", "gx", "gy")
    rows = P("gz", "gx", "gy", None)
    placed = (
        P(None, "gz", "gx", "gy"), tile, tile, tile,
        P("gz", "gx", "gy", None, None), rows, rows, rows, P(), P(), P(),
    )
    return jax.shard_map(
        per_device, mesh=mesh, in_specs=placed, out_specs=(tile, tile, tile), check_vma=False
    )
```

```python
import functools

import jax
import jax.numpy as jnp
from jax import lax
from jax.experimental import pallas as pl
from jax.experimental.pallas import tpu as pltpu
from jax.sharding import PartitionSpec as P

SWEEPS = 6
THETA = 1.01
DELTA = 0.99
LANES = 128
EDGE = 8
F32 = jnp.float32
BF16 = jnp.bfloat16
I32 = jnp.int32


def steps():
    sigma = THETA / DELTA
    rho = 1.0 / sigma
    found = [(0.0, 1.0 / THETA)]
    for _ in range(SWEEPS - 1):
        rho_new = 1.0 / (2.0 * sigma - rho)
        found.append((rho_new * rho, 2.0 * rho_new / DELTA))
        rho = rho_new
    return found


def iota(shape, dim):
    return lax.broadcasted_iota(I32, shape, dim)


def dot(a, b, ca, cb):
    return lax.dot_general(a, b, (((ca,), (cb,)), ((), ())), preferred_element_type=F32)


def parts(v):
    high = v.astype(BF16)
    return high, (v - high.astype(F32)).astype(BF16)


def pick_rows(hot, rows):
    high, low = parts(rows)
    got = dot(hot, jnp.concatenate([high, low], axis=1), 1, 0)
    width = rows.shape[1]
    return got[:, :width] + got[:, width:]


def column(row):
    same = iota((LANES, LANES), 0) == iota((LANES, LANES), 1)
    found = []
    for at in range(0, row.shape[1], LANES):
        piece = jnp.broadcast_to(row[:, at : at + LANES], (LANES, LANES))
        found.append(jnp.sum(jnp.where(same, piece, 0), axis=1, keepdims=True))
    return jnp.concatenate(found, axis=0)


def hot_of(cond):
    return jnp.where(cond, F32(1.0), F32(0.0)).astype(BF16)


def edge_lanes():
    r, y = iota((2 * EDGE, LANES), 0), iota((2 * EDGE, LANES), 1)
    return hot_of(y == jnp.where(r < EDGE, r, r + LANES - 2 * EDGE))


def call(kernel, outs, ins, name, scratch=(), limit=32, flops=0, smem=(), hbm=False):
    bytes_of = lambda a: a.size * a.dtype.itemsize
    return pl.pallas_call(
        kernel,
        out_shape=[jax.ShapeDtypeStruct(s, t) for s, t in outs],
        in_specs=[
            pl.BlockSpec(memory_space=pltpu.SMEM if i in smem else pltpu.HBM if hbm else pltpu.VMEM)
            for i in range(len(ins))
        ],
        out_specs=[pl.BlockSpec(memory_space=pltpu.VMEM) for _ in outs],
        scratch_shapes=list(scratch),
        compiler_params=pltpu.CompilerParams(vmem_limit_bytes=limit << 20),
        cost_estimate=pl.CostEstimate(
            flops=flops,
            bytes_accessed=sum(bytes_of(a) for a in ins)
            + sum(jax.ShapeDtypeStruct(s, t).size * 4 for s, t in outs),
            transcendentals=0,
        ),
        name=name,
    )(*ins)


def dispatch_kernel(peers, slots, *refs):
    far, out, near, sems = refs[:6], refs[6], refs[7:13], refs[13]
    copies = [pltpu.make_async_copy(a, b, sems.at[i]) for i, (a, b) in enumerate(zip(far, near))]
    for copy in copies[3:] + copies[:3]:
        copy.start()
    for copy in copies[3:]:
        copy.wait()
    ef, den, mob, owner, block, live = near
    n = owner.shape[1]
    own = owner[...]
    own_col = column(own)
    pos = jnp.zeros((1, n), I32)
    for at in range(0, n, LANES):
        r = iota((LANES, n), 0) + at
        earlier = (own_col[at : at + LANES] == own) & (r < iota((LANES, n), 1))
        pos = pos + jnp.sum(jnp.where(earlier, 1, 0), axis=0, keepdims=True)
    dest = own * (slots + 1) + pos
    hot = hot_of(iota((peers * (slots + 1), n), 0) == dest)
    named = hot_of(iota((peers, n), 0) == own)
    at_slot = iota((LANES, n), 0) == pos
    code = block[...] + 1
    high = jnp.where(at_slot, code // 32, 0).astype(F32).astype(BF16)
    low = jnp.where(at_slot, code % 32, 0).astype(F32).astype(BF16)
    labels = dot(named, high, 1, 1) * 32.0 + dot(named, low, 1, 1)
    live_col = column(live[...])
    for copy in copies[:3]:
        copy.wait()
    esq = ef[0] * ef[0] + ef[1] * ef[1] + ef[2] * ef[2]
    heat = 0.2 * den[...] * mob[...] * esq
    heat = jnp.where(iota(heat.shape, 1) < live_col, heat, F32(0.0))
    out[...] = pick_rows(hot, heat)
    out[pl.ds(slots, peers, stride=slots + 1), :] = labels


def after_kernel(slots, ef, owner, gain, hot):
    n = owner.shape[1]
    esq = ef[0] * ef[0] + ef[1] * ef[1] + ef[2] * ef[2]
    gain[...] = -2.0 * lax.rsqrt(esq + 1.0)
    own = owner[...]
    own_col = column(own)
    for at in range(0, n, LANES):
        r = iota((LANES, n), 0) + at
        piece = own_col[at : at + LANES]
        earlier = (piece == own) & (iota((LANES, n), 1) < r)
        pos = jnp.sum(jnp.where(earlier, 1, 0), axis=1, keepdims=True)
        size = (LANES, hot.shape[1])
        hot[pl.ds(at, LANES), :] = hot_of(jnp.broadcast_to(piece * slots + pos, size) == iota(size, 1))


def labels_of(received, peers, slots):
    got = received[pl.ds(slots, peers, stride=slots + 1), :]
    high = jnp.floor(got * (1.0 / 32.0))
    return high.astype(BF16), (got - 32.0 * high).astype(BF16)


def combine_kernel(peers, slots, received, source, first, last):
    n = source.shape[0]
    total = received.shape[0]
    high, low = labels_of(received, peers, slots)
    j = iota((LANES, total), 1)
    spread = hot_of(iota((LANES, total), 0) == j - (slots + 1) * lax.div(j, slots + 1))
    named = dot(high, spread, 1, 0) * 32.0 + dot(low, spread, 1, 0)
    mine = iota((peers, total), 0) == lax.div(iota((peers, total), 1), slots + 1)
    ids = jnp.sum(jnp.where(mine, named, 0.0), axis=0, keepdims=True).astype(I32)
    picks = hot_of(iota((n, total), 0) + 1 == ids)
    source[...] = pick_rows(picks, received[...])
    first[...] = source[pl.ds(0, LANES), :]
    last[...] = source[pl.ds(n - LANES, LANES), :]


def ids_kernel(peers, slots, received, hot):
    total = peers * slots
    high, low = labels_of(received, peers, slots)
    own = hot_of(lax.div(iota((total, peers), 0), slots) == iota((total, peers), 1))
    named = dot(own, high, 1, 0) * 32.0 + dot(own, low, 1, 0)
    i = iota((total, LANES), 0)
    mine = iota((total, LANES), 1) == i - slots * lax.div(i, slots)
    found = jnp.sum(jnp.where(mine, named, 0.0), axis=1, keepdims=True) - 1.0
    hot[...] = hot_of(jnp.broadcast_to(found.astype(I32), hot.shape) == iota(hot.shape, 1))


def start_z_kernel(far, x0, material, near, up, down):
    layers, xcells = material.shape
    n = layers * xcells
    mat = (material[...] + 1).astype(F32)
    rows = far * xcells
    zeros = lambda k: jnp.zeros((k, LANES), F32)
    near[pl.ds(0, n), :] = x0[...]
    near[pl.ds(n, EDGE), :] = jnp.concatenate([mat, zeros(EDGE - layers)], axis=0)
    up[pl.ds(0, rows), :] = x0[pl.ds(n - rows, rows), :]
    up[pl.ds(rows, EDGE), :] = jnp.concatenate([mat[layers - far :], zeros(EDGE - far)], axis=0)
    down[pl.ds(0, rows), :] = x0[pl.ds(0, rows), :]
    down[pl.ds(rows, EDGE), :] = jnp.concatenate([mat[:far], zeros(EDGE - far)], axis=0)


def start_x_kernel(far, low2, low, own, high, high2, xz, mats, xlow, xhigh):
    found = [(low2, k) for k in range(far)]
    for ref in (low, own, high):
        found += [(ref, k) for k in range(4)]
    found += [(high2, k) for k in range(far)]
    count = len(found)
    for k, (ref, at) in enumerate(found):
        piece = ref[pl.ds(at * LANES, LANES), :]
        xz[k] = piece
        xlow[pl.ds(k * EDGE, EDGE), :] = piece[:EDGE]
        xhigh[pl.ds(k * EDGE, EDGE), :] = piece[LANES - EDGE :]
        mats[pl.ds(k, 1), :] = ref[pl.ds(ref.shape[0] - EDGE + at, 1), :]
    xlow[pl.ds(count * EDGE, count), :] = mats[...]
    xhigh[pl.ds(count * EDGE, count), :] = mats[...]


def pack_x_kernel(source, start_low, start_high, xlow, xhigh):
    top = start_low.shape[0]
    xlow[pl.ds(0, top), :] = start_low[...]
    xhigh[pl.ds(0, top), :] = start_high[...]
    for k in range(source.shape[0] // LANES):
        to = pl.ds(top + k * EDGE, EDGE)
        xlow[to, :] = source[pl.ds(k * LANES, EDGE), :]
        xhigh[to, :] = source[pl.ds((k + 1) * LANES - EDGE, EDGE), :]


def flat_sides(rows):
    high, low = parts(rows)
    edges = edge_lanes()
    return dot(edges, high, 1, 1) + dot(edges, low, 1, 1)


def pack_y_kernel(xz, mats, own, after, before, xm, full, sides, heat_sides, flat_mat, ylow, yhigh):
    count = xz.shape[0]
    blank = jnp.zeros((EDGE, LANES), F32)
    for k in range(count):
        part = pl.ds(k * EDGE, EDGE)
        xm[k, pl.ds(0, EDGE)] = blank
        xm[k, pl.ds(EDGE, EDGE)] = before[part, :]
        xm[k, pl.ds(2 * EDGE, LANES)] = xz[k]
        xm[k, pl.ds(LANES + 2 * EDGE, EDGE)] = after[part, :]
        xm[k, pl.ds(LANES + 3 * EDGE, EDGE)] = blank
    top = count * (EDGE + 1)
    size = LANES + 2 * EDGE
    layers = own.shape[0] // LANES
    for k in range(layers):
        part = pl.ds(top + k * EDGE, EDGE)
        full[pl.ds(k * size, EDGE), :] = before[part, :]
        full[pl.ds(k * size + EDGE, LANES), :] = own[pl.ds(k * LANES, LANES), :]
        full[pl.ds(k * size + EDGE + LANES, EDGE), :] = after[part, :]
    rows = LANES + 2 * EDGE
    total = count * rows
    found = flat_sides(xm[:, EDGE : EDGE + rows].reshape(total, LANES))
    sides[...] = found
    beside = pl.ds(count * EDGE, count)
    around = jnp.concatenate([before[beside, :], mats[...], after[beside, :]], axis=0)
    q = iota((1, total), 1)
    layer = lax.div(q, rows)
    row = q - layer * rows
    tile = jnp.where(row < EDGE, 0, jnp.where(row < LANES + EDGE, 1, 2))
    lane = row - EDGE + LANES * (1 - tile)
    spread = hot_of(iota((LANES, total), 0) == lane)
    named = dot(around.astype(BF16), spread, 1, 0)
    mine = iota((3 * count, total), 0) == tile * count + layer
    mat = jnp.sum(jnp.where(mine, named, 0.0), axis=0, keepdims=True)
    flat_mat[...] = jnp.broadcast_to(mat, (EDGE, total))
    heat_found = flat_sides(full[...])
    heat_sides[...] = heat_found
    third = total // 3
    ylow[:, pl.ds(0, total)] = found[:EDGE]
    yhigh[:, pl.ds(0, total)] = found[EDGE:]
    rest = jnp.zeros((2 * EDGE, third - layers * rows), F32)
    block = jnp.concatenate([heat_found, rest], axis=1)
    ylow[:, pl.ds(total, third)] = block[:EDGE]
    yhigh[:, pl.ds(total, third)] = block[EDGE:]
    for i in range(3):
        ylow[pl.ds(EDGE - 3 + i, 1), pl.ds(total, third)] = mat[:, i * third : (i + 1) * third]
        yhigh[pl.ds(i, 1), pl.ds(total, third)] = mat[:, i * third : (i + 1) * third]


def three_parts(v):
    high = v.astype(BF16)
    rest = v - high.astype(F32)
    mid = rest.astype(BF16)
    return high, mid, (rest - mid.astype(F32)).astype(BF16)


def ends_of(strip):
    return jnp.concatenate([strip[EDGE - 1 : EDGE], strip[3 * EDGE : 3 * EDGE + 1]], axis=0)


def end_lanes(depth, times):
    r, y = iota((depth, times * LANES), 0), iota((depth, times * LANES), 1)
    first = (r % 2 == 0) & (y == (r // 2) * LANES)
    last = (r % 2 == 1) & (y == (r // 2) * LANES + LANES - 1)
    return hot_of(first | last)


def turned(v, by, axis):
    return pltpu.roll(v, by % v.shape[axis], axis)


def strip_of(sides, before, after):
    return jnp.concatenate([before, sides, after], axis=0)


def pack_z_kernel(full, sides, before, after, out):
    n = full.shape[0]
    out[pl.ds(0, n), :] = full[...]
    at = before.shape[1] * 3 // 4
    strip = strip_of(sides[...], before[:, at : at + n], after[:, at : at + n])
    blocks = -(-n // LANES)
    strip = jnp.concatenate([strip, jnp.zeros((4 * EDGE, blocks * LANES - n), F32)], axis=1)
    for i in range(blocks):
        out[pl.ds(n + 4 * EDGE * i, 4 * EDGE), :] = strip[:, i * LANES : (i + 1) * LANES]


def weights_kernel(base, soft, heat, xm, sides, flat_mat, before, after, wz, wx, wy, wyw, inv, b0, strips, cond, cols, ends):
    count, rows = inv.shape[0], inv.shape[1]
    total = count * rows
    third = pl.ds(total, total // 3)
    mat = jnp.concatenate(
        [
            flat_mat[0:1],
            jnp.concatenate([before[pl.ds(i, 1), third] for i in range(3)], axis=1),
            jnp.concatenate([after[pl.ds(EDGE - 3 + i, 1), third] for i in range(3)], axis=1),
        ],
        axis=0,
    )
    tables = []
    for values in (base, soft, heat):
        found = jnp.zeros(mat.shape, F32)
        for m in range(values.shape[0]):
            found = jnp.where(mat == F32(m + 1), values[m], found)
        tables.append(found)
    own = [p for t in tables for p in three_parts(t[0:1])]
    r, y = iota((9, 3 * LANES), 0), iota((9, 3 * LANES), 1)
    cols[...] = dot(jnp.concatenate(own, axis=0), hot_of(lax.div(r, 3) == lax.div(y, LANES)), 0, 0)
    wide = lambda t, i: jnp.broadcast_to(t[i : i + 1], (EDGE, total))
    kb, ks, cf = (jnp.concatenate([wide(t, 1), wide(t, 0), wide(t, 0), wide(t, 2)], axis=0) for t in tables)
    sx = strip_of(sides[...], before[:, :total], after[:, :total])
    sc = kb / (1.0 + ks * sx)
    down = lambda by, axis: 0.5 * (sc + turned(sc, by, axis))
    around = [down(rows, 1), down(-rows, 1), down(1, 1), down(-1, 1), down(1, 0), down(-1, 0)]
    diag = cf
    for w in around:
        diag = diag + w
    si = jnp.where(cf > 0.0, 1.0 / diag, 0.0)
    for i, w in enumerate(around):
        strips[i] = w * si
    strips[6] = si
    strips[7] = cf * sx * si
    strips[8] = sx
    got = [dot(p, end_lanes(2, 1), 0, 0) for p in three_parts(ends_of(sc))]
    ends[...] = got[0] + got[1] + got[2]

    piece = 16
    blank = jnp.zeros((EDGE, LANES), F32)

    @pl.loop(0, count)
    def _(k):
        cond[k, pl.ds(0, EDGE)] = blank
        cond[k, pl.ds(rows + EDGE, EDGE)] = blank
        wx[k, pl.ds(0, EDGE)] = blank
        wx[k, pl.ds(rows + EDGE, EDGE)] = blank
        for at in range(0, rows, piece):
            part = pl.ds(pl.multiple_of(k * rows + at, 8), piece)
            x = xm[k, pl.ds(EDGE + at, piece)]
            cond[k, pl.ds(EDGE + at, piece)] = cols[part, 0:LANES] / (1.0 + cols[part, LANES : 2 * LANES] * x)

    first, last = iota((piece, LANES), 1) == 0, iota((piece, LANES), 1) == LANES - 1
    wz[0] = 0.5 * (cond[0, pl.ds(EDGE, rows)] + cond[1, pl.ds(EDGE, rows)])

    @pl.loop(1, count - 1)
    def _(k):
        for at in range(0, rows, piece):
            here = pl.ds(EDGE + at, piece)
            part = pl.ds(pl.multiple_of(k * rows + at, 8), piece)
            to = pl.ds(at, piece)
            c, end = cond[k, here], ends[part, :]
            up = 0.5 * (c + cond[k + 1, here])
            low = 0.5 * (c + cond[k - 1, here])
            right = 0.5 * (c + cond[k, pl.ds(EDGE + at + 1, piece)])
            left = 0.5 * (c + cond[k, pl.ds(EDGE + at - 1, piece)])
            e = 0.5 * (c + jnp.where(last, end, turned(c, -1, 1)))
            w = 0.5 * (c + jnp.where(first, end, turned(c, 1, 1)))
            cf = cols[part, 2 * LANES : 3 * LANES]
            diag = cf + up + low + right + left + e + w
            i = jnp.where(cf > 0.0, 1.0 / diag, 0.0)
            wz[k, to] = up
            wx[k, here] = right
            wy[k, to] = e
            wyw[k, to] = w
            inv[k, to] = i
            b0[k, to] = cf * xm[k, here] * i


def sweep_kernel(xm, wz, wx, wy, wyw, inv, b0, strips, low, own, high,
                 out, pull, full, b, d, xa, xb, ends):
    count, rows, _ = inv.shape
    total = count * rows
    factors = steps()

    layers = out.shape[0] // LANES
    n = layers * rows
    skip = (count - 3 * layers) // 2
    sb = jnp.zeros((4 * EDGE, total), F32)
    blocks = -(-n // LANES)
    blank = jnp.zeros((4 * EDGE, total - blocks * LANES), F32)
    for i, ref in enumerate((low, own, high)):
        start = skip + i * layers
        for k in range(layers):
            full[start + k] = ref[pl.ds(k * rows, rows), :]
        cells = [ref[pl.ds(n + 4 * EDGE * j, 4 * EDGE), :] for j in range(blocks)]
        sb = sb + turned(jnp.concatenate(cells + [blank], axis=1), start * rows, 1)
    for k in range(skip):
        full[k] = jnp.zeros((rows, LANES), F32)
        full[count - 1 - k] = jnp.zeros((rows, LANES), F32)
    sb = strips[7] + sb * strips[6]
    sx, sd = strips[8], None
    kept = [ends_of(sx)]
    for s, (keep, add) in enumerate(factors[:-1]):
        lanes = slice(s * LANES, total - s * LANES)
        part = lambda i: strips[i, :, lanes]
        near = part(0) * turned(sx, rows, 1) + part(1) * turned(sx, -rows, 1)
        near += part(2) * turned(sx, 1, 1) + part(3) * turned(sx, -1, 1)
        near += part(4) * turned(sx, 1, 0) + part(5) * turned(sx, -1, 0)
        step = add * (sb[:, lanes] - sx + near)
        sd = step if sd is None else step + keep * sd
        sx, sd = (sx + sd)[:, LANES:-LANES], sd[:, LANES:-LANES]
        kept.append(ends_of(sx))
    place_in = end_lanes(2, 1)
    place_in = jnp.concatenate([place_in, place_in], axis=0)
    for s, pair in enumerate(kept):
        start = (1 + s) * rows // LANES * LANES
        stop = -(-(count - 1 - s) * rows // LANES) * LANES
        ends[start:stop, s * LANES : (s + 1) * LANES] = dot(
            jnp.concatenate(parts(pair[:, start - s * LANES : stop - s * LANES]), axis=0), place_in, 0, 0)

    piece = 24
    first, last = iota((piece, LANES), 1) == 0, iota((piece, LANES), 1) == LANES - 1
    blank = jnp.zeros((EDGE, LANES), F32)

    @pl.loop(0, count)
    def _(k):
        for ref in (xa, xb):
            ref[k, pl.ds(0, EDGE)] = blank
            ref[k, pl.ds(rows + EDGE, EDGE)] = blank

    for s, (keep, add) in enumerate(factors):
        src, into = (xm if s == 0 else (xa if s % 2 else xb)), (xb if s % 2 else xa)

        @pl.loop(1 + s, count - 1 - s)
        def _(k):
            for at in range(0, rows, piece):
                here, to = pl.ds(EDGE + at, piece), pl.ds(at, piece)
                x = src[k, here]
                end = ends[pl.ds(pl.multiple_of(k * rows + at, 8), piece), s * LANES : (s + 1) * LANES]
                e = jnp.where(last, end, turned(x, -1, 1))
                w = jnp.where(first, end, turned(x, 1, 1))
                near = wz[k, to] * src[k + 1, here] + wz[k - 1, to] * src[k - 1, here]
                near += wx[k, here] * src[k, pl.ds(EDGE + at + 1, piece)]
                near += wx[k, pl.ds(EDGE + at - 1, piece)] * src[k, pl.ds(EDGE + at - 1, piece)]
                near += wy[k, to] * e + wyw[k, to] * w
                if s == 0:
                    rhs = b0[k, to] + full[k, to] * inv[k, to]
                    b[k, to] = rhs
                else:
                    rhs = b[k, to]
                step = add * (rhs - x + inv[k, to] * near)
                if s > 0:
                    step = step + keep * d[k, to]
                if s < SWEEPS - 1:
                    d[k, to] = step
                into[k, here] = x + step

    final = xb if SWEEPS % 2 == 0 else xa
    for k in range(4):
        out[pl.ds(k * LANES, LANES), :] = final[SWEEPS + k, pl.ds(2 * EDGE, LANES)]
    scale = 1.0
    for _, add in factors:
        scale = scale * add
    tile = pl.ds(EDGE, LANES)
    for i, (start, way) in enumerate(((1, 1), (count - 2, -1))):
        gain = scale * inv[start, tile]
        for j in range(1, SWEEPS):
            at = start + way * j
            gain = gain * inv[at, tile] * wz[at - 1 if way > 0 else at, tile]
        pull[pl.ds(i * LANES, LANES), :] = gain


def reply_kernel(x, pull, low2, high2, hot, out, replies):
    n = out.shape[0]
    first, last = pl.ds(0, LANES), pl.ds(n - LANES, LANES)
    out[...] = x[...]
    out[first, :] = x[first, :] + pull[pl.ds(0, LANES), :] * low2[...]
    out[last, :] = x[last, :] + pull[pl.ds(LANES, LANES), :] * high2[...]
    replies[...] = pick_rows(hot[...], out[...])


def final_kernel(returned, hot, gain, mob, mobility, ionization):
    back = pick_rows(hot[...], returned[...])
    mobility[...] = mob[...] * jnp.exp(-0.7 * back)
    ionization[...] = jnp.exp(gain[...] * (1.0 + 0.3 * back))


def shifted(v, axis, by):
    count = lax.axis_size(axis)
    pairs = [(i, i + by) for i in range(count) if 0 <= i + by < count]
    return lax.ppermute(v, axis, pairs) if pairs else jnp.zeros_like(v)


def swapped(a, b, axis):
    count = lax.axis_size(axis)
    found = []
    for v, odd in ((a, 0), (b, 1)):
        pairs = [p for i in range(odd, count - 1, 2) for p in ((i, i + 1), (i + 1, i))]
        found.append(lax.ppermute(v, axis, pairs) if pairs else jnp.zeros_like(v))
    return found


def exchanged(v):
    lines = v.reshape(v.shape[0], 1, v.shape[1])
    return lax.all_to_all(lines, ("gx", "gy"), split_axis=0, concat_axis=0, tiled=True).reshape(v.shape)


def per_device(
    efield, density, mobility_prev, thermal_prev, owner, block, live, material,
    mat_conductivity, mat_softening, mat_capacity,
):
    layers, xcells, width = density.shape
    n = layers * xcells
    peers = lax.axis_size("gx") * lax.axis_size("gy")
    slots = max(2, 2 * n // peers)
    line = peers * (slots + 1)
    flat = lambda a: a.reshape(n, width)
    ef = efield.reshape(3, n, width)
    den, mob, x0 = flat(density), flat(mobility_prev), flat(thermal_prev)
    own, blk, liv = owner.reshape(1, n), block.reshape(1, n), live.reshape(1, n)
    mat = material.reshape(layers, xcells)
    sized = lambda *s: (s, F32)

    given = [ef, den, mob, own, blk, liv]
    [sent] = call(
        functools.partial(dispatch_kernel, peers, slots), [sized(line, width)], given, "dispatch", flops=10**8, hbm=True, limit=60,
        scratch=[pltpu.VMEM(a.shape, a.dtype) for a in given] + [pltpu.SemaphoreType.DMA((len(given),))])
    received = exchanged(sent)

    far = SWEEPS - layers
    count = layers + 2 * SWEEPS
    rows = xcells + 2 * EDGE
    total = count * rows
    aside = sized(far * xcells + EDGE, width)
    near, up, down = call(
        functools.partial(start_z_kernel, far), [sized(n + EDGE, width), aside, aside], [x0, mat], "start_z")
    low, high = shifted(near, "gz", 1), shifted(near, "gz", -1)
    low2, high2 = shifted(up, "gz", 2), shifted(down, "gz", -2)
    gain, dest = call(functools.partial(after_kernel, slots), [sized(n, width), ((n, peers * slots), BF16)], [ef, own], "gain")
    edge = sized(count * (EDGE + 1), width)
    xz, mats, start_low, start_high = call(
        functools.partial(start_x_kernel, far), [sized(count, xcells, width), sized(count, width), edge, edge],
        [low2, low, near, high, high2], "start_x")
    received, start_low, start_high, gain, dest = lax.optimization_barrier(
        (received, start_low, start_high, gain, dest))

    source, first, last = call(
        functools.partial(combine_kernel, peers, slots), [sized(n, width)] + [sized(xcells, width)] * 2,
        [received], "combine", flops=10**8)
    [ids] = call(functools.partial(ids_kernel, peers, slots), [((peers * slots, n), BF16)], [received], "ids")
    edge = sized(count * (EDGE + 1) + layers * EDGE, width)
    xlow, xhigh = call(pack_x_kernel, [edge, edge], [source, start_low, start_high], "pack_x")
    before, after = shifted(xhigh, "gx", 1), shifted(xlow, "gx", -1)
    before, after, ids = lax.optimization_barrier((before, after, ids))
    tall, tile, flat_edge = sized(count, rows + 2 * EDGE, width), sized(count, rows, width), sized(2 * EDGE, total)
    inner = layers * rows
    y_edge = sized(EDGE, total + total // 3)
    xm, full, sides, heat_sides, flat_mat, ylow, yhigh = call(
        pack_y_kernel,
        [tall, sized(inner, width), flat_edge, sized(2 * EDGE, inner), sized(EDGE, total), y_edge, y_edge],
        [xz, mats, source, after, before], "pack_y")
    even = lax.axis_index("gy") % 2 == 0
    one, two = swapped(jnp.where(even, yhigh, ylow), jnp.where(even, ylow, yhigh), "gy")
    before, after = jnp.where(even, two, one), jnp.where(even, one, two)
    blocks = -(-inner // LANES)
    [around] = call(
        pack_z_kernel, [sized(inner + 4 * EDGE * blocks, width)], [full, heat_sides, before, after], "pack_z")
    low, high = shifted(around, "gz", 1), shifted(around, "gz", -1)
    weights = call(
        weights_kernel, [tile, tall, tile, tile, tile, tile, sized(9, 4 * EDGE, total)],
        [mat_conductivity, mat_softening, mat_capacity, xm, sides, flat_mat, before, after], "weights",
        scratch=[pltpu.VMEM((count, rows + 2 * EDGE, width), F32), pltpu.VMEM((total, 3 * width), F32),
                 pltpu.VMEM((total, width), F32)],
        limit=32, flops=10**9, smem=(0, 1, 2))
    first, last, weights = lax.optimization_barrier((first, last, weights))
    low2, high2 = shifted(last, "gz", 2), shifted(first, "gz", -2)
    x, pull = call(
        sweep_kernel, [sized(n, width), sized(2 * xcells, width)],
        [xm] + list(weights) + [low, around, high], "sweeps",
        scratch=[pltpu.VMEM((count, rows, width), F32)] * 3 + [pltpu.VMEM((count, rows + 2 * EDGE, width), F32)] * 2
        + [pltpu.VMEM((total, SWEEPS * width), F32)],
        limit=36, flops=10**8)
    x, pull, low2, high2 = lax.optimization_barrier((x, pull, low2, high2))
    x, replies = call(
        reply_kernel, [sized(n, width), sized(peers * slots, width)], [x, pull, low2, high2, ids], "reply", flops=10**8)
    returned = exchanged(replies)
    mobility, ionization = call(final_kernel, [sized(n, width)] * 2, [returned, dest, gain, mob], "finish", flops=10**8)
    shape = density.shape
    return x.reshape(shape), mobility.reshape(shape), ionization.reshape(shape)


def solution(mesh):
    tile = P("gz", "gx", "gy")
    rows = P("gz", "gx", "gy", None)
    placed = (
        P(None, "gz", "gx", "gy"), tile, tile, tile,
        P("gz", "gx", "gy", None, None), rows, rows, rows, P(), P(), P(),
    )
    return jax.shard_map(
        per_device, mesh=mesh, in_specs=placed, out_specs=(tile, tile, tile), check_vma=False
    )
```

```python
import functools

import jax
import jax.numpy as jnp
from jax import lax
from jax.experimental import pallas as pl
from jax.experimental.pallas import tpu as pltpu
from jax.sharding import PartitionSpec as P

SWEEPS = 6
THETA = 1.01
DELTA = 0.99
LANES = 128
EDGE = 8
F32 = jnp.float32
BF16 = jnp.bfloat16
I32 = jnp.int32


def steps():
    sigma = THETA / DELTA
    rho = 1.0 / sigma
    found = [(0.0, 1.0 / THETA)]
    for _ in range(SWEEPS - 1):
        rho_new = 1.0 / (2.0 * sigma - rho)
        found.append((rho_new * rho, 2.0 * rho_new / DELTA))
        rho = rho_new
    return found


def iota(shape, dim):
    return lax.broadcasted_iota(I32, shape, dim)


def dot(a, b, ca, cb):
    return lax.dot_general(a, b, (((ca,), (cb,)), ((), ())), preferred_element_type=F32)


def parts(v):
    high = v.astype(BF16)
    return high, (v - high.astype(F32)).astype(BF16)


def pick_rows(hot, rows):
    high, low = parts(rows)
    got = dot(hot, jnp.concatenate([high, low], axis=1), 1, 0)
    width = rows.shape[1]
    return got[:, :width] + got[:, width:]


def column(row):
    same = iota((LANES, LANES), 0) == iota((LANES, LANES), 1)
    found = []
    for at in range(0, row.shape[1], LANES):
        piece = jnp.broadcast_to(row[:, at : at + LANES], (LANES, LANES))
        found.append(jnp.sum(jnp.where(same, piece, 0), axis=1, keepdims=True))
    return jnp.concatenate(found, axis=0)


def hot_of(cond):
    return jnp.where(cond, F32(1.0), F32(0.0)).astype(BF16)


def edge_lanes():
    r, y = iota((2 * EDGE, LANES), 0), iota((2 * EDGE, LANES), 1)
    return hot_of(y == jnp.where(r < EDGE, r, r + LANES - 2 * EDGE))


def call(kernel, outs, ins, name, scratch=(), limit=32, flops=0, smem=(), hbm=False):
    bytes_of = lambda a: a.size * a.dtype.itemsize
    return pl.pallas_call(
        kernel,
        out_shape=[jax.ShapeDtypeStruct(s, t) for s, t in outs],
        in_specs=[
            pl.BlockSpec(memory_space=pltpu.SMEM if i in smem else pltpu.HBM if hbm else pltpu.VMEM)
            for i in range(len(ins))
        ],
        out_specs=[pl.BlockSpec(memory_space=pltpu.VMEM) for _ in outs],
        scratch_shapes=list(scratch),
        compiler_params=pltpu.CompilerParams(vmem_limit_bytes=limit << 20),
        cost_estimate=pl.CostEstimate(
            flops=flops,
            bytes_accessed=sum(bytes_of(a) for a in ins)
            + sum(jax.ShapeDtypeStruct(s, t).size * 4 for s, t in outs),
            transcendentals=0,
        ),
        name=name,
    )(*ins)


def dispatch_kernel(peers, slots, *refs):
    far, out, near, sems = refs[:6], refs[6], refs[7:13], refs[13]
    copies = [pltpu.make_async_copy(a, b, sems.at[i]) for i, (a, b) in enumerate(zip(far, near))]
    for copy in copies[3:] + copies[:3]:
        copy.start()
    for copy in copies[3:]:
        copy.wait()
    ef, den, mob, owner, block, live = near
    n = owner.shape[1]
    own = owner[...]
    own_col = column(own)
    pos = jnp.zeros((1, n), I32)
    for at in range(0, n, LANES):
        r = iota((LANES, n), 0) + at
        earlier = (own_col[at : at + LANES] == own) & (r < iota((LANES, n), 1))
        pos = pos + jnp.sum(jnp.where(earlier, 1, 0), axis=0, keepdims=True)
    dest = own * (slots + 1) + pos
    hot = hot_of(iota((peers * (slots + 1), n), 0) == dest)
    named = hot_of(iota((peers, n), 0) == own)
    at_slot = iota((LANES, n), 0) == pos
    code = block[...] + 1
    high = jnp.where(at_slot, code // 32, 0).astype(F32).astype(BF16)
    low = jnp.where(at_slot, code % 32, 0).astype(F32).astype(BF16)
    labels = dot(named, high, 1, 1) * 32.0 + dot(named, low, 1, 1)
    live_col = column(live[...])
    for copy in copies[:3]:
        copy.wait()
    esq = ef[0] * ef[0] + ef[1] * ef[1] + ef[2] * ef[2]
    heat = 0.2 * den[...] * mob[...] * esq
    heat = jnp.where(iota(heat.shape, 1) < live_col, heat, F32(0.0))
    out[...] = pick_rows(hot, heat)
    out[pl.ds(slots, peers, stride=slots + 1), :] = labels


def after_kernel(slots, ef, owner, gain, hot):
    n = owner.shape[1]
    esq = ef[0] * ef[0] + ef[1] * ef[1] + ef[2] * ef[2]
    gain[...] = -2.0 * lax.rsqrt(esq + 1.0)
    own = owner[...]
    own_col = column(own)
    for at in range(0, n, LANES):
        r = iota((LANES, n), 0) + at
        piece = own_col[at : at + LANES]
        earlier = (piece == own) & (iota((LANES, n), 1) < r)
        pos = jnp.sum(jnp.where(earlier, 1, 0), axis=1, keepdims=True)
        size = (LANES, hot.shape[1])
        hot[pl.ds(at, LANES), :] = hot_of(jnp.broadcast_to(piece * slots + pos, size) == iota(size, 1))


def labels_of(received, peers, slots):
    got = received[pl.ds(slots, peers, stride=slots + 1), :]
    high = jnp.floor(got * (1.0 / 32.0))
    return high.astype(BF16), (got - 32.0 * high).astype(BF16)


def combine_kernel(peers, slots, received, source, first, last):
    n = source.shape[0]
    total = received.shape[0]
    high, low = labels_of(received, peers, slots)
    j = iota((LANES, total), 1)
    spread = hot_of(iota((LANES, total), 0) == j - (slots + 1) * lax.div(j, slots + 1))
    named = dot(high, spread, 1, 0) * 32.0 + dot(low, spread, 1, 0)
    mine = iota((peers, total), 0) == lax.div(iota((peers, total), 1), slots + 1)
    ids = jnp.sum(jnp.where(mine, named, 0.0), axis=0, keepdims=True).astype(I32)
    picks = hot_of(iota((n, total), 0) + 1 == ids)
    source[...] = pick_rows(picks, received[...])
    first[...] = source[pl.ds(0, LANES), :]
    last[...] = source[pl.ds(n - LANES, LANES), :]


def ids_kernel(peers, slots, received, hot):
    total = peers * slots
    high, low = labels_of(received, peers, slots)
    own = hot_of(lax.div(iota((total, peers), 0), slots) == iota((total, peers), 1))
    named = dot(own, high, 1, 0) * 32.0 + dot(own, low, 1, 0)
    i = iota((total, LANES), 0)
    mine = iota((total, LANES), 1) == i - slots * lax.div(i, slots)
    found = jnp.sum(jnp.where(mine, named, 0.0), axis=1, keepdims=True) - 1.0
    hot[...] = hot_of(jnp.broadcast_to(found.astype(I32), hot.shape) == iota(hot.shape, 1))


def start_z_kernel(far, x0, material, near, up, down):
    layers, xcells = material.shape
    n = layers * xcells
    mat = (material[...] + 1).astype(F32)
    rows = far * xcells
    zeros = lambda k: jnp.zeros((k, LANES), F32)
    near[pl.ds(0, n), :] = x0[...]
    near[pl.ds(n, EDGE), :] = jnp.concatenate([mat, zeros(EDGE - layers)], axis=0)
    up[pl.ds(0, rows), :] = x0[pl.ds(n - rows, rows), :]
    up[pl.ds(rows, EDGE), :] = jnp.concatenate([mat[layers - far :], zeros(EDGE - far)], axis=0)
    down[pl.ds(0, rows), :] = x0[pl.ds(0, rows), :]
    down[pl.ds(rows, EDGE), :] = jnp.concatenate([mat[:far], zeros(EDGE - far)], axis=0)


def start_x_kernel(far, low2, low, own, high, high2, xz, mats, xlow, xhigh):
    found = [(low2, k) for k in range(far)]
    for ref in (low, own, high):
        found += [(ref, k) for k in range(4)]
    found += [(high2, k) for k in range(far)]
    count = len(found)
    for k, (ref, at) in enumerate(found):
        piece = ref[pl.ds(at * LANES, LANES), :]
        xz[k] = piece
        xlow[pl.ds(k * EDGE, EDGE), :] = piece[:EDGE]
        xhigh[pl.ds(k * EDGE, EDGE), :] = piece[LANES - EDGE :]
        mats[pl.ds(k, 1), :] = ref[pl.ds(ref.shape[0] - EDGE + at, 1), :]
    xlow[pl.ds(count * EDGE, count), :] = mats[...]
    xhigh[pl.ds(count * EDGE, count), :] = mats[...]


def pack_x_kernel(source, start_low, start_high, xlow, xhigh):
    top = start_low.shape[0]
    xlow[pl.ds(0, top), :] = start_low[...]
    xhigh[pl.ds(0, top), :] = start_high[...]
    for k in range(source.shape[0] // LANES):
        to = pl.ds(top + k * EDGE, EDGE)
        xlow[to, :] = source[pl.ds(k * LANES, EDGE), :]
        xhigh[to, :] = source[pl.ds((k + 1) * LANES - EDGE, EDGE), :]


def flat_sides(rows):
    high, low = parts(rows)
    edges = edge_lanes()
    return dot(edges, high, 1, 1) + dot(edges, low, 1, 1)


def pack_y_kernel(xz, mats, own, after, before, xm, full, sides, heat_sides, flat_mat, ylow, yhigh):
    count = xz.shape[0]
    blank = jnp.zeros((EDGE, LANES), F32)
    for k in range(count):
        part = pl.ds(k * EDGE, EDGE)
        xm[k, pl.ds(0, EDGE)] = blank
        xm[k, pl.ds(EDGE, EDGE)] = before[part, :]
        xm[k, pl.ds(2 * EDGE, LANES)] = xz[k]
        xm[k, pl.ds(LANES + 2 * EDGE, EDGE)] = after[part, :]
        xm[k, pl.ds(LANES + 3 * EDGE, EDGE)] = blank
    top = count * (EDGE + 1)
    size = LANES + 2 * EDGE
    layers = own.shape[0] // LANES
    for k in range(layers):
        part = pl.ds(top + k * EDGE, EDGE)
        full[pl.ds(k * size, EDGE), :] = before[part, :]
        full[pl.ds(k * size + EDGE, LANES), :] = own[pl.ds(k * LANES, LANES), :]
        full[pl.ds(k * size + EDGE + LANES, EDGE), :] = after[part, :]
    rows = LANES + 2 * EDGE
    total = count * rows
    found = flat_sides(xm[:, EDGE : EDGE + rows].reshape(total, LANES))
    sides[...] = found
    beside = pl.ds(count * EDGE, count)
    around = jnp.concatenate([before[beside, :], mats[...], after[beside, :]], axis=0)
    q = iota((1, total), 1)
    layer = lax.div(q, rows)
    row = q - layer * rows
    tile = jnp.where(row < EDGE, 0, jnp.where(row < LANES + EDGE, 1, 2))
    lane = row - EDGE + LANES * (1 - tile)
    spread = hot_of(iota((LANES, total), 0) == lane)
    named = dot(around.astype(BF16), spread, 1, 0)
    mine = iota((3 * count, total), 0) == tile * count + layer
    mat = jnp.sum(jnp.where(mine, named, 0.0), axis=0, keepdims=True)
    flat_mat[...] = jnp.broadcast_to(mat, (EDGE, total))
    heat_found = flat_sides(full[...])
    heat_sides[...] = heat_found
    third = total // 3
    ylow[:, pl.ds(0, total)] = found[:EDGE]
    yhigh[:, pl.ds(0, total)] = found[EDGE:]
    rest = jnp.zeros((2 * EDGE, third - layers * rows), F32)
    block = jnp.concatenate([heat_found, rest], axis=1)
    ylow[:, pl.ds(total, third)] = block[:EDGE]
    yhigh[:, pl.ds(total, third)] = block[EDGE:]
    for i in range(3):
        ylow[pl.ds(EDGE - 3 + i, 1), pl.ds(total, third)] = mat[:, i * third : (i + 1) * third]
        yhigh[pl.ds(i, 1), pl.ds(total, third)] = mat[:, i * third : (i + 1) * third]


def three_parts(v):
    high = v.astype(BF16)
    rest = v - high.astype(F32)
    mid = rest.astype(BF16)
    return high, mid, (rest - mid.astype(F32)).astype(BF16)


def ends_of(strip):
    return jnp.concatenate([strip[EDGE - 1 : EDGE], strip[3 * EDGE : 3 * EDGE + 1]], axis=0)


def end_lanes(depth, times):
    r, y = iota((depth, times * LANES), 0), iota((depth, times * LANES), 1)
    first = (r % 2 == 0) & (y == (r // 2) * LANES)
    last = (r % 2 == 1) & (y == (r // 2) * LANES + LANES - 1)
    return hot_of(first | last)


def turned(v, by, axis):
    return pltpu.roll(v, by % v.shape[axis], axis)


def strip_of(sides, before, after):
    return jnp.concatenate([before, sides, after], axis=0)


def pack_z_kernel(full, sides, before, after, out):
    n = full.shape[0]
    out[pl.ds(0, n), :] = full[...]
    at = before.shape[1] * 3 // 4
    strip = strip_of(sides[...], before[:, at : at + n], after[:, at : at + n])
    blocks = -(-n // LANES)
    strip = jnp.concatenate([strip, jnp.zeros((4 * EDGE, blocks * LANES - n), F32)], axis=1)
    for i in range(blocks):
        out[pl.ds(n + 4 * EDGE * i, 4 * EDGE), :] = strip[:, i * LANES : (i + 1) * LANES]


def weights_kernel(base, soft, heat, xm, sides, flat_mat, before, after, wz, wx, wy, wyw, inv, b0, strips, cond, cols, ends):
    count, rows = inv.shape[0], inv.shape[1]
    total = count * rows
    third = pl.ds(total, total // 3)
    mat = jnp.concatenate(
        [
            flat_mat[0:1],
            jnp.concatenate([before[pl.ds(i, 1), third] for i in range(3)], axis=1),
            jnp.concatenate([after[pl.ds(EDGE - 3 + i, 1), third] for i in range(3)], axis=1),
        ],
        axis=0,
    )
    tables = []
    for values in (base, soft, heat):
        found = jnp.zeros(mat.shape, F32)
        for m in range(values.shape[0]):
            found = jnp.where(mat == F32(m + 1), values[m], found)
        tables.append(found)
    own = [p for t in tables for p in three_parts(t[0:1])]
    r, y = iota((9, 3 * LANES), 0), iota((9, 3 * LANES), 1)
    cols[...] = dot(jnp.concatenate(own, axis=0), hot_of(lax.div(r, 3) == lax.div(y, LANES)), 0, 0)
    wide = lambda t, i: jnp.broadcast_to(t[i : i + 1], (EDGE, total))
    kb, ks, cf = (jnp.concatenate([wide(t, 1), wide(t, 0), wide(t, 0), wide(t, 2)], axis=0) for t in tables)
    sx = strip_of(sides[...], before[:, :total], after[:, :total])
    sc = kb / (1.0 + ks * sx)
    down = lambda by, axis: 0.5 * (sc + turned(sc, by, axis))
    around = [down(rows, 1), down(-rows, 1), down(1, 1), down(-1, 1), down(1, 0), down(-1, 0)]
    diag = cf
    for w in around:
        diag = diag + w
    si = jnp.where(cf > 0.0, 1.0 / diag, 0.0)
    for i, w in enumerate(around):
        strips[i] = w * si
    strips[6] = si
    strips[7] = cf * sx * si
    strips[8] = sx
    got = [dot(p, end_lanes(2, 1), 0, 0) for p in three_parts(ends_of(sc))]
    ends[...] = got[0] + got[1] + got[2]

    piece = 16
    blank = jnp.zeros((EDGE, LANES), F32)

    @pl.loop(0, count)
    def _(k):
        cond[k, pl.ds(0, EDGE)] = blank
        cond[k, pl.ds(rows + EDGE, EDGE)] = blank
        wx[k, pl.ds(0, EDGE)] = blank
        wx[k, pl.ds(rows + EDGE, EDGE)] = blank
        for at in range(0, rows, piece):
            part = pl.ds(pl.multiple_of(k * rows + at, 8), piece)
            x = xm[k, pl.ds(EDGE + at, piece)]
            cond[k, pl.ds(EDGE + at, piece)] = cols[part, 0:LANES] / (1.0 + cols[part, LANES : 2 * LANES] * x)

    first, last = iota((piece, LANES), 1) == 0, iota((piece, LANES), 1) == LANES - 1
    wz[0] = 0.5 * (cond[0, pl.ds(EDGE, rows)] + cond[1, pl.ds(EDGE, rows)])

    @pl.loop(1, count - 1)
    def _(k):
        for at in range(0, rows, piece):
            here = pl.ds(EDGE + at, piece)
            part = pl.ds(pl.multiple_of(k * rows + at, 8), piece)
            to = pl.ds(at, piece)
            c, end = cond[k, here], ends[part, :]
            up = 0.5 * (c + cond[k + 1, here])
            low = 0.5 * (c + cond[k - 1, here])
            right = 0.5 * (c + cond[k, pl.ds(EDGE + at + 1, piece)])
            left = 0.5 * (c + cond[k, pl.ds(EDGE + at - 1, piece)])
            e = 0.5 * (c + jnp.where(last, end, turned(c, -1, 1)))
            w = 0.5 * (c + jnp.where(first, end, turned(c, 1, 1)))
            cf = cols[part, 2 * LANES : 3 * LANES]
            diag = cf + up + low + right + left + e + w
            i = jnp.where(cf > 0.0, 1.0 / diag, 0.0)
            wz[k, to] = up
            wx[k, here] = right
            wy[k, to] = e
            wyw[k, to] = w
            inv[k, to] = i
            b0[k, to] = cf * xm[k, here] * i


def sweep_kernel(xm, wz, wx, wy, wyw, inv, b0, strips, low, own, high,
                 out, pull, full, b, d, xa, xb, ends):
    count, rows, _ = inv.shape
    total = count * rows
    factors = steps()

    layers = out.shape[0] // LANES
    n = layers * rows
    skip = (count - 3 * layers) // 2
    sb = jnp.zeros((4 * EDGE, total), F32)
    blocks = -(-n // LANES)
    blank = jnp.zeros((4 * EDGE, total - blocks * LANES), F32)
    for i, ref in enumerate((low, own, high)):
        start = skip + i * layers
        for k in range(layers):
            full[start + k] = ref[pl.ds(k * rows, rows), :]
        cells = [ref[pl.ds(n + 4 * EDGE * j, 4 * EDGE), :] for j in range(blocks)]
        sb = sb + turned(jnp.concatenate(cells + [blank], axis=1), start * rows, 1)
    for k in range(skip):
        full[k] = jnp.zeros((rows, LANES), F32)
        full[count - 1 - k] = jnp.zeros((rows, LANES), F32)
    sb = strips[7] + sb * strips[6]
    sx, sd = strips[8], None
    kept = [ends_of(sx)]
    for s, (keep, add) in enumerate(factors[:-1]):
        lanes = slice(s * LANES, total - s * LANES)
        part = lambda i: strips[i, :, lanes]
        near = part(0) * turned(sx, rows, 1) + part(1) * turned(sx, -rows, 1)
        near += part(2) * turned(sx, 1, 1) + part(3) * turned(sx, -1, 1)
        near += part(4) * turned(sx, 1, 0) + part(5) * turned(sx, -1, 0)
        step = add * (sb[:, lanes] - sx + near)
        sd = step if sd is None else step + keep * sd
        sx, sd = (sx + sd)[:, LANES:-LANES], sd[:, LANES:-LANES]
        kept.append(ends_of(sx))
    place_in = end_lanes(2, 1)
    place_in = jnp.concatenate([place_in, place_in], axis=0)
    for s, pair in enumerate(kept):
        start = (1 + s) * rows // LANES * LANES
        stop = -(-(count - 1 - s) * rows // LANES) * LANES
        ends[start:stop, s * LANES : (s + 1) * LANES] = dot(
            jnp.concatenate(parts(pair[:, start - s * LANES : stop - s * LANES]), axis=0), place_in, 0, 0)

    piece = 48
    first, last = iota((piece, LANES), 1) == 0, iota((piece, LANES), 1) == LANES - 1
    blank = jnp.zeros((EDGE, LANES), F32)

    @pl.loop(0, count)
    def _(k):
        for ref in (xa, xb):
            ref[k, pl.ds(0, EDGE)] = blank
            ref[k, pl.ds(rows + EDGE, EDGE)] = blank

    for s, (keep, add) in enumerate(factors):
        src, into = (xm if s == 0 else (xa if s % 2 else xb)), (xb if s % 2 else xa)

        @pl.loop(1 + s, count - 1 - s)
        def _(k):
            for at in range(0, rows, piece):
                here, to = pl.ds(EDGE + at, piece), pl.ds(at, piece)
                x = src[k, here]
                end = ends[pl.ds(pl.multiple_of(k * rows + at, 8), piece), s * LANES : (s + 1) * LANES]
                e = jnp.where(last, end, turned(x, -1, 1))
                w = jnp.where(first, end, turned(x, 1, 1))
                near = wz[k, to] * src[k + 1, here] + wz[k - 1, to] * src[k - 1, here]
                near += wx[k, here] * src[k, pl.ds(EDGE + at + 1, piece)]
                near += wx[k, pl.ds(EDGE + at - 1, piece)] * src[k, pl.ds(EDGE + at - 1, piece)]
                near += wy[k, to] * e + wyw[k, to] * w
                if s == 0:
                    rhs = b0[k, to] + full[k, to] * inv[k, to]
                    b[k, to] = rhs
                else:
                    rhs = b[k, to]
                step = add * (rhs - x + inv[k, to] * near)
                if s > 0:
                    step = step + keep * d[k, to]
                if s < SWEEPS - 1:
                    d[k, to] = step
                into[k, here] = x + step

    final = xb if SWEEPS % 2 == 0 else xa
    for k in range(4):
        out[pl.ds(k * LANES, LANES), :] = final[SWEEPS + k, pl.ds(2 * EDGE, LANES)]
    scale = 1.0
    for _, add in factors:
        scale = scale * add
    tile = pl.ds(EDGE, LANES)
    for i, (start, way) in enumerate(((1, 1), (count - 2, -1))):
        gain = scale * inv[start, tile]
        for j in range(1, SWEEPS):
            at = start + way * j
            gain = gain * inv[at, tile] * wz[at - 1 if way > 0 else at, tile]
        pull[pl.ds(i * LANES, LANES), :] = gain


def reply_kernel(x, pull, low2, high2, hot, out, replies):
    n = out.shape[0]
    first, last = pl.ds(0, LANES), pl.ds(n - LANES, LANES)
    out[...] = x[...]
    out[first, :] = x[first, :] + pull[pl.ds(0, LANES), :] * low2[...]
    out[last, :] = x[last, :] + pull[pl.ds(LANES, LANES), :] * high2[...]
    replies[...] = pick_rows(hot[...], out[...])


def final_kernel(returned, hot, gain, mob, mobility, ionization):
    back = pick_rows(hot[...], returned[...])
    mobility[...] = mob[...] * jnp.exp(-0.7 * back)
    ionization[...] = jnp.exp(gain[...] * (1.0 + 0.3 * back))


def shifted(v, axis, by):
    count = lax.axis_size(axis)
    pairs = [(i, i + by) for i in range(count) if 0 <= i + by < count]
    return lax.ppermute(v, axis, pairs) if pairs else jnp.zeros_like(v)


def swapped(a, b, axis):
    count = lax.axis_size(axis)
    found = []
    for v, odd in ((a, 0), (b, 1)):
        pairs = [p for i in range(odd, count - 1, 2) for p in ((i, i + 1), (i + 1, i))]
        found.append(lax.ppermute(v, axis, pairs) if pairs else jnp.zeros_like(v))
    return found


def exchanged(v):
    lines = v.reshape(v.shape[0], 1, v.shape[1])
    return lax.all_to_all(lines, ("gx", "gy"), split_axis=0, concat_axis=0, tiled=True).reshape(v.shape)


def per_device(
    efield, density, mobility_prev, thermal_prev, owner, block, live, material,
    mat_conductivity, mat_softening, mat_capacity,
):
    layers, xcells, width = density.shape
    n = layers * xcells
    peers = lax.axis_size("gx") * lax.axis_size("gy")
    slots = max(2, 2 * n // peers)
    line = peers * (slots + 1)
    flat = lambda a: a.reshape(n, width)
    ef = efield.reshape(3, n, width)
    den, mob, x0 = flat(density), flat(mobility_prev), flat(thermal_prev)
    own, blk, liv = owner.reshape(1, n), block.reshape(1, n), live.reshape(1, n)
    mat = material.reshape(layers, xcells)
    sized = lambda *s: (s, F32)

    given = [ef, den, mob, own, blk, liv]
    [sent] = call(
        functools.partial(dispatch_kernel, peers, slots), [sized(line, width)], given, "dispatch", flops=10**8, hbm=True, limit=60,
        scratch=[pltpu.VMEM(a.shape, a.dtype) for a in given] + [pltpu.SemaphoreType.DMA((len(given),))])
    received = exchanged(sent)

    far = SWEEPS - layers
    count = layers + 2 * SWEEPS
    rows = xcells + 2 * EDGE
    total = count * rows
    aside = sized(far * xcells + EDGE, width)
    near, up, down = call(
        functools.partial(start_z_kernel, far), [sized(n + EDGE, width), aside, aside], [x0, mat], "start_z")
    low, high = shifted(near, "gz", 1), shifted(near, "gz", -1)
    low2, high2 = shifted(up, "gz", 2), shifted(down, "gz", -2)
    gain, dest = call(functools.partial(after_kernel, slots), [sized(n, width), ((n, peers * slots), BF16)], [ef, own], "gain")
    edge = sized(count * (EDGE + 1), width)
    xz, mats, start_low, start_high = call(
        functools.partial(start_x_kernel, far), [sized(count, xcells, width), sized(count, width), edge, edge],
        [low2, low, near, high, high2], "start_x")
    received, start_low, start_high, gain, dest = lax.optimization_barrier(
        (received, start_low, start_high, gain, dest))

    source, first, last = call(
        functools.partial(combine_kernel, peers, slots), [sized(n, width)] + [sized(xcells, width)] * 2,
        [received], "combine", flops=10**8)
    [ids] = call(functools.partial(ids_kernel, peers, slots), [((peers * slots, n), BF16)], [received], "ids")
    edge = sized(count * (EDGE + 1) + layers * EDGE, width)
    xlow, xhigh = call(pack_x_kernel, [edge, edge], [source, start_low, start_high], "pack_x")
    before, after = shifted(xhigh, "gx", 1), shifted(xlow, "gx", -1)
    before, after, ids = lax.optimization_barrier((before, after, ids))
    tall, tile, flat_edge = sized(count, rows + 2 * EDGE, width), sized(count, rows, width), sized(2 * EDGE, total)
    inner = layers * rows
    y_edge = sized(EDGE, total + total // 3)
    xm, full, sides, heat_sides, flat_mat, ylow, yhigh = call(
        pack_y_kernel,
        [tall, sized(inner, width), flat_edge, sized(2 * EDGE, inner), sized(EDGE, total), y_edge, y_edge],
        [xz, mats, source, after, before], "pack_y")
    even = lax.axis_index("gy") % 2 == 0
    one, two = swapped(jnp.where(even, yhigh, ylow), jnp.where(even, ylow, yhigh), "gy")
    before, after = jnp.where(even, two, one), jnp.where(even, one, two)
    blocks = -(-inner // LANES)
    [around] = call(
        pack_z_kernel, [sized(inner + 4 * EDGE * blocks, width)], [full, heat_sides, before, after], "pack_z")
    low, high = shifted(around, "gz", 1), shifted(around, "gz", -1)
    weights = call(
        weights_kernel, [tile, tall, tile, tile, tile, tile, sized(9, 4 * EDGE, total)],
        [mat_conductivity, mat_softening, mat_capacity, xm, sides, flat_mat, before, after], "weights",
        scratch=[pltpu.VMEM((count, rows + 2 * EDGE, width), F32), pltpu.VMEM((total, 3 * width), F32),
                 pltpu.VMEM((total, width), F32)],
        limit=32, flops=10**9, smem=(0, 1, 2))
    first, last, weights = lax.optimization_barrier((first, last, weights))
    low2, high2 = shifted(last, "gz", 2), shifted(first, "gz", -2)
    x, pull = call(
        sweep_kernel, [sized(n, width), sized(2 * xcells, width)],
        [xm] + list(weights) + [low, around, high], "sweeps",
        scratch=[pltpu.VMEM((count, rows, width), F32)] * 3 + [pltpu.VMEM((count, rows + 2 * EDGE, width), F32)] * 2
        + [pltpu.VMEM((total, SWEEPS * width), F32)],
        limit=36, flops=10**8)
    x, pull, low2, high2 = lax.optimization_barrier((x, pull, low2, high2))
    x, replies = call(
        reply_kernel, [sized(n, width), sized(peers * slots, width)], [x, pull, low2, high2, ids], "reply", flops=10**8)
    returned = exchanged(replies)
    mobility, ionization = call(final_kernel, [sized(n, width)] * 2, [returned, dest, gain, mob], "finish", flops=10**8)
    shape = density.shape
    return x.reshape(shape), mobility.reshape(shape), ionization.reshape(shape)


def solution(mesh):
    tile = P("gz", "gx", "gy")
    rows = P("gz", "gx", "gy", None)
    placed = (
        P(None, "gz", "gx", "gy"), tile, tile, tile,
        P("gz", "gx", "gy", None, None), rows, rows, rows, P(), P(), P(),
    )
    return jax.shard_map(
        per_device, mesh=mesh, in_specs=placed, out_specs=(tile, tile, tile), check_vma=False
    )
```
